512 devices in a mesh: regime: 8 (over y, core), obj: 64 (over x, z).
Axes of the slice: x: 4, y: 4, z: 16, core: 2. Of those that a mesh axis runs over, the one named last changes fastest.
Arguments:
- local_jac: bfloat16 [7, 245760], P(None, ('regime', 'obj')), may hold values from -6 to 6
- global_jac: bfloat16 [245760, 512], P(('regime', 'obj')), may hold values from -0.1331338 to 0.1331338
- coeff_index: int32 [4, 245760], P(None, ('regime', 'obj')), may hold values from 0 to 511
- coeff_weight: bfloat16 [4, 245760], P(None, ('regime', 'obj')), may hold values from -2.065591 to 2.065591
- residual: float32 [245760], P(('regime', 'obj')), may hold values from -10 to 10
- obs_weight: float32 [245760], P(('regime', 'obj')), may hold values from 0.3 to 3
- obs_count: int32 [4096], P(('regime', 'obj')), may hold values from 1 to 60
- local_prior: float32 [7, 4096], P(None, ('regime', 'obj')), may hold values from 0.3 to 3
- regional_prior: float32 [8, 512], P('regime'), may hold values from 0.1 to 1
- global_prior: float32 [512], replicated, may hold values from 0.3 to 3
Outputs:
- local_step: float32 [7, 4096], P(None, ('regime', 'obj'))
- regional_step: float32 [8, 512], P('regime')
- global_step: float32 [512], replicated
The draws below stay inside these ranges and needn't reach their ends.
All inputs are finite; a program needn't handle non-finite values.
Results may differ from the reference program's by a relative error of at most 0.0005.
The reference program's roundings to bfloat16 on the way (of `joined` and `scaled`) count: a program that leaves them out, or rounds other values in their place, can miss the bound.
Values sent between devices are 32-bit elements; how exact they have to be, the bound alone decides.
No kernel may reach another device: no remote copies, remote signals or barrier semaphores. Data moves between devices by JAX's collectives and lax.ppermute only.
A program may use at most 64 MiB of HBM per device.

```python
import math
import jax
import jax.numpy as jnp
from jax import lax

R = 512
G = 512
NLOC = 7
OBS = 60
KR = 4
OBJ_DEV = 8
OBJECTS = 4096
ROWS = 245760
REGIMES = 8
N_REGIME = 8
N_OBJ = 64


def regional_scaling():
    return 5.0 * (N_OBJ * OBJ_DEV * OBS * KR // R) ** (-0.5)


def global_scaling():
    return 6.0 * (N_REGIME * N_OBJ * OBJ_DEV * OBS) ** (-0.5)


def index_table(key):
    total = OBJ_DEV * OBS * N_REGIME * N_OBJ
    base = jax.random.randint(jax.random.fold_in(key, 11), (total,), 0, R, dtype=jnp.int32)
    taps = jnp.arange(KR, dtype=jnp.int32)
    return (base[None, :] + taps[:, None]) % R


def weight_table(key):
    total = OBJ_DEV * OBS * N_REGIME * N_OBJ
    inner = jax.random.fold_in(key, 12)
    place_key = jax.random.fold_in(key, 16)
    where = jax.random.uniform(place_key, (total,), jnp.float32, 0.0, 1.0)
    amplitude = jnp.clip(jax.random.normal(inner, (total,), jnp.float32), -3.8, 3.8)
    amplitude = amplitude * (2.5 * regional_scaling())
    first = -0.5 * (1.0 - where) * (1.0 - where)
    second = 1.5 * where * where - 2.0 * where
    third = -1.5 * where * where + where + 0.5
    fourth = 0.5 * where * where
    stencil = jnp.stack([first, second, third, fourth], axis=0)
    return stencil * amplitude[None, :]


def draw_coeff_index(key, part):
    return index_table(key)


def draw_coeff_weight(key, part):
    return weight_table(key).astype(jnp.bfloat16)


def draw_global_jac(key, part):
    blocks = N_REGIME * N_OBJ
    rows_block = OBJ_DEV * OBS
    indices = index_table(key)
    weights = weight_table(key)
    mix_key = jax.random.fold_in(key, 13)
    map_key = jax.random.fold_in(key, 14)
    noise_key = jax.random.fold_in(key, 15)
    other_key = jax.random.fold_in(key, 17)
    strength = 0.85
    raw_mix = jnp.clip(jax.random.normal(mix_key, (G, G), jnp.float32), -4.0, 4.0)
    raw_other = jnp.clip(jax.random.normal(other_key, (G, G), jnp.float32), -4.0, 4.0)
    raw_map = jnp.clip(jax.random.normal(map_key, (N_REGIME, R, G), jnp.float32), -4.0, 4.0)
    identity = jnp.eye(G, dtype=jnp.float32)
    left_mix = identity + strength * G ** (-0.5) * raw_mix
    right_mix = identity + strength * G ** (-0.5) * raw_other
    levels = 0.015 * (2.5 / 0.015) ** (jnp.arange(G, dtype=jnp.float32) / max(G - 1, 1))
    mixing = jnp.dot(left_mix * levels[None, :], right_mix, precision=lax.Precision.HIGHEST)
    cell_map = raw_map * (N_REGIME * R) ** (-0.5)
    scale_global = global_scaling()
    limit = 10.0 * scale_global

    def one_block(block):
        start = block * rows_block
        block_key = jax.random.fold_in(noise_key, block)
        noise = jnp.clip(jax.random.normal(block_key, (rows_block, G), jnp.float32), -4.0, 4.0)
        mixed = jnp.dot(noise, mixing, precision=lax.Precision.HIGHEST)
        block_index = lax.dynamic_slice_in_dim(indices, start, rows_block, 1)
        block_weight = lax.dynamic_slice_in_dim(weights, start, rows_block, 1)
        group_map = lax.dynamic_index_in_dim(cell_map, block // N_OBJ, 0, keepdims=False)
        regional = jnp.zeros((rows_block, G), jnp.float32)
        for k in range(KR):
            regional = regional + block_weight[k][:, None] * group_map[block_index[k]]
        value = jnp.clip(scale_global * mixed + regional, -limit, limit)
        return value.astype(jnp.bfloat16)
    stacked = lax.map(one_block, jnp.arange(blocks, dtype=jnp.int32))
    return stacked.reshape(blocks * rows_block, G)


def draw_residual(key, part):
    total = OBJ_DEV * OBS * N_REGIME * N_OBJ
    position = jnp.arange(total, dtype=jnp.float32) / total
    group = jnp.arange(total, dtype=jnp.int32) // (total // N_REGIME)
    levels = 0.6 * (1.6 / 0.6) ** (jnp.arange(N_REGIME, dtype=jnp.float32) / max(N_REGIME - 1, 1))
    order = jax.random.permutation(jax.random.fold_in(key, 21), N_REGIME)
    group_level = levels[order][group]
    spread = 0.55 * (1.0 + 2.0 * position) * group_level
    noise_key = jax.random.fold_in(key, 22)
    noise = jnp.clip(jax.random.normal(noise_key, (total,), jnp.float32), -3.5, 3.5)
    return noise * spread


def place_ends(drawn, rng, least, largest):
    longest = drawn.shape.index(max(drawn.shape))
    spots = []
    for shift in (0, 1):
        where = [jax.random.randint(jax.random.fold_in(rng, axis), (), 0, length) for axis, length in enumerate(drawn.shape)]
        where[longest] = (where[longest] + shift) % drawn.shape[longest]
        spots.append(tuple(where))
    return drawn.at[spots[0]].set(least).at[spots[1]].set(largest)


def shard_levels(rng, shape, cuts, smallest, high):
    def one(axis_at, blocks):
        heights = jax.random.uniform(jax.random.fold_in(jax.random.fold_in(rng, 6), axis_at), (blocks,), jnp.float32, smallest / len(cuts), high / len(cuts))
        return jnp.repeat(jnp.exp(heights), shape[axis_at] // blocks).reshape((-1,) + (1,) * (len(shape) - axis_at - 1))

    gain = one(*cuts[0])
    for cut in cuts[1:]:
        gain = gain * one(*cut)
    return gain


def bell_draw(stream_key, dims, scale, reach, split=(), kind=jnp.bfloat16):
    drawn = jax.random.normal(stream_key, dims, jnp.float32) * scale
    if len(split) > 0:
        drawn = shard_levels(stream_key, dims, split, -0.22, 0.18) * drawn
    return jnp.clip(drawn, min=-reach, max=reach).astype(kind)


def setup_inputs(seed: int = 0) -> dict:
    streams_of = jax.random.split(jax.random.key(seed), 11)
    return {
        "local_jac": bell_draw(streams_of[0], (NLOC, ROWS), 1.0, 6.0, ((1, 512),)),
        "global_jac": draw_global_jac(jax.random.fold_in(streams_of[10], 71), 0),
        "coeff_index": draw_coeff_index(jax.random.fold_in(streams_of[10], 71), 0),
        "coeff_weight": draw_coeff_weight(jax.random.fold_in(streams_of[10], 71), 0),
        "residual": draw_residual(jax.random.fold_in(streams_of[10], 71), 0),
        "obs_weight": jnp.clip(jnp.exp(math.log(3.0) - 2.3025851 * jax.random.uniform(streams_of[5], (ROWS,), jnp.float32) ** shard_levels(streams_of[5], (ROWS,), ((0, 512),), -0.2, 0.2)), 0.3, 3.0),
        "obs_count": place_ends(jax.random.randint(streams_of[6], (OBJECTS,), 1, OBS + 1), jax.random.fold_in(streams_of[6], 1), 1, OBS).astype(jnp.int32),
        "local_prior": jnp.clip(jnp.exp(math.log(3.0) - 2.3025851 * jax.random.uniform(streams_of[7], (NLOC, OBJECTS), jnp.float32) ** shard_levels(streams_of[7], (NLOC, OBJECTS), ((1, 512),), -0.2, 0.2)), 0.3, 3.0),
        "regional_prior": jnp.clip(jnp.exp(math.log(1.0) - 2.3025851 * jax.random.uniform(streams_of[8], (REGIMES, R), jnp.float32) ** shard_levels(streams_of[8], (REGIMES, R), ((0, 8),), -0.2, 0.2)), 0.1, 1.0),
        "global_prior": jnp.clip(jnp.exp(jax.random.uniform(streams_of[9], (G,), jnp.float32, math.log(0.3), math.log(3.0))), 0.3, 3.0),
    }


def live_weight(obs_weight, obs_count, observed):
    objects = obs_count.shape[0]
    position = jnp.arange(observed, dtype=jnp.int32)
    present = (position[None, :] < obs_count[:, None]).reshape(objects * observed)
    return (jnp.where(present, obs_weight, jnp.float32(0.0)), present)

def jacobian(coeff_index, coeff_weight, global_jac, regional_width):
    columns = jnp.arange(regional_width, dtype=jnp.int32)
    regional = jnp.zeros((coeff_index.shape[1], regional_width), jnp.float32)
    for k in range(coeff_index.shape[0]):
        regional = regional + jnp.where(coeff_index[k][:, None] == columns[None, :], coeff_weight[k][:, None].astype(jnp.float32), jnp.float32(0.0))
    return jnp.concatenate([regional.astype(jnp.bfloat16), global_jac], axis=1)

def cholesky_small(entries):
    order = len(entries)
    factor = [[None] * order for i in range(order)]
    for j in range(order):
        diagonal = entries[j][j]
        for k in range(j):
            diagonal = diagonal - factor[j][k] * factor[j][k]
        factor[j][j] = jnp.sqrt(diagonal)
        for i in range(j + 1, order):
            current = entries[i][j]
            for k in range(j):
                current = current - factor[i][k] * factor[j][k]
            factor[i][j] = current / factor[j][j]
    return factor

def broaden(entry, like):
    return entry.reshape(entry.shape + (1,) * (like.ndim - 1))

def forward_small(factor, target):
    result = []
    for a in range(len(target)):
        current = target[a]
        for k in range(a):
            current = current - broaden(factor[a][k], current) * result[k]
        result.append(current / broaden(factor[a][a], current))
    return result

def backward_small(factor, target):
    order = len(target)
    result = [None] * order
    for a in reversed(range(order)):
        current = target[a]
        for k in range(a + 1, order):
            current = current - broaden(factor[k][a], current) * result[k]
        result[a] = current / broaden(factor[a][a], current)
    return result

def factor_local(local_jac, weight, local_prior, objects):
    nparams = local_jac.shape[0]
    local_rows = local_jac.astype(jnp.float32).reshape(nparams, objects, -1)
    weighted_local = local_rows * weight.reshape(objects, -1)[None]
    small_normal = jnp.einsum('anp,bnp->abn', weighted_local, local_rows, precision=lax.Precision.HIGHEST)
    entries = [[small_normal[a, b] + (local_prior[a] if a == b else 0.0) for b in range(nparams)] for a in range(nparams)]
    return (cholesky_small(entries), weighted_local)

def assemble(local_jac, global_jac, coeff_index, coeff_weight, residual, obs_weight, obs_count, local_prior, regional_width):
    objects = obs_count.shape[0]
    observed = local_jac.shape[1] // objects
    nparams = local_jac.shape[0]
    weight, present = live_weight(obs_weight, obs_count, observed)
    joined = jacobian(coeff_index, coeff_weight, global_jac, regional_width)
    scaled = (joined.astype(jnp.float32) * weight[:, None]).astype(jnp.bfloat16)
    normal = jnp.dot(scaled.T.astype(jnp.float32), joined.astype(jnp.float32), preferred_element_type=jnp.float32)
    gradient = jnp.dot(residual, scaled.astype(jnp.float32), precision=lax.Precision.HIGHEST)
    factor, weighted_local = factor_local(local_jac, weight, local_prior, objects)
    coupling = jnp.einsum('anp,npc->anc', weighted_local, joined.reshape(objects, observed, -1).astype(jnp.float32), precision=lax.Precision.HIGHEST)
    local_gradient = lax.optimization_barrier(jnp.sum(weighted_local * residual.reshape(objects, observed)[None], axis=2))
    reduced = forward_small(factor, [coupling[a] for a in range(nparams)])
    reduced_gradient = forward_small(factor, [local_gradient[a] for a in range(nparams)])
    stacked = jnp.concatenate(reduced, axis=0)
    vector = jnp.concatenate(reduced_gradient, axis=0)
    normal = normal - jnp.dot(stacked.T, stacked, precision=lax.Precision.HIGHEST)
    gradient = gradient - jnp.dot(vector, stacked, precision=lax.Precision.HIGHEST)
    return (normal, gradient)

def local_solution(local_jac, global_jac, coeff_index, coeff_weight, residual, obs_weight, obs_count, local_prior, update, regional_width):
    objects = obs_count.shape[0]
    observed = local_jac.shape[1] // objects
    nparams = local_jac.shape[0]
    weight, present = live_weight(obs_weight, obs_count, observed)
    joined = jacobian(coeff_index, coeff_weight, global_jac, regional_width)
    factor, weighted_local = factor_local(local_jac, weight, local_prior, objects)
    moved = jnp.dot(joined.astype(jnp.float32), update, precision=lax.Precision.HIGHEST)
    target = lax.optimization_barrier(jnp.sum(weighted_local * (residual - moved).reshape(objects, observed)[None], axis=2))
    solved = backward_small(factor, forward_small(factor, [target[a] for a in range(nparams)]))
    return jnp.stack(solved, axis=0)

def cho_apply(factor, target):
    return jax.scipy.linalg.cho_solve((factor, True), target)

def reference(local_jac, global_jac, coeff_index, coeff_weight, residual, obs_weight, obs_count, local_prior, regional_prior, global_prior):
    blocks = N_REGIME * N_OBJ
    rows_block = OBJ_DEV * OBS
    weight, present = live_weight(obs_weight, obs_count, OBS)
    damping = jnp.sum(weight * residual * residual) / jnp.sum(present.astype(jnp.float32))
    pieces = (local_jac.reshape(NLOC, blocks, rows_block).transpose(1, 0, 2), global_jac.reshape(blocks, rows_block, G), coeff_index.reshape(KR, blocks, rows_block).transpose(1, 0, 2), coeff_weight.reshape(KR, blocks, rows_block).transpose(1, 0, 2), residual.reshape(blocks, rows_block), obs_weight.reshape(blocks, rows_block), obs_count.reshape(blocks, OBJ_DEV), local_prior.reshape(NLOC, blocks, OBJ_DEV).transpose(1, 0, 2))

    def accumulate(carry, item):
        normal, gradient = assemble(*item, R)
        return ((carry[0] + normal, carry[1] + gradient), None)
    global_matrix = jnp.zeros((G, G), jnp.float32)
    global_vector = jnp.zeros((G,), jnp.float32)
    saved = []
    for group in range(N_REGIME):
        members = tuple((piece[group * N_OBJ:(group + 1) * N_OBJ] for piece in pieces))
        start = (jnp.zeros((R + G, R + G), jnp.float32), jnp.zeros((R + G,), jnp.float32))
        (schur, rhs), unused = lax.scan(accumulate, start, members)
        regional_factor = jnp.linalg.cholesky(schur[:R, :R] + damping * jnp.diag(regional_prior[group]))
        block = schur[:R, R:]
        coupled = cho_apply(regional_factor, block)
        shifted = cho_apply(regional_factor, rhs[:R])
        global_matrix = global_matrix + schur[R:, R:] - jnp.dot(block.T, coupled, precision=lax.Precision.HIGHEST)
        global_vector = global_vector + rhs[R:] - jnp.dot(shifted, block, precision=lax.Precision.HIGHEST)
        saved.append((regional_factor, block, rhs[:R]))
    global_factor = jnp.linalg.cholesky(global_matrix + damping * jnp.diag(global_prior))
    global_step = cho_apply(global_factor, global_vector)
    regional_rows = []
    for group in range(N_REGIME):
        regional_factor, block, rhs_regional = saved[group]
        regional_rows.append(cho_apply(regional_factor, rhs_regional - jnp.dot(block, global_step, precision=lax.Precision.HIGHEST)))
    regional_step = jnp.stack(regional_rows, axis=0)
    updates = jnp.concatenate([regional_step, jnp.broadcast_to(global_step[None], (N_REGIME, G))], axis=1)
    updates = jnp.repeat(updates, N_OBJ, axis=0)

    def solve_block(item):
        return local_solution(*item[:8], item[8], R)
    local_blocks = lax.map(solve_block, pieces + (updates,))
    local_step = local_blocks.transpose(1, 0, 2).reshape(NLOC, blocks * OBJ_DEV)
    return (local_step, regional_step, global_step)
```

```python
import jax
import jax.numpy as jnp
from jax import lax
from jax.experimental import pallas as pl
from jax.experimental.pallas import tpu as pltpu
from jax.sharding import Mesh, PartitionSpec as P

f32 = jnp.float32
bf16 = jnp.bfloat16
HIGHEST = lax.Precision.HIGHEST

NB = 128
NBLK = 4
PAIRS = [(i, j) for i in range(NBLK) for j in range(i, NBLK)]
SLOT = {pair: at for at, pair in enumerate(PAIRS)}
TRI = len(PAIRS) * NB
REG_PARTS = 8
PART = TRI // REG_PARTS
PART_ROWS = PART + 8
MAIN_ROWS = 1536
SUM_AT = TRI + 8
CHUNK = 48
RPAD = 64

LAYERS = ("x", "z")
GROUPS = ("y", "core")


def tn(a, b, precision=None):
    return lax.dot_general(
        a, b, (((0,), (0,)), ((), ())), precision=precision, preferred_element_type=f32
    )


def nt(a, b, precision=None):
    return lax.dot_general(
        a, b, (((1,), (1,)), ((), ())), precision=precision, preferred_element_type=f32
    )


def nn(a, b, precision=None):
    return jnp.dot(a, b, precision=precision, preferred_element_type=f32)


def pieces(value):
    first = value.astype(bf16)
    rest = value - first.astype(f32)
    second = rest.astype(bf16)
    third = (rest - second.astype(f32)).astype(bf16)
    return first, second, third


def cholesky_small(entries):
    order = len(entries)
    factor = [[None] * order for i in range(order)]
    for j in range(order):
        diagonal = entries[j][j]
        for k in range(j):
            diagonal = diagonal - factor[j][k] * factor[j][k]
        factor[j][j] = jnp.sqrt(diagonal)
        for i in range(j + 1, order):
            current = entries[i][j]
            for k in range(j):
                current = current - factor[i][k] * factor[j][k]
            factor[i][j] = current / factor[j][j]
    return factor


def forward_small(factor, target):
    result = []
    for a in range(len(target)):
        current = target[a]
        for k in range(a):
            current = current - factor[a][k] * result[k]
        result.append(current / factor[a][a])
    return result


def backward_small(factor, target):
    order = len(target)
    result = [None] * order
    for a in reversed(range(order)):
        current = target[a]
        for k in range(a + 1, order):
            current = current - factor[k][a] * result[k]
        result[a] = current / factor[a][a]
    return result


def store_split(ref, slot, block):
    done = 0
    while done < NB:
        flat = slot * NB + done
        part, off = flat // PART, flat % PART
        take = min(NB - done, PART - off)
        start = part * PART_ROWS + off
        ref[start : start + take, :] = block[done : done + take]
        done += take


def assemble_kernel(
    lj_ref, gj_ref, ci_ref, cw_ref, res_ref, ow_ref, cnt_ref, lp_ref,
    gg_ref, main_ref, rg_ref, red_ref, aux_ref,
    left, right, padded,
):
    rows = gj_ref.shape[0]
    nparams = lj_ref.shape[0]
    objects = 8
    observed = rows // objects
    width = gj_ref.shape[1]
    res = res_ref[...]
    position = lax.broadcasted_iota(jnp.int32, (objects, rows), 1)
    owner = lax.broadcasted_iota(jnp.int32, (objects, rows), 0)
    count = jnp.zeros((objects, rows), jnp.int32)
    for n in range(objects):
        count = jnp.where(owner == n, cnt_ref[n], count)
    local = position - owner * observed
    present = (local >= 0) & (local < observed) & (local < count)
    live = jnp.where(present, jnp.broadcast_to(ow_ref[...], (objects, rows)), 0.0)
    weight = jnp.sum(live, axis=0, keepdims=True)
    misfit = jnp.sum(weight * res * res, axis=1, keepdims=True)
    counted = jnp.sum(
        jnp.sum(jnp.where(present, 1.0, 0.0), axis=0, keepdims=True), axis=1, keepdims=True
    )

    padded[...] = jnp.zeros_like(padded)
    padded[0:1, :rows] = weight
    padded[1:5, :rows] = ci_ref[...].astype(f32)
    padded[5:9, :rows] = cw_ref[...].astype(f32)
    for block in range(padded.shape[1] // NB):
        columns = padded[:, block * NB : (block + 1) * NB].T
        low = block * NB
        while low < min((block + 1) * NB, rows):
            high = min(low + 32, rows)
            here = columns[low - block * NB : high - block * NB]
            weights = here[:, 0:1]
            lanes = lax.broadcasted_iota(jnp.int32, (high - low, width), 1).astype(f32)
            total = jnp.zeros((high - low, width), f32)
            for k in range(4):
                total = total + jnp.where(here[:, 1 + k : 2 + k] == lanes, here[:, 5 + k : 6 + k], 0.0)
            joined = total.astype(bf16)
            for at, value in ((0, joined), (width, gj_ref[low:high, :])):
                scaled = (value.astype(f32) * weights).astype(bf16)
                right[low:high, at : at + width] = value
                right[rows + low : rows + high, at : at + width] = scaled
                left[low:high, at : at + width] = (scaled.astype(f32) * 0.5).astype(bf16)
                left[rows + low : rows + high, at : at + width] = (value.astype(f32) * 0.5).astype(bf16)
            low = high

    jac = lj_ref[...].astype(f32)
    weighted = [jac[a : a + 1, :] * live for a in range(nparams)]
    entries = [[None] * nparams for a in range(nparams)]
    owner8 = lax.broadcasted_iota(jnp.int32, (objects, objects), 0)
    lane8 = lax.broadcasted_iota(jnp.int32, (objects, objects), 1)
    for a in range(nparams):
        for b in range(a + 1):
            value = jnp.sum(weighted[a] * jac[b : b + 1, :], axis=1, keepdims=True)
            if a == b:
                prior = jnp.broadcast_to(lp_ref[a : a + 1, :], (objects, objects))
                value = value + jnp.sum(jnp.where(owner8 == lane8, prior, 0.0), axis=1, keepdims=True)
            entries[a][b] = value
    factor = cholesky_small(entries)
    local_gradient = [jnp.sum(weighted[a] * res, axis=1, keepdims=True) for a in range(nparams)]
    reduced_gradient = forward_small(factor, local_gradient)

    blank = jnp.zeros((8, rows), f32)
    stacked = jnp.concatenate(weighted + [blank], axis=0)
    everything = right[0:rows, :]
    coupling = None
    for piece in pieces(stacked):
        term = nn(piece, everything)
        coupling = term if coupling is None else coupling + term
    reduced = forward_small(factor, [coupling[8 * a : 8 * a + 8] for a in range(nparams)])
    joint = jnp.concatenate(reduced + [jnp.zeros((8, 2 * width), f32)], axis=0)
    red_ref[...] = joint
    r0, r1, r2 = pieces(joint)
    base = 2 * rows
    for at, (one, two) in enumerate(((r0, r0), (r0, r1), (r1, r0), (r1, r1), (r0, r2), (r2, r0))):
        left[base + at * RPAD : base + (at + 1) * RPAD, :] = -one
        right[base + at * RPAD : base + (at + 1) * RPAD, :] = two

    lane = lax.broadcasted_iota(jnp.int32, (objects, NB), 1)
    aux = jnp.zeros((objects, NB), f32)
    at = 0
    for a in range(nparams):
        for b in range(a + 1):
            aux = jnp.where(lane == at, factor[a][b], aux)
            at += 1
    for a in range(nparams):
        aux = jnp.where(lane == at, reduced_gradient[a], aux)
        at += 1
    aux_ref[...] = aux

    first, second, third = pieces(res)
    lhs = jnp.concatenate(
        [first.astype(f32), second.astype(f32), third.astype(f32), jnp.zeros((13, rows), f32)], axis=0
    ).astype(bf16)
    gradient = jnp.sum(nn(lhs, right[rows : 2 * rows, :]), axis=0, keepdims=True)
    for a in range(nparams):
        gradient = gradient - jnp.sum(reduced_gradient[a] * reduced[a], axis=0, keepdims=True)
    for at in range(8):
        main_ref[TRI + at : TRI + at + 1, :] = gradient[:, at * NB : (at + 1) * NB]

    row_lane = lax.broadcasted_iota(jnp.int32, (8, NB), 1)
    scalars = jnp.where(row_lane == 0, misfit, jnp.where(row_lane == 1, counted, 0.0))
    for part in range(REG_PARTS):
        gg_ref[part * PART_ROWS + PART : (part + 1) * PART_ROWS, :] = scalars
    for i in range(NBLK):
        for half in range(2):
            at = half * width
            value = tn(left[:, at + i * NB : at + (i + 1) * NB], right[:, at + i * NB : at + width])
            for j in range(i, NBLK):
                block = value[:, (j - i) * NB : (j - i + 1) * NB]
                slot = SLOT[i, j]
                if half == 0:
                    main_ref[slot * NB : (slot + 1) * NB, :] = block
                else:
                    store_split(gg_ref, slot, block)
        value = 2.0 * tn(left[0:rows, i * NB : (i + 1) * NB], right[0:rows, width:]) + tn(
            left[base:, i * NB : (i + 1) * NB], right[base:, width:]
        )
        for c in range(NBLK):
            rg_ref[c * width + i * NB : c * width + (i + 1) * NB, :] = value[:, c * NB : (c + 1) * NB]


def lane_take(value, at):
    return jnp.take_along_axis(value, jnp.full(value.shape, at, jnp.int32), axis=1)


def spread(value, at):
    return jnp.broadcast_to(value[at : at + 1], (8, NB))


def tree(terms):
    terms = list(terms)
    while len(terms) > 1:
        paired = [terms[a] + terms[a + 1] for a in range(0, len(terms) - 1, 2)]
        terms = paired + ([terms[-1]] if len(terms) % 2 else [])
    return terms[0]


def reciprocal(value):
    guess = pltpu.reciprocal(value, approx=True)
    guess = guess * (2.0 - value * guess)
    return guess * (2.0 - value * guess)


def invert_block(ref):
    lane = lax.broadcasted_iota(jnp.int32, (8, NB), 1)
    sub = lax.broadcasted_iota(jnp.int32, (8, NB), 0)

    def group(g, carry):
        base = pl.multiple_of(8 * g, 8)
        panel = ref[pl.ds(base, 8), :]
        columns = [lane_take(panel, base + i) for i in range(8)]
        e = [[None] * 8 for i in range(8)]
        for i in range(8):
            for j in range(i, 8):
                e[i][j] = spread(columns[j], i)

        def get(i, j):
            return e[min(i, j)][max(i, j)]

        for k in range(0, 8, 2):
            a, b, c = e[k][k], e[k][k + 1], e[k + 1][k + 1]
            q = reciprocal(a * c - b * b)
            pa, pb, pc = c * q, -(b * q), a * q
            others = [i for i in range(8) if i not in (k, k + 1)]
            c0 = {i: get(i, k) for i in others}
            c1 = {i: get(i, k + 1) for i in others}
            s0 = {i: c0[i] * pa + c1[i] * pb for i in others}
            s1 = {i: c0[i] * pb + c1[i] * pc for i in others}
            for at, i in enumerate(others):
                for j in others[at:]:
                    e[i][j] = e[i][j] - s0[i] * c0[j] - s1[i] * c1[j]
            for i in others:
                e[min(i, k)][max(i, k)] = s0[i]
                e[min(i, k + 1)][max(i, k + 1)] = s1[i]
            e[k][k], e[k][k + 1], e[k + 1][k + 1] = -pa, -pb, -pc

        inside = (lane >= base) & (lane < base + 8)
        source = [
            jnp.where(inside, jnp.where(lane == base + i, 1.0, 0.0), spread(panel, i)) for i in range(8)
        ]
        rows = [tree([get(i, j) * source[j] for j in range(8)]) for i in range(8)]
        for t in range(NB // 8):
            tile = ref[8 * t : 8 * t + 8, :]
            terms = [jnp.where(inside, 0.0, tile)]
            terms = terms + [lane_take(tile, base + i) * rows[i] for i in range(8)]
            ref[8 * t : 8 * t + 8, :] = tree(terms)
        last = rows[7]
        for i in range(7):
            last = jnp.where(sub == i, rows[i], last)
        ref[pl.ds(base, 8), :] = -last
        return carry

    lax.fori_loop(0, NB // 8, group, 0)


def damped(block, damping, profile):
    row = lax.broadcasted_iota(jnp.int32, (NB, NB), 0)
    col = lax.broadcasted_iota(jnp.int32, (NB, NB), 1)
    return block + jnp.where(row == col, damping * profile, 0.0)


def factor_steps(tri, inv, ratio, vec, solved):
    for p in range(NBLK):
        slot = SLOT[p, p]
        inv[...] = tri[slot * NB : (slot + 1) * NB, :]
        invert_block(inv)
        pivot = inv[...]
        tri[slot * NB : (slot + 1) * NB, :] = pivot
        solved[p] = nn(vec[p], pivot, HIGHEST)
        if p + 1 < NBLK:
            others = range(p + 1, NBLK)
            block = jnp.concatenate([tri[SLOT[p, j] * NB : (SLOT[p, j] + 1) * NB, :] for j in others], axis=1)
            scaled = nn(pivot, block, HIGHEST)
            for j in others:
                at = SLOT[p, j] * NB
                ratio[at : at + NB, :] = scaled[:, (j - p - 1) * NB : (j - p) * NB]
            step = nn(solved[p], block, HIGHEST)
            for i in others:
                off = (i - p - 1) * NB
                change = tn(block[:, off : off + NB], scaled[:, off:], HIGHEST)
                for j in range(i, NBLK):
                    at = SLOT[i, j] * NB
                    tri[at : at + NB, :] = tri[at : at + NB, :] - change[:, (j - i) * NB : (j - i + 1) * NB]
                vec[i] = vec[i] - step[:, off : off + NB]


def regional_kernel(main_ref, prior_ref, tri_ref, ratio_ref, solved_ref, inv, vec):
    scal = main_ref[SUM_AT + PART : SUM_AT + PART + 8, :]
    damping = scal[0:1, 0:1] / scal[0:1, 1:2]
    tri_ref[...] = main_ref[0:TRI, :]
    for p in range(NBLK):
        slot = SLOT[p, p]
        profile = prior_ref[0:1, p * NB : (p + 1) * NB]
        tri_ref[slot * NB : (slot + 1) * NB, :] = damped(
            tri_ref[slot * NB : (slot + 1) * NB, :], damping, profile
        )
        vec[p] = jnp.broadcast_to(main_ref[TRI + p : TRI + p + 1, :], (8, NB))
    ratio_ref[...] = jnp.zeros_like(ratio_ref)
    factor_steps(tri_ref, inv, ratio_ref, vec, solved_ref)


def coupling_kernel(main_ref, rg_ref, tri_ref, ratio_ref, solved_ref, out_ref, gb_ref, b, t, v):
    width = NBLK * NB
    for c in range(NBLK):
        b[:, c * NB : (c + 1) * NB] = rg_ref[c * width : (c + 1) * width, :]
        v[:, c * NB : (c + 1) * NB] = jnp.broadcast_to(
            main_ref[TRI + NBLK + c : TRI + NBLK + c + 1, :], (8, NB)
        )
    t[...] = jnp.zeros_like(t)
    for p in range(NBLK):
        here = b[p * NB : (p + 1) * NB, :]
        slot = SLOT[p, p]
        scaled = nn(tri_ref[slot * NB : (slot + 1) * NB, :], here, HIGHEST)
        gb_ref[p * NB : (p + 1) * NB, :] = scaled
        v[...] = v[...] - nn(solved_ref[p], here, HIGHEST)
        for i in range(p + 1, NBLK):
            at = SLOT[p, i] * NB
            b[i * NB : (i + 1) * NB, :] = b[i * NB : (i + 1) * NB, :] - tn(
                tri_ref[at : at + NB, :], scaled, HIGHEST
            )
        for i in range(NBLK):
            rows = slice(i * NB, (i + 1) * NB)
            t[rows, i * NB :] = t[rows, i * NB :] + tn(here[:, i * NB : (i + 1) * NB], scaled[:, i * NB :], HIGHEST)
    for (i, j), slot in SLOT.items():
        store_split(out_ref, slot, t[i * NB : (i + 1) * NB, j * NB : (j + 1) * NB])
    sub = lax.broadcasted_iota(jnp.int32, (8, NB), 0)
    tail = jnp.zeros((8, NB), f32)
    for c in range(NBLK):
        tail = jnp.where(sub == c, v[:, c * NB : (c + 1) * NB], tail)
    for part in range(REG_PARTS):
        out_ref[part * PART_ROWS + PART : (part + 1) * PART_ROWS, :] = tail


def finish_kernel(
    g_ref, v_ref, main_ref, prior_ref, ratio_ref, solved_ref, gb_ref, red_ref, aux_ref,
    local_ref, regional_ref, global_ref,
    tri, inv, gratio, vec, gsolved,
):
    nparams = local_ref.shape[0]
    width = NBLK * NB
    scal = main_ref[SUM_AT + PART : SUM_AT + PART + 8, :]
    damping = scal[0:1, 0:1] / scal[0:1, 1:2]
    tri[...] = g_ref[...]
    for p in range(NBLK):
        slot = SLOT[p, p]
        profile = prior_ref[0:1, p * NB : (p + 1) * NB]
        tri[slot * NB : (slot + 1) * NB, :] = damped(tri[slot * NB : (slot + 1) * NB, :], damping, profile)
        vec[p] = jnp.broadcast_to(v_ref[p : p + 1, :], (8, NB))
    factor_steps(tri, inv, gratio, vec, gsolved)

    def back(ratio, start):
        found = [None] * NBLK
        for p in reversed(range(NBLK)):
            current = start[p]
            for j in range(p + 1, NBLK):
                at = SLOT[p, j] * NB
                current = current - nt(found[j], ratio[at : at + NB, :], HIGHEST)
            found[p] = current
        return found

    global_step = jnp.concatenate(back(gratio, [gsolved[p] for p in range(NBLK)]), axis=1)
    moved = nt(global_step, gb_ref[...], HIGHEST)
    regional = back(
        ratio_ref, [solved_ref[p] - moved[:, p * NB : (p + 1) * NB] for p in range(NBLK)]
    )
    regional_step = jnp.concatenate(regional, axis=1)
    regional_ref[...] = regional_step[0:1, :]
    global_ref[...] = global_step[0:1, :]

    aux = aux_ref[...]
    at = 0
    factor = [[None] * nparams for a in range(nparams)]
    for a in range(nparams):
        for c in range(a + 1):
            factor[a][c] = aux[:, at : at + 1]
            at += 1
    update = jnp.concatenate([regional_step, global_step], axis=1)
    target = []
    for a in range(nparams):
        target.append(
            aux[:, at : at + 1] - jnp.sum(red_ref[8 * a : 8 * a + 8, :] * update, axis=1, keepdims=True)
        )
        at += 1
    found = backward_small(factor, target)
    sub = lax.broadcasted_iota(jnp.int32, (8, 8), 0)
    lane = lax.broadcasted_iota(jnp.int32, (8, 8), 1)
    for a in range(nparams):
        local_ref[a : a + 1, :] = jnp.sum(jnp.where(sub == lane, found[a], 0.0), axis=0, keepdims=True)


def shape(*dims, dtype=f32):
    return jax.ShapeDtypeStruct(dims, dtype)


VMEM = pl.BlockSpec(memory_space=pltpu.VMEM)
SMEM = pl.BlockSpec(memory_space=pltpu.SMEM)


def call(kernel, out_shape, scratch, specs, flops):
    return pl.pallas_call(
        kernel,
        out_shape=out_shape,
        in_specs=specs,
        out_specs=[VMEM] * len(out_shape),
        scratch_shapes=scratch,
        name=kernel.__name__,
        compiler_params=pltpu.CompilerParams(vmem_limit_bytes=40 * 1024 * 1024),
        cost_estimate=pl.CostEstimate(flops=flops, bytes_accessed=4_000_000, transcendentals=0),
    )


def part_sums(value, axis, parts):
    moved = lax.all_to_all(value, axis, 0, 0, tiled=True)
    return jnp.sum(moved.reshape((parts, value.shape[0] // parts) + value.shape[1:]), axis=0)


def sum_layers(value, nx, nz):
    piece = part_sums(value, "x", nx)
    piece = part_sums(piece, "z", nz)
    copies = jnp.broadcast_to(piece[None], (nz,) + piece.shape).reshape((-1,) + piece.shape[1:])
    whole = lax.all_to_all(copies, "z", 0, 0, tiled=True)
    return lax.all_gather(whole, "x", axis=0, tiled=True)


def body(
    local_jac,
    global_jac,
    coeff_index,
    coeff_weight,
    residual,
    obs_weight,
    obs_count,
    local_prior,
    regional_prior,
    global_prior,
):
    nx, nz = lax.axis_size("x"), lax.axis_size("z")
    rows = residual.shape[0]
    nparams = local_jac.shape[0]
    width = global_jac.shape[1]
    stack = 2 * rows + 6 * RPAD
    gg, main, rg, red, aux = call(
        assemble_kernel,
        [
            shape(REG_PARTS * PART_ROWS, NB),
            shape(SUM_AT, NB),
            shape(NBLK * width, NB),
            shape(RPAD, 2 * width),
            shape(8, NB),
        ],
        [
            pltpu.VMEM((stack, 2 * width), bf16),
            pltpu.VMEM((stack, 2 * width), bf16),
            pltpu.VMEM((NB, 512), f32),
        ],
        [VMEM, VMEM, VMEM, VMEM, VMEM, VMEM, SMEM, VMEM],
        2_000_000_000,
    )(
        local_jac, global_jac, coeff_index, coeff_weight, residual[None], obs_weight[None],
        obs_count, local_prior,
    )
    share = part_sums(gg, GROUPS, REG_PARTS)
    main = jnp.concatenate([main, share, jnp.zeros((MAIN_ROWS - SUM_AT - PART_ROWS, NB), f32)], axis=0)
    main = sum_layers(main, nx, nz)
    rg = sum_layers(rg, nx, nz)
    tri, ratio, solved = call(
        regional_kernel,
        [shape(TRI, NB), shape(TRI, NB), shape(NBLK, 8, NB)],
        [pltpu.VMEM((NB, NB), f32), pltpu.VMEM((NBLK, 8, NB), f32)],
        [VMEM, VMEM],
        20_000_000_000,
    )(main, regional_prior)
    outer, gb = call(
        coupling_kernel,
        [shape(REG_PARTS * PART_ROWS, NB), shape(width, width)],
        [pltpu.VMEM((width, width), f32), pltpu.VMEM((width, width), f32), pltpu.VMEM((8, width), f32)],
        [VMEM] * 5,
        4_000_000_000,
    )(main, rg, tri, ratio, solved)
    outer = part_sums(outer, GROUPS, REG_PARTS)
    mine = main[SUM_AT : SUM_AT + PART] - outer[:PART]
    matrix = lax.all_gather(mine, GROUPS, axis=0, tiled=True)
    local_step, regional_step, global_step = call(
        finish_kernel,
        [shape(nparams, 8), shape(1, width), shape(1, width)],
        [
            pltpu.VMEM((TRI, NB), f32),
            pltpu.VMEM((NB, NB), f32),
            pltpu.VMEM((TRI, NB), f32),
            pltpu.VMEM((NBLK, 8, NB), f32),
            pltpu.VMEM((NBLK, 8, NB), f32),
        ],
        [VMEM] * 9,
        20_000_000_000,
    )(matrix, outer[PART:], main, global_prior[None], ratio, solved, gb, red, aux)
    return local_step, regional_step, global_step[0]


def solution(mesh):
    devices = mesh.devices.reshape(4, 2, 4, 16)
    split = Mesh(devices, ("y", "core", "x", "z"))
    both = GROUPS + LAYERS
    return jax.shard_map(
        body,
        mesh=split,
        in_specs=(
            P(None, both),
            P(both, None),
            P(None, both),
            P(None, both),
            P(both),
            P(both),
            P(both),
            P(None, both),
            P(GROUPS, None),
            P(),
        ),
        out_specs=(P(None, both), P(GROUPS, None), P()),
        check_vma=False,
    )
```

```python
import jax
import jax.numpy as jnp
from jax import lax
from jax.experimental import pallas as pl
from jax.experimental.pallas import tpu as pltpu
from jax.sharding import Mesh, PartitionSpec as P

f32 = jnp.float32
bf16 = jnp.bfloat16
HIGHEST = lax.Precision.HIGHEST

NB = 128
NBLK = 4
PB = 64
PAIRS = [(i, j) for i in range(NBLK) for j in range(i, NBLK)]
SLOT = {pair: at for at, pair in enumerate(PAIRS)}
TRI = len(PAIRS) * NB
REG_PARTS = 8
PART = TRI // REG_PARTS
PART_ROWS = PART + 8
MAIN_ROWS = 1536
SUM_AT = TRI + 8
CHUNK = 48
RPAD = 64

LAYERS = ("x", "z")
GROUPS = ("y", "core")


def tn(a, b, precision=None):
    return lax.dot_general(
        a, b, (((0,), (0,)), ((), ())), precision=precision, preferred_element_type=f32
    )


def nt(a, b, precision=None):
    return lax.dot_general(
        a, b, (((1,), (1,)), ((), ())), precision=precision, preferred_element_type=f32
    )


def nn(a, b, precision=None):
    return jnp.dot(a, b, precision=precision, preferred_element_type=f32)


def pieces(value):
    first = value.astype(bf16)
    rest = value - first.astype(f32)
    second = rest.astype(bf16)
    third = (rest - second.astype(f32)).astype(bf16)
    return first, second, third


def cholesky_small(entries):
    order = len(entries)
    factor = [[None] * order for i in range(order)]
    for j in range(order):
        diagonal = entries[j][j]
        for k in range(j):
            diagonal = diagonal - factor[j][k] * factor[j][k]
        factor[j][j] = jnp.sqrt(diagonal)
        for i in range(j + 1, order):
            current = entries[i][j]
            for k in range(j):
                current = current - factor[i][k] * factor[j][k]
            factor[i][j] = current / factor[j][j]
    return factor


def forward_small(factor, target):
    result = []
    for a in range(len(target)):
        current = target[a]
        for k in range(a):
            current = current - factor[a][k] * result[k]
        result.append(current / factor[a][a])
    return result


def backward_small(factor, target):
    order = len(target)
    result = [None] * order
    for a in reversed(range(order)):
        current = target[a]
        for k in range(a + 1, order):
            current = current - factor[k][a] * result[k]
        result[a] = current / factor[a][a]
    return result


def store_split(ref, slot, block):
    done = 0
    while done < NB:
        flat = slot * NB + done
        part, off = flat // PART, flat % PART
        take = min(NB - done, PART - off)
        start = part * PART_ROWS + off
        ref[start : start + take, :] = block[done : done + take]
        done += take


def assemble_kernel(
    lj_ref, gj_ref, ci_ref, cw_ref, res_ref, ow_ref, cnt_ref, lp_ref, rp_ref, gp_ref,
    gg_ref, main_ref, rg_ref, red_ref, aux_ref, prior_ref,
    left, right, padded,
):
    rows = gj_ref.shape[0]
    nparams = lj_ref.shape[0]
    objects = 8
    observed = rows // objects
    width = gj_ref.shape[1]
    res = res_ref[...]
    prior_ref[:, :width] = jnp.broadcast_to(rp_ref[...], (8, width))
    prior_ref[:, width:] = jnp.broadcast_to(gp_ref[...], (8, width))
    position = lax.broadcasted_iota(jnp.int32, (objects, rows), 1)
    owner = lax.broadcasted_iota(jnp.int32, (objects, rows), 0)
    count = jnp.zeros((objects, rows), jnp.int32)
    for n in range(objects):
        count = jnp.where(owner == n, cnt_ref[n], count)
    local = position - owner * observed
    present = (local >= 0) & (local < observed) & (local < count)
    live = jnp.where(present, jnp.broadcast_to(ow_ref[...], (objects, rows)), 0.0)
    weight = jnp.sum(live, axis=0, keepdims=True)
    misfit = jnp.sum(weight * res * res, axis=1, keepdims=True)
    counted = jnp.sum(
        jnp.sum(jnp.where(present, 1.0, 0.0), axis=0, keepdims=True), axis=1, keepdims=True
    )

    padded[...] = jnp.zeros_like(padded)
    padded[0:1, :rows] = weight
    padded[1:5, :rows] = ci_ref[...].astype(f32)
    padded[5:9, :rows] = cw_ref[...].astype(f32)
    for block in range(padded.shape[1] // NB):
        columns = padded[:, block * NB : (block + 1) * NB].T
        low = block * NB
        while low < min((block + 1) * NB, rows):
            high = min(low + 32, rows)
            here = columns[low - block * NB : high - block * NB]
            weights = here[:, 0:1]
            lanes = lax.broadcasted_iota(jnp.int32, (high - low, width), 1).astype(f32)
            total = jnp.zeros((high - low, width), f32)
            for k in range(4):
                total = total + jnp.where(here[:, 1 + k : 2 + k] == lanes, here[:, 5 + k : 6 + k], 0.0)
            joined = total.astype(bf16)
            for at, value in ((0, joined), (width, gj_ref[low:high, :])):
                scaled = (value.astype(f32) * weights).astype(bf16)
                right[low:high, at : at + width] = value
                right[rows + low : rows + high, at : at + width] = scaled
                left[low:high, at : at + width] = (scaled.astype(f32) * 0.5).astype(bf16)
                left[rows + low : rows + high, at : at + width] = (value.astype(f32) * 0.5).astype(bf16)
            low = high

    jac = lj_ref[...].astype(f32)
    weighted = [jac[a : a + 1, :] * live for a in range(nparams)]
    entries = [[None] * nparams for a in range(nparams)]
    owner8 = lax.broadcasted_iota(jnp.int32, (objects, objects), 0)
    lane8 = lax.broadcasted_iota(jnp.int32, (objects, objects), 1)
    for a in range(nparams):
        for b in range(a + 1):
            value = jnp.sum(weighted[a] * jac[b : b + 1, :], axis=1, keepdims=True)
            if a == b:
                prior = jnp.broadcast_to(lp_ref[a : a + 1, :], (objects, objects))
                value = value + jnp.sum(jnp.where(owner8 == lane8, prior, 0.0), axis=1, keepdims=True)
            entries[a][b] = value
    factor = cholesky_small(entries)
    local_gradient = [jnp.sum(weighted[a] * res, axis=1, keepdims=True) for a in range(nparams)]
    reduced_gradient = forward_small(factor, local_gradient)

    blank = jnp.zeros((8, rows), f32)
    stacked = jnp.concatenate(weighted + [blank], axis=0)
    everything = right[0:rows, :]
    coupling = None
    for piece in pieces(stacked):
        term = nn(piece, everything)
        coupling = term if coupling is None else coupling + term
    reduced = forward_small(factor, [coupling[8 * a : 8 * a + 8] for a in range(nparams)])
    joint = jnp.concatenate(reduced + [jnp.zeros((8, 2 * width), f32)], axis=0)
    red_ref[...] = joint
    r0, r1, r2 = pieces(joint)
    base = 2 * rows
    for at, (one, two) in enumerate(((r0, r0), (r0, r1), (r1, r0), (r1, r1), (r0, r2), (r2, r0))):
        left[base + at * RPAD : base + (at + 1) * RPAD, :] = -one
        right[base + at * RPAD : base + (at + 1) * RPAD, :] = two

    lane = lax.broadcasted_iota(jnp.int32, (objects, NB), 1)
    aux = jnp.zeros((objects, NB), f32)
    at = 0
    for a in range(nparams):
        for b in range(a + 1):
            aux = jnp.where(lane == at, factor[a][b], aux)
            at += 1
    for a in range(nparams):
        aux = jnp.where(lane == at, reduced_gradient[a], aux)
        at += 1
    aux_ref[...] = aux

    first, second, third = pieces(res)
    lhs = jnp.concatenate(
        [first.astype(f32), second.astype(f32), third.astype(f32), jnp.zeros((13, rows), f32)], axis=0
    ).astype(bf16)
    gradient = jnp.sum(nn(lhs, right[rows : 2 * rows, :]), axis=0, keepdims=True)
    for a in range(nparams):
        gradient = gradient - jnp.sum(reduced_gradient[a] * reduced[a], axis=0, keepdims=True)
    for at in range(8):
        main_ref[TRI + at : TRI + at + 1, :] = gradient[:, at * NB : (at + 1) * NB]

    row_lane = lax.broadcasted_iota(jnp.int32, (8, NB), 1)
    scalars = jnp.where(row_lane == 0, misfit, jnp.where(row_lane == 1, counted, 0.0))
    for part in range(REG_PARTS):
        gg_ref[part * PART_ROWS + PART : (part + 1) * PART_ROWS, :] = scalars
    for i in range(NBLK):
        for half in range(2):
            at = half * width
            value = tn(left[:, at + i * NB : at + (i + 1) * NB], right[:, at + i * NB : at + width])
            for j in range(i, NBLK):
                block = value[:, (j - i) * NB : (j - i + 1) * NB]
                slot = SLOT[i, j]
                if half == 0:
                    main_ref[slot * NB : (slot + 1) * NB, :] = block
                else:
                    store_split(gg_ref, slot, block)
        value = 2.0 * tn(left[0:rows, i * NB : (i + 1) * NB], right[0:rows, width:]) + tn(
            left[base:, i * NB : (i + 1) * NB], right[base:, width:]
        )
        for c in range(NBLK):
            rg_ref[c * width + i * NB : c * width + (i + 1) * NB, :] = value[:, c * NB : (c + 1) * NB]


def spread(value, at):
    return jnp.broadcast_to(value[at : at + 1], (8, 128))


def reciprocal(value):
    guess = pltpu.reciprocal(value, approx=True)
    return guess * (2.0 - value * guess)


def invert_pivot(ref):
    lane = lax.broadcasted_iota(jnp.int32, (8, 128), 1)
    sub = lax.broadcasted_iota(jnp.int32, (8, 128), 0)
    col = lane & (PB - 1)
    half = lane - col
    tiles = PB // 16

    def pick(value, index):
        return jnp.take_along_axis(value, index, axis=1)

    def group(g, carry):
        at = pl.multiple_of(8 * lax.rem(g, tiles), 8)
        side = lax.div(g, tiles) * PB
        base = 8 * g
        source = ref[pl.ds(at, 8), :]
        panel = pick(source, col + side)
        columns = [pick(source, jnp.full((8, 128), side + base + j, jnp.int32)) for j in range(8)]
        for k in range(0, 8, 2):
            c0, c1 = columns[k], columns[k + 1]
            a, b, c = spread(c0, k), spread(c1, k), spread(c1, k + 1)
            q = reciprocal(a * c - b * b)
            pa, pb, pc = c * q, b * q, a * q
            s0, s1 = sub == k, sub == k + 1
            m0, m1 = col == base + k, col == base + k + 1
            r0 = jnp.where(m0, 1.0, jnp.where(m1, 0.0, spread(panel, k)))
            r1 = jnp.where(m1, 1.0, jnp.where(m0, 0.0, spread(panel, k + 1)))
            n0 = pa * r0 - pb * r1
            n1 = pc * r1 - pb * r0
            rest = jnp.where(m0 | m1, 0.0, panel) - c0 * n0 - c1 * n1
            panel = jnp.where(s0, n0, jnp.where(s1, n1, rest))
            for j in range(k + 2, 8):
                r0, r1 = spread(columns[j], k), spread(columns[j], k + 1)
                n0 = pa * r0 - pb * r1
                n1 = pc * r1 - pb * r0
                columns[j] = jnp.where(s0, n0, jnp.where(s1, n1, columns[j] - c0 * n0 - c1 * n1))
        rows = [spread(panel, i) for i in range(8)]
        inside = (col >= base) & (col < base + 8)
        for t in range(tiles):
            tile = ref[8 * t : 8 * t + 8, :]
            terms = [pick(tile, half + (base + i)) * rows[i] for i in range(8)]
            kept = jnp.where(inside, 0.0, tile) - terms[0]
            ref[8 * t : 8 * t + 8, :] = (kept - terms[1] - (terms[2] + terms[3])) - (
                (terms[4] + terms[5]) + (terms[6] + terms[7])
            )
        here = ref[pl.ds(at, 8), :]
        ref[pl.ds(at, 8), :] = jnp.where(half == side, panel, here)
        return carry

    lax.fori_loop(0, PB // 8, group, 0)


def split_product(a, b):
    a0, a1, a2 = pieces(a)
    b0, b1, b2 = pieces(b)
    left = jnp.concatenate([a0, a0, a1, a1, a0, a2], axis=0)
    right = jnp.concatenate([b0, b1, b0, b1, b2, b0], axis=0)
    return tn(left, right)


def eliminate(a, packed, lower_ref, pivot_ref):
    size = NBLK * NB
    lane = lax.broadcasted_iota(jnp.int32, (PB, size), 1)
    sub = lax.broadcasted_iota(jnp.int32, (PB, size), 0)
    lane32 = lax.broadcasted_iota(jnp.int32, (PB // 2, 128), 1)
    first = lane32 < PB
    for p in range(size // PB):
        r0 = PB * p
        c0 = 128 * (p // 2)
        odd = p % 2 == 1
        row = a[r0 : r0 + PB, :]
        tile = row[:, c0 : c0 + 128]
        turned = pltpu.roll(tile, PB, 1)
        one, two = (turned, tile) if odd else (tile, turned)
        packed[...] = jnp.where(first, one[: PB // 2], two[PB // 2 :])
        invert_pivot(packed)
        inverse = packed[...]
        moved = pltpu.roll(inverse, PB, 1)
        pivot = jnp.concatenate([jnp.where(first, inverse, 0.0), jnp.where(first, moved, 0.0)], axis=0)
        if odd:
            placed = jnp.concatenate([jnp.where(first, 0.0, moved), jnp.where(first, 0.0, inverse)], axis=0)
        else:
            placed = pivot
        pivot_ref[r0 : r0 + PB, :] = placed
        unit = jnp.where(lane == sub + r0, 1.0, 0.0)
        lower_ref[r0 : r0 + PB, :] = jnp.where(lane < r0, row, unit)
        if r0 + PB < size:
            inside = (lane >= r0) & (lane < r0 + PB)
            scaled = split_product(pivot[:, :PB], jnp.where(inside, unit, row))
            c1 = 128 * ((p + 1) // 2)
            below = jnp.where(lane >= r0 + PB, row, 0.0)[:, c1:]
            change = split_product(below, scaled)
            wide = lax.broadcasted_iota(jnp.int32, (size - c1, 128), 1)
            own = (wide >= r0 - c0) & (wide < r0 - c0 + PB)
            a[c1:, c0 : c0 + 128] = jnp.where(own, 0.0, a[c1:, c0 : c0 + 128])
            a[c1:, :] = a[c1:, :] - change


def damped(block, damping, profile):
    row = lax.broadcasted_iota(jnp.int32, (NB, NB), 0)
    col = lax.broadcasted_iota(jnp.int32, (NB, NB), 1)
    return block + jnp.where(row == col, damping * profile, 0.0)


def unpack(source, a, damping, profile):
    a[...] = jnp.zeros_like(a)
    for (i, j), slot in SLOT.items():
        block = source[slot * NB : (slot + 1) * NB, :]
        if i == j:
            block = damped(block, damping, profile[:, i * NB : (i + 1) * NB])
        a[i * NB : (i + 1) * NB, j * NB : (j + 1) * NB] = block


def read_damping(main_ref):
    scal = main_ref[SUM_AT + PART : SUM_AT + PART + 8, :]
    return scal[0:1, 0:1] / scal[0:1, 1:2]


def pivot_times(pivot_ref, row):
    return jnp.concatenate(
        [nn(row[:, i * NB : (i + 1) * NB], pivot_ref[i * NB : (i + 1) * NB, :], HIGHEST) for i in range(NBLK)],
        axis=1,
    )


def wide_row(ref, at):
    return jnp.concatenate(
        [jnp.broadcast_to(ref[at + c : at + c + 1, :], (8, NB)) for c in range(NBLK)], axis=1
    )


def regional_kernel(main_ref, prior_ref, lower_ref, pivot_ref, a, packed):
    unpack(main_ref, a, read_damping(main_ref), prior_ref[0:1, : NBLK * NB])
    eliminate(a, packed, lower_ref, pivot_ref)


def coupling_kernel(main_ref, rg_ref, lower_ref, pivot_ref, out_ref, scaled_ref, q_ref, b, u):
    width = NBLK * NB
    for c in range(NBLK):
        b[:, c * NB : (c + 1) * NB] = rg_ref[c * width : (c + 1) * width, :]
    for i in range(NBLK):
        rows = slice(i * NB, (i + 1) * NB)
        value = nn(lower_ref[rows, : (i + 1) * NB], b[: (i + 1) * NB, :], HIGHEST)
        u[rows, :] = value
        scaled_ref[rows, :] = nn(pivot_ref[rows, :], value, HIGHEST)
    for i in range(NBLK):
        value = tn(u[:, i * NB : (i + 1) * NB], scaled_ref[:, i * NB :], HIGHEST)
        for j in range(i, NBLK):
            store_split(out_ref, SLOT[i, j], value[:, (j - i) * NB : (j - i + 1) * NB])
    q = pivot_times(pivot_ref, nt(wide_row(main_ref, TRI), lower_ref[...], HIGHEST))
    q_ref[...] = q
    v = wide_row(main_ref, TRI + NBLK) - nn(q, u[...], HIGHEST)
    sub = lax.broadcasted_iota(jnp.int32, (8, NB), 0)
    tail = jnp.zeros((8, NB), f32)
    for c in range(NBLK):
        tail = jnp.where(sub == c, v[:, c * NB : (c + 1) * NB], tail)
    for part in range(REG_PARTS):
        out_ref[part * PART_ROWS + PART : (part + 1) * PART_ROWS, :] = tail


def finish_kernel(
    g_ref, v_ref, main_ref, prior_ref, flower_ref, scaled_ref, q_ref, red_ref, aux_ref,
    local_ref, regional_ref, global_ref,
    a, packed, lower, pivot,
):
    nparams = local_ref.shape[0]
    width = NBLK * NB
    unpack(g_ref, a, read_damping(main_ref), prior_ref[0:1, width:])
    eliminate(a, packed, lower, pivot)
    whole = lower[...]
    forward = pivot_times(pivot, nt(wide_row(v_ref, 0), whole, HIGHEST))
    global_step = nn(forward, whole, HIGHEST)
    regional_step = nn(q_ref[...] - nt(global_step, scaled_ref[...], HIGHEST), flower_ref[...], HIGHEST)
    regional_ref[...] = regional_step[0:1, :]
    global_ref[...] = global_step[0:1, :]

    aux = aux_ref[...]
    at = 0
    factor = [[None] * nparams for i in range(nparams)]
    for i in range(nparams):
        for c in range(i + 1):
            factor[i][c] = aux[:, at : at + 1]
            at += 1
    update = jnp.concatenate([regional_step, global_step], axis=1)
    target = []
    for i in range(nparams):
        target.append(
            aux[:, at : at + 1] - jnp.sum(red_ref[8 * i : 8 * i + 8, :] * update, axis=1, keepdims=True)
        )
        at += 1
    found = backward_small(factor, target)
    sub = lax.broadcasted_iota(jnp.int32, (8, 8), 0)
    lane = lax.broadcasted_iota(jnp.int32, (8, 8), 1)
    for i in range(nparams):
        local_ref[i : i + 1, :] = jnp.sum(jnp.where(sub == lane, found[i], 0.0), axis=0, keepdims=True)


def shape(*dims, dtype=f32):
    return jax.ShapeDtypeStruct(dims, dtype)


VMEM = pl.BlockSpec(memory_space=pltpu.VMEM)
SMEM = pl.BlockSpec(memory_space=pltpu.SMEM)


def whole_block(dims):
    return pl.BlockSpec(dims, lambda i: (0,) * len(dims))


def call(kernel, out_shape, scratch, specs, flops, grid=()):
    return pl.pallas_call(
        kernel,
        grid=grid,
        out_shape=out_shape,
        in_specs=specs,
        out_specs=[VMEM] * len(out_shape),
        scratch_shapes=scratch,
        name=kernel.__name__,
        compiler_params=pltpu.CompilerParams(vmem_limit_bytes=40 * 1024 * 1024),
        cost_estimate=pl.CostEstimate(flops=flops, bytes_accessed=4_000_000, transcendentals=0),
    )


def part_sums(value, axis, parts):
    moved = lax.all_to_all(value, axis, 0, 0, tiled=True)
    return jnp.sum(moved.reshape((parts, value.shape[0] // parts) + value.shape[1:]), axis=0)


def copies_back(piece, axis, parts):
    copies = jnp.broadcast_to(piece[None], (parts,) + piece.shape).reshape((-1,) + piece.shape[1:])
    return lax.all_to_all(copies, axis, 0, 0, tiled=True)


def body(
    local_jac,
    global_jac,
    coeff_index,
    coeff_weight,
    residual,
    obs_weight,
    obs_count,
    local_prior,
    regional_prior,
    global_prior,
):
    nx, nz = lax.axis_size("x"), lax.axis_size("z")
    rows = residual.shape[0]
    nparams = local_jac.shape[0]
    width = global_jac.shape[1]
    stack = 2 * rows + 6 * RPAD
    gg, main, rg, red, aux, prior = call(
        assemble_kernel,
        [
            shape(REG_PARTS * PART_ROWS, NB),
            shape(SUM_AT, NB),
            shape(NBLK * width, NB),
            shape(RPAD, 2 * width),
            shape(8, NB),
            shape(8, 2 * width),
        ],
        [
            pltpu.VMEM((stack, 2 * width), bf16),
            pltpu.VMEM((stack, 2 * width), bf16),
            pltpu.VMEM((NB, 512), f32),
        ],
        [
            whole_block(local_jac.shape), whole_block(global_jac.shape), whole_block(coeff_index.shape),
            whole_block(coeff_weight.shape), whole_block((1, rows)), whole_block((1, rows)), SMEM,
            whole_block(local_prior.shape), whole_block((1, width)), whole_block((1, width)),
        ],
        2_000_000_000,
        grid=(1,),
    )(
        local_jac, global_jac, coeff_index, coeff_weight, residual[None], obs_weight[None],
        obs_count, local_prior, regional_prior, global_prior[None],
    )
    share = part_sums(gg, GROUPS, REG_PARTS)
    rg = lax.psum_scatter(rg, "x", scatter_dimension=0, tiled=True)
    main = jnp.concatenate([main, share, jnp.zeros((MAIN_ROWS - SUM_AT - PART_ROWS, NB), f32)], axis=0)
    main = part_sums(main, "x", nx)
    both = part_sums(jnp.concatenate([main, rg], axis=0), "z", nz)
    both = copies_back(both, "z", nz)
    main = lax.all_gather(both[: MAIN_ROWS // nx], "x", axis=0, tiled=True)
    main, rg = lax.optimization_barrier((main, both[MAIN_ROWS // nx :]))
    rg = copies_back(rg, "x", nx)
    lower, pivot = call(
        regional_kernel,
        [shape(width, width), shape(width, NB)],
        [pltpu.VMEM((width, width), f32), pltpu.VMEM((PB // 2, 128), f32)],
        [VMEM] * 2,
        20_000_000_000,
    )(main, prior)
    outer, scaled, q = call(
        coupling_kernel,
        [shape(REG_PARTS * PART_ROWS, NB), shape(width, width), shape(8, width)],
        [pltpu.VMEM((width, width), f32), pltpu.VMEM((width, width), f32)],
        [VMEM] * 4,
        4_000_000_000,
    )(main, rg, lower, pivot)
    outer = part_sums(outer, GROUPS, REG_PARTS)
    mine = main[SUM_AT : SUM_AT + PART] - outer[:PART]
    matrix = lax.all_gather(mine, GROUPS, axis=0, tiled=True)
    local_step, regional_step, global_step = call(
        finish_kernel,
        [shape(nparams, 8), shape(1, width), shape(1, width)],
        [
            pltpu.VMEM((width, width), f32),
            pltpu.VMEM((PB // 2, 128), f32),
            pltpu.VMEM((width, width), f32),
            pltpu.VMEM((width, NB), f32),
        ],
        [VMEM] * 9,
        20_000_000_000,
    )(matrix, outer[PART:], main, prior, lower, scaled, q, red, aux)
    return local_step, regional_step, global_step[0]


def solution(mesh):
    devices = mesh.devices.reshape(4, 2, 4, 16)
    split = Mesh(devices, ("y", "core", "x", "z"))
    both = GROUPS + LAYERS
    return jax.shard_map(
        body,
        mesh=split,
        in_specs=(
            P(None, both),
            P(both, None),
            P(None, both),
            P(None, both),
            P(both),
            P(both),
            P(both),
            P(None, both),
            P(GROUPS, None),
            P(),
        ),
        out_specs=(P(None, both), P(GROUPS, None), P()),
        check_vma=False,
    )
```

```python
import jax
import jax.numpy as jnp
from jax import lax
from jax.experimental import pallas as pl
from jax.experimental.pallas import tpu as pltpu
from jax.sharding import Mesh, PartitionSpec as P

f32 = jnp.float32
bf16 = jnp.bfloat16
HIGHEST = lax.Precision.HIGHEST

NB = 128
NBLK = 4
PB = 64
PAIRS = [(i, j) for i in range(NBLK) for j in range(i, NBLK)]
SLOT = {pair: at for at, pair in enumerate(PAIRS)}
TRI = len(PAIRS) * NB
REG_PARTS = 8
PART = TRI // REG_PARTS
PART_ROWS = PART + 8
MAIN_PART = TRI // 4
MAIN_PITCH = 384
SUM_AT = MAIN_PART + 8
CHUNK = 48
RPAD = 64

LAYERS = ("x", "z")
GROUPS = ("y", "core")


def tn(a, b, precision=None):
    return lax.dot_general(
        a, b, (((0,), (0,)), ((), ())), precision=precision, preferred_element_type=f32
    )


def nt(a, b, precision=None):
    return lax.dot_general(
        a, b, (((1,), (1,)), ((), ())), precision=precision, preferred_element_type=f32
    )


def nn(a, b, precision=None):
    return jnp.dot(a, b, precision=precision, preferred_element_type=f32)


def pieces(value):
    first = value.astype(bf16)
    rest = value - first.astype(f32)
    second = rest.astype(bf16)
    third = (rest - second.astype(f32)).astype(bf16)
    return first, second, third


def cholesky_small(entries):
    order = len(entries)
    factor = [[None] * order for i in range(order)]
    for j in range(order):
        diagonal = entries[j][j]
        for k in range(j):
            diagonal = diagonal - factor[j][k] * factor[j][k]
        factor[j][j] = jnp.sqrt(diagonal)
        for i in range(j + 1, order):
            current = entries[i][j]
            for k in range(j):
                current = current - factor[i][k] * factor[j][k]
            factor[i][j] = current / factor[j][j]
    return factor


def forward_small(factor, target):
    result = []
    for a in range(len(target)):
        current = target[a]
        for k in range(a):
            current = current - factor[a][k] * result[k]
        result.append(current / factor[a][a])
    return result


def backward_small(factor, target):
    order = len(target)
    result = [None] * order
    for a in reversed(range(order)):
        current = target[a]
        for k in range(a + 1, order):
            current = current - factor[k][a] * result[k]
        result[a] = current / factor[a][a]
    return result


def spans(slot, part, pitch):
    done = 0
    while done < NB:
        flat = slot * NB + done
        take = min(NB - done, part - flat % part)
        yield done, take, flat // part * pitch + flat % part
        done += take


def store_split(ref, slot, block, part=PART, pitch=PART_ROWS):
    for done, take, start in spans(slot, part, pitch):
        ref[start : start + take, :] = block[done : done + take]


def presence(cnt_ref, rows, objects=8):
    position = lax.broadcasted_iota(jnp.int32, (objects, rows), 1)
    owner = lax.broadcasted_iota(jnp.int32, (objects, rows), 0)
    count = jnp.zeros((objects, rows), jnp.int32)
    for n in range(objects):
        count = jnp.where(owner == n, cnt_ref[n], count)
    local = position - owner * (rows // objects)
    return (local >= 0) & (local < rows // objects) & (local < count)


def misfit_kernel(res_ref, ow_ref, cnt_ref, out_ref):
    rows = res_ref.shape[1]
    present = presence(cnt_ref, rows)
    value = jnp.where(present, ow_ref[...] * res_ref[...] * res_ref[...], 0.0)
    misfit = jnp.sum(jnp.sum(value, axis=0, keepdims=True), axis=1, keepdims=True)
    counted = jnp.sum(
        jnp.sum(jnp.where(present, 1.0, 0.0), axis=0, keepdims=True), axis=1, keepdims=True
    )
    lane = lax.broadcasted_iota(jnp.int32, out_ref.shape, 1)
    row = lax.broadcasted_iota(jnp.int32, out_ref.shape, 0) % 8
    out_ref[...] = jnp.where(row == 0, jnp.where(lane == 0, misfit, jnp.where(lane == 1, counted, 0.0)), 0.0)


def assemble_kernel(
    lj_ref, gj_ref, ci_ref, cw_ref, res_ref, ow_ref, cnt_ref, lp_ref, rp_ref, gp_ref,
    gg_ref, main_ref, rg_ref, red_ref, aux_ref, prior_ref,
    left, right, padded,
):
    rows = gj_ref.shape[0]
    nparams = lj_ref.shape[0]
    objects = 8
    observed = rows // objects
    width = gj_ref.shape[1]
    res = res_ref[...]
    prior_ref[:, :width] = jnp.broadcast_to(rp_ref[...], (8, width))
    prior_ref[:, width:] = jnp.broadcast_to(gp_ref[...], (8, width))
    live = jnp.where(presence(cnt_ref, rows), jnp.broadcast_to(ow_ref[...], (objects, rows)), 0.0)
    weight = jnp.sum(live, axis=0, keepdims=True)

    padded[...] = jnp.zeros_like(padded)
    padded[0:1, :rows] = weight
    padded[1:5, :rows] = ci_ref[...].astype(f32)
    padded[5:9, :rows] = cw_ref[...].astype(f32)
    for block in range(padded.shape[1] // NB):
        columns = padded[:, block * NB : (block + 1) * NB].T
        low = block * NB
        while low < min((block + 1) * NB, rows):
            high = min(low + 32, rows)
            here = columns[low - block * NB : high - block * NB]
            weights = here[:, 0:1]
            lanes = lax.broadcasted_iota(jnp.int32, (high - low, width), 1).astype(f32)
            total = jnp.zeros((high - low, width), f32)
            for k in range(4):
                total = total + jnp.where(here[:, 1 + k : 2 + k] == lanes, here[:, 5 + k : 6 + k], 0.0)
            joined = total.astype(bf16)
            for at, value in ((0, joined), (width, gj_ref[low:high, :])):
                scaled = (value.astype(f32) * weights).astype(bf16)
                right[low:high, at : at + width] = value
                right[rows + low : rows + high, at : at + width] = scaled
                left[low:high, at : at + width] = (scaled.astype(f32) * 0.5).astype(bf16)
                left[rows + low : rows + high, at : at + width] = (value.astype(f32) * 0.5).astype(bf16)
            low = high

    jac = lj_ref[...].astype(f32)
    weighted = [jac[a : a + 1, :] * live for a in range(nparams)]
    entries = [[None] * nparams for a in range(nparams)]
    owner8 = lax.broadcasted_iota(jnp.int32, (objects, objects), 0)
    lane8 = lax.broadcasted_iota(jnp.int32, (objects, objects), 1)
    for a in range(nparams):
        for b in range(a + 1):
            value = jnp.sum(weighted[a] * jac[b : b + 1, :], axis=1, keepdims=True)
            if a == b:
                prior = jnp.broadcast_to(lp_ref[a : a + 1, :], (objects, objects))
                value = value + jnp.sum(jnp.where(owner8 == lane8, prior, 0.0), axis=1, keepdims=True)
            entries[a][b] = value
    factor = cholesky_small(entries)
    local_gradient = [jnp.sum(weighted[a] * res, axis=1, keepdims=True) for a in range(nparams)]
    reduced_gradient = forward_small(factor, local_gradient)

    blank = jnp.zeros((8, rows), f32)
    stacked = jnp.concatenate(weighted + [blank], axis=0)
    everything = right[0:rows, :]
    coupling = None
    for piece in pieces(stacked):
        term = nn(piece, everything)
        coupling = term if coupling is None else coupling + term
    reduced = forward_small(factor, [coupling[8 * a : 8 * a + 8] for a in range(nparams)])
    joint = jnp.concatenate(reduced + [jnp.zeros((8, 2 * width), f32)], axis=0)
    red_ref[...] = joint
    r0, r1, r2 = pieces(joint)
    base = 2 * rows
    for at, (one, two) in enumerate(((r0, r0), (r0, r1), (r1, r0), (r1, r1), (r0, r2), (r2, r0))):
        left[base + at * RPAD : base + (at + 1) * RPAD, :] = -one
        right[base + at * RPAD : base + (at + 1) * RPAD, :] = two

    lane = lax.broadcasted_iota(jnp.int32, (objects, NB), 1)
    aux = jnp.zeros((objects, NB), f32)
    at = 0
    for a in range(nparams):
        for b in range(a + 1):
            aux = jnp.where(lane == at, factor[a][b], aux)
            at += 1
    for a in range(nparams):
        aux = jnp.where(lane == at, reduced_gradient[a], aux)
        at += 1
    aux_ref[...] = aux

    first, second, third = pieces(res)
    lhs = jnp.concatenate(
        [first.astype(f32), second.astype(f32), third.astype(f32), jnp.zeros((13, rows), f32)], axis=0
    ).astype(bf16)
    gradient = jnp.sum(nn(lhs, right[rows : 2 * rows, :]), axis=0, keepdims=True)
    for a in range(nparams):
        gradient = gradient - jnp.sum(reduced_gradient[a] * reduced[a], axis=0, keepdims=True)
    for part in range(4):
        main_ref[part * MAIN_PITCH + MAIN_PART : (part + 1) * MAIN_PITCH, :] = jnp.zeros(
            (MAIN_PITCH - MAIN_PART, NB), f32
        )
        for at in range(2):
            line = 2 * part + at
            main_ref[part * MAIN_PITCH + MAIN_PART + at : part * MAIN_PITCH + MAIN_PART + at + 1, :] = (
                gradient[:, line * NB : (line + 1) * NB]
            )
    for i in range(NBLK):
        for half in range(2):
            at = half * width
            value = tn(left[:, at + i * NB : at + (i + 1) * NB], right[:, at + i * NB : at + width])
            for j in range(i, NBLK):
                block = value[:, (j - i) * NB : (j - i + 1) * NB]
                slot = SLOT[i, j]
                if half == 0:
                    store_split(main_ref, slot, block, MAIN_PART, MAIN_PITCH)
                else:
                    gg_ref[slot * NB : (slot + 1) * NB, :] = block
        value = 2.0 * tn(left[0:rows, i * NB : (i + 1) * NB], right[0:rows, width:]) + tn(
            left[base:, i * NB : (i + 1) * NB], right[base:, width:]
        )
        for c in range(NBLK):
            rg_ref[c * width + i * NB : c * width + (i + 1) * NB, :] = value[:, c * NB : (c + 1) * NB]


def spread(value, at):
    return jnp.broadcast_to(value[at : at + 1], (8, 128))


def reciprocal(value):
    guess = pltpu.reciprocal(value, approx=True)
    return guess * (2.0 - value * guess)


def invert_pivot(ref):
    lane = lax.broadcasted_iota(jnp.int32, (8, 128), 1)
    sub = lax.broadcasted_iota(jnp.int32, (8, 128), 0)
    col = lane & (PB - 1)
    half = lane - col
    tiles = PB // 16

    def pick(value, index):
        return jnp.take_along_axis(value, index, axis=1)

    def group(g, carry):
        at = pl.multiple_of(8 * lax.rem(g, tiles), 8)
        side = lax.div(g, tiles) * PB
        base = 8 * g
        source = ref[pl.ds(at, 8), :]
        panel = pick(source, col + side)
        columns = [pick(source, jnp.full((8, 128), side + base + j, jnp.int32)) for j in range(8)]
        for k in range(0, 8, 2):
            c0, c1 = columns[k], columns[k + 1]
            a, b, c = spread(c0, k), spread(c1, k), spread(c1, k + 1)
            q = reciprocal(a * c - b * b)
            pa, pb, pc = c * q, b * q, a * q
            s0, s1 = sub == k, sub == k + 1
            m0, m1 = col == base + k, col == base + k + 1
            r0 = jnp.where(m0, 1.0, jnp.where(m1, 0.0, spread(panel, k)))
            r1 = jnp.where(m1, 1.0, jnp.where(m0, 0.0, spread(panel, k + 1)))
            n0 = pa * r0 - pb * r1
            n1 = pc * r1 - pb * r0
            rest = jnp.where(m0 | m1, 0.0, panel) - c0 * n0 - c1 * n1
            panel = jnp.where(s0, n0, jnp.where(s1, n1, rest))
            for j in range(k + 2, 8):
                r0, r1 = spread(columns[j], k), spread(columns[j], k + 1)
                n0 = pa * r0 - pb * r1
                n1 = pc * r1 - pb * r0
                columns[j] = jnp.where(s0, n0, jnp.where(s1, n1, columns[j] - c0 * n0 - c1 * n1))
        rows = [spread(panel, i) for i in range(8)]
        inside = (col >= base) & (col < base + 8)
        for t in range(tiles):
            tile = ref[8 * t : 8 * t + 8, :]
            terms = [pick(tile, half + (base + i)) * rows[i] for i in range(8)]
            kept = jnp.where(inside, 0.0, tile) - terms[0]
            ref[8 * t : 8 * t + 8, :] = (kept - terms[1] - (terms[2] + terms[3])) - (
                (terms[4] + terms[5]) + (terms[6] + terms[7])
            )
        here = ref[pl.ds(at, 8), :]
        ref[pl.ds(at, 8), :] = jnp.where(half == side, panel, here)
        return carry

    lax.fori_loop(0, PB // 8, group, 0)


def split_product(a, b):
    a0, a1, a2 = pieces(a)
    b0, b1, b2 = pieces(b)
    left = jnp.concatenate([a0, a0, a1, a1, a0, a2], axis=0)
    right = jnp.concatenate([b0, b1, b0, b1, b2, b0], axis=0)
    return tn(left, right)


def eliminate(a, packed, lower_ref, pivot_ref):
    size = NBLK * NB
    lane = lax.broadcasted_iota(jnp.int32, (PB, size), 1)
    sub = lax.broadcasted_iota(jnp.int32, (PB, size), 0)
    lane32 = lax.broadcasted_iota(jnp.int32, (PB // 2, 128), 1)
    first = lane32 < PB
    for p in range(size // PB):
        r0 = PB * p
        c0 = 128 * (p // 2)
        odd = p % 2 == 1
        row = a[r0 : r0 + PB, :]
        tile = row[:, c0 : c0 + 128]
        turned = pltpu.roll(tile, PB, 1)
        one, two = (turned, tile) if odd else (tile, turned)
        packed[...] = jnp.where(first, one[: PB // 2], two[PB // 2 :])
        invert_pivot(packed)
        inverse = packed[...]
        moved = pltpu.roll(inverse, PB, 1)
        pivot = jnp.concatenate([jnp.where(first, inverse, 0.0), jnp.where(first, moved, 0.0)], axis=0)
        if odd:
            placed = jnp.concatenate([jnp.where(first, 0.0, moved), jnp.where(first, 0.0, inverse)], axis=0)
        else:
            placed = pivot
        pivot_ref[r0 : r0 + PB, :] = placed
        unit = jnp.where(lane == sub + r0, 1.0, 0.0)
        lower_ref[r0 : r0 + PB, :] = jnp.where(lane < r0, row, unit)
        if r0 + PB < size:
            inside = (lane >= r0) & (lane < r0 + PB)
            scaled = split_product(pivot[:, :PB], jnp.where(inside, unit, row))
            c1 = 128 * ((p + 1) // 2)
            below = jnp.where(lane >= r0 + PB, row, 0.0)[:, c1:]
            change = split_product(below, scaled)
            wide = lax.broadcasted_iota(jnp.int32, (size - c1, 128), 1)
            own = (wide >= r0 - c0) & (wide < r0 - c0 + PB)
            a[c1:, c0 : c0 + 128] = jnp.where(own, 0.0, a[c1:, c0 : c0 + 128])
            a[c1:, :] = a[c1:, :] - change


def damped(block, damping, profile):
    row = lax.broadcasted_iota(jnp.int32, (NB, NB), 0)
    col = lax.broadcasted_iota(jnp.int32, (NB, NB), 1)
    return block + jnp.where(row == col, damping * profile, 0.0)


def unpack(source, a, damping, profile, part=TRI, pitch=TRI):
    a[...] = jnp.zeros_like(a)
    for (i, j), slot in SLOT.items():
        block = jnp.concatenate(
            [source[start : start + take, :] for done, take, start in spans(slot, part, pitch)], axis=0
        )
        if i == j:
            block = damped(block, damping, profile[:, i * NB : (i + 1) * NB])
        a[i * NB : (i + 1) * NB, j * NB : (j + 1) * NB] = block


def read_damping(main_ref):
    scal = main_ref[SUM_AT : SUM_AT + 1, :]
    for part in range(1, 4):
        at = part * MAIN_PITCH + SUM_AT
        scal = scal + main_ref[at : at + 1, :]
    return scal[:, 0:1] / scal[:, 1:2]


def pivot_times(pivot_ref, row):
    return jnp.concatenate(
        [nn(row[:, i * NB : (i + 1) * NB], pivot_ref[i * NB : (i + 1) * NB, :], HIGHEST) for i in range(NBLK)],
        axis=1,
    )


def wide_row(ref, places):
    return jnp.concatenate([jnp.broadcast_to(ref[at : at + 1, :], (8, NB)) for at in places], axis=1)


def gradient_row(main_ref, half):
    lines = range(NBLK * half, NBLK * half + NBLK)
    return wide_row(main_ref, [line // 2 * MAIN_PITCH + MAIN_PART + line % 2 for line in lines])


def regional_kernel(main_ref, prior_ref, lower_ref, pivot_ref, a, packed):
    unpack(main_ref, a, read_damping(main_ref), prior_ref[0:1, : NBLK * NB], MAIN_PART, MAIN_PITCH)
    eliminate(a, packed, lower_ref, pivot_ref)


def coupling_kernel(main_ref, rg_ref, lower_ref, pivot_ref, out_ref, scaled_ref, q_ref, share_ref, b, u):
    width = NBLK * NB
    for c in range(NBLK):
        pitch = width + PART
        b[:, c * NB : (c + 1) * NB] = rg_ref[c * pitch : c * pitch + width, :]
        part = rg_ref[c * pitch + width : (c + 1) * pitch, :]
        share_ref[...] = part if c == 0 else share_ref[...] + part
    for i in range(NBLK):
        rows = slice(i * NB, (i + 1) * NB)
        value = nn(lower_ref[rows, : (i + 1) * NB], b[: (i + 1) * NB, :], HIGHEST)
        u[rows, :] = value
        scaled_ref[rows, :] = nn(pivot_ref[rows, :], value, HIGHEST)
    for i in range(NBLK):
        value = tn(u[:, i * NB : (i + 1) * NB], scaled_ref[:, i * NB :], HIGHEST)
        for j in range(i, NBLK):
            store_split(out_ref, SLOT[i, j], value[:, (j - i) * NB : (j - i + 1) * NB])
    q = pivot_times(pivot_ref, nt(gradient_row(main_ref, 0), lower_ref[...], HIGHEST))
    q_ref[...] = q
    v = gradient_row(main_ref, 1) - nn(q, u[...], HIGHEST)
    sub = lax.broadcasted_iota(jnp.int32, (8, NB), 0)
    tail = jnp.zeros((8, NB), f32)
    for c in range(NBLK):
        tail = jnp.where(sub == c, v[:, c * NB : (c + 1) * NB], tail)
    for part in range(REG_PARTS):
        out_ref[part * PART_ROWS + PART : (part + 1) * PART_ROWS, :] = tail


def finish_kernel(
    g_ref, v_ref, main_ref, prior_ref, flower_ref, scaled_ref, q_ref, red_ref, aux_ref,
    local_ref, regional_ref, global_ref,
    a, packed, lower, pivot,
):
    nparams = local_ref.shape[0]
    width = NBLK * NB
    unpack(g_ref, a, read_damping(main_ref), prior_ref[0:1, width:])
    eliminate(a, packed, lower, pivot)
    whole = lower[...]
    forward = pivot_times(pivot, nt(wide_row(v_ref, range(NBLK)), whole, HIGHEST))
    global_step = nn(forward, whole, HIGHEST)
    regional_step = nn(q_ref[...] - nt(global_step, scaled_ref[...], HIGHEST), flower_ref[...], HIGHEST)
    regional_ref[...] = regional_step[0:1, :]
    global_ref[...] = global_step[0:1, :]

    aux = aux_ref[...]
    at = 0
    factor = [[None] * nparams for i in range(nparams)]
    for i in range(nparams):
        for c in range(i + 1):
            factor[i][c] = aux[:, at : at + 1]
            at += 1
    update = jnp.concatenate([regional_step, global_step], axis=1)
    target = []
    for i in range(nparams):
        target.append(
            aux[:, at : at + 1] - jnp.sum(red_ref[8 * i : 8 * i + 8, :] * update, axis=1, keepdims=True)
        )
        at += 1
    found = backward_small(factor, target)
    sub = lax.broadcasted_iota(jnp.int32, (8, 8), 0)
    lane = lax.broadcasted_iota(jnp.int32, (8, 8), 1)
    for i in range(nparams):
        local_ref[i : i + 1, :] = jnp.sum(jnp.where(sub == lane, found[i], 0.0), axis=0, keepdims=True)


def shape(*dims, dtype=f32):
    return jax.ShapeDtypeStruct(dims, dtype)


VMEM = pl.BlockSpec(memory_space=pltpu.VMEM)
SMEM = pl.BlockSpec(memory_space=pltpu.SMEM)


def whole_block(dims):
    return pl.BlockSpec(dims, lambda i: (0,) * len(dims))


def call(kernel, out_shape, scratch, specs, flops, grid=(), limit=40):
    return pl.pallas_call(
        kernel,
        grid=grid,
        out_shape=out_shape,
        in_specs=specs,
        out_specs=[VMEM] * len(out_shape),
        scratch_shapes=scratch,
        name=kernel.__name__,
        compiler_params=pltpu.CompilerParams(vmem_limit_bytes=limit * 1024 * 1024),
        cost_estimate=pl.CostEstimate(flops=flops, bytes_accessed=4_000_000, transcendentals=0),
    )


def part_sums(value, axis, parts):
    moved = lax.all_to_all(value, axis, 0, 0, tiled=True)
    return jnp.sum(moved.reshape((parts, value.shape[0] // parts) + value.shape[1:]), axis=0)


def copies_back(piece, axis, parts):
    copies = jnp.broadcast_to(piece[None], (parts,) + piece.shape).reshape((-1,) + piece.shape[1:])
    return lax.all_to_all(copies, axis, 0, 0, tiled=True)


def body(
    local_jac,
    global_jac,
    coeff_index,
    coeff_weight,
    residual,
    obs_weight,
    obs_count,
    local_prior,
    regional_prior,
    global_prior,
):
    nx, nz = lax.axis_size("x"), lax.axis_size("z")
    rows = residual.shape[0]
    nparams = local_jac.shape[0]
    width = global_jac.shape[1]
    stack = 2 * rows + 6 * RPAD
    sums = call(
        misfit_kernel,
        [shape(8 * REG_PARTS, NB)],
        [],
        [whole_block((1, rows)), whole_block((1, rows)), SMEM],
        1_000_000,
        grid=(1,),
    )(residual[None], obs_weight[None], obs_count)[0]
    sums, obs_count = lax.optimization_barrier((sums, obs_count))
    sums = lax.all_to_all(sums, GROUPS, 0, 0, tiled=True)
    gg, main, rg, red, aux, prior = call(
        assemble_kernel,
        [
            shape(TRI, NB),
            shape(4 * MAIN_PITCH, NB),
            shape(NBLK * width, NB),
            shape(RPAD, 2 * width),
            shape(8, NB),
            shape(8, 2 * width),
        ],
        [
            pltpu.VMEM((stack, 2 * width), bf16),
            pltpu.VMEM((stack, 2 * width), bf16),
            pltpu.VMEM((NB, 512), f32),
        ],
        [
            whole_block(local_jac.shape), whole_block(global_jac.shape), whole_block(coeff_index.shape),
            whole_block(coeff_weight.shape), whole_block((1, rows)), whole_block((1, rows)), SMEM,
            whole_block(local_prior.shape), whole_block((1, width)), whole_block((1, width)),
        ],
        8_000_000_000,
        grid=(1,),
        limit=60,
    )(
        local_jac, global_jac, coeff_index, coeff_weight, residual[None], obs_weight[None],
        obs_count, local_prior, regional_prior, global_prior[None],
    )
    sums, gg, main, rg = lax.optimization_barrier((sums, gg, main, rg))
    rg = lax.psum_scatter(rg, "x", scatter_dimension=0, tiled=True)
    share = lax.psum_scatter(gg, GROUPS, scatter_dimension=0, tiled=True)
    main = part_sums(main, "x", nx)
    sums = jnp.sum(sums.reshape(REG_PARTS, 8, NB), axis=0)
    main = main + jnp.pad(sums, ((SUM_AT, MAIN_PITCH - SUM_AT - 8), (0, 0)))
    main = copies_back(part_sums(main, "z", nz), "z", nz)
    rest = jnp.concatenate([rg, share], axis=0)
    main, rest = lax.optimization_barrier((main, rest))
    rest = part_sums(rest, "z", nz)
    main = lax.all_gather(main, "x", axis=0, tiled=True)
    main, rest = lax.optimization_barrier((main, rest))
    rest = copies_back(rest, "z", nz)
    lower, pivot = call(
        regional_kernel,
        [shape(width, width), shape(width, NB)],
        [pltpu.VMEM((width, width), f32), pltpu.VMEM((PB // 2, 128), f32)],
        [VMEM] * 2,
        20_000_000_000,
    )(main, prior)
    rg = copies_back(rest, "x", nx)
    outer, scaled, q, share = call(
        coupling_kernel,
        [shape(REG_PARTS * PART_ROWS, NB), shape(width, width), shape(8, width), shape(PART, NB)],
        [pltpu.VMEM((width, width), f32), pltpu.VMEM((width, width), f32)],
        [VMEM] * 4,
        4_000_000_000,
    )(main, rg, lower, pivot)
    outer = part_sums(outer, GROUPS, REG_PARTS)
    mine = share - outer[:PART]
    matrix = lax.all_gather(mine, GROUPS, axis=0, tiled=True)
    local_step, regional_step, global_step = call(
        finish_kernel,
        [shape(nparams, 8), shape(1, width), shape(1, width)],
        [
            pltpu.VMEM((width, width), f32),
            pltpu.VMEM((PB // 2, 128), f32),
            pltpu.VMEM((width, width), f32),
            pltpu.VMEM((width, NB), f32),
        ],
        [VMEM] * 9,
        20_000_000_000,
    )(matrix, outer[PART:], main, prior, lower, scaled, q, red, aux)
    return local_step, regional_step, global_step[0]


def solution(mesh):
    devices = mesh.devices.reshape(4, 2, 4, 16)
    split = Mesh(devices, ("y", "core", "x", "z"))
    both = GROUPS + LAYERS
    return jax.shard_map(
        body,
        mesh=split,
        in_specs=(
            P(None, both),
            P(both, None),
            P(None, both),
            P(None, both),
            P(both),
            P(both),
            P(both),
            P(None, both),
            P(GROUPS, None),
            P(),
        ),
        out_specs=(P(None, both), P(GROUPS, None), P()),
        check_vma=False,
    )
```

```python
import jax
import jax.numpy as jnp
from jax import lax
from jax.experimental import pallas as pl
from jax.experimental.pallas import tpu as pltpu
from jax.sharding import Mesh, PartitionSpec as P

f32 = jnp.float32
bf16 = jnp.bfloat16
HIGHEST = lax.Precision.HIGHEST

NB = 128
NBLK = 4
PB = 64
PAIRS = [(i, j) for i in range(NBLK) for j in range(i, NBLK)]
SLOT = {pair: at for at, pair in enumerate(PAIRS)}
TRI = len(PAIRS) * NB
REG_PARTS = 8
PART = TRI // REG_PARTS
PART_ROWS = PART + 8
MAIN_ROWS = 1536
SUM_AT = TRI + 8
CHUNK = 48
RPAD = 64

LAYERS = ("x", "z")
GROUPS = ("y", "core")


def tn(a, b, precision=None):
    return lax.dot_general(
        a, b, (((0,), (0,)), ((), ())), precision=precision, preferred_element_type=f32
    )


def nt(a, b, precision=None):
    return lax.dot_general(
        a, b, (((1,), (1,)), ((), ())), precision=precision, preferred_element_type=f32
    )


def nn(a, b, precision=None):
    return jnp.dot(a, b, precision=precision, preferred_element_type=f32)


def pieces(value):
    first = value.astype(bf16)
    rest = value - first.astype(f32)
    second = rest.astype(bf16)
    third = (rest - second.astype(f32)).astype(bf16)
    return first, second, third


def cholesky_small(entries):
    order = len(entries)
    factor = [[None] * order for i in range(order)]
    for j in range(order):
        diagonal = entries[j][j]
        for k in range(j):
            diagonal = diagonal - factor[j][k] * factor[j][k]
        factor[j][j] = jnp.sqrt(diagonal)
        for i in range(j + 1, order):
            current = entries[i][j]
            for k in range(j):
                current = current - factor[i][k] * factor[j][k]
            factor[i][j] = current / factor[j][j]
    return factor


def forward_small(factor, target):
    result = []
    for a in range(len(target)):
        current = target[a]
        for k in range(a):
            current = current - factor[a][k] * result[k]
        result.append(current / factor[a][a])
    return result


def backward_small(factor, target):
    order = len(target)
    result = [None] * order
    for a in reversed(range(order)):
        current = target[a]
        for k in range(a + 1, order):
            current = current - factor[k][a] * result[k]
        result[a] = current / factor[a][a]
    return result


def store_split(ref, slot, block):
    done = 0
    while done < NB:
        flat = slot * NB + done
        part, off = flat // PART, flat % PART
        take = min(NB - done, PART - off)
        start = part * PART_ROWS + off
        ref[start : start + take, :] = block[done : done + take]
        done += take


def assemble_kernel(
    lj_ref, gj_ref, ci_ref, cw_ref, res_ref, ow_ref, cnt_ref, lp_ref, rp_ref, gp_ref,
    gg_ref, main_ref, rg_ref, red_ref, aux_ref, prior_ref,
    left, right, padded,
):
    rows = gj_ref.shape[0]
    nparams = lj_ref.shape[0]
    objects = 8
    observed = rows // objects
    width = gj_ref.shape[1]
    res = res_ref[...]
    prior_ref[:, :width] = jnp.broadcast_to(rp_ref[...], (8, width))
    prior_ref[:, width:] = jnp.broadcast_to(gp_ref[...], (8, width))
    position = lax.broadcasted_iota(jnp.int32, (objects, rows), 1)
    owner = lax.broadcasted_iota(jnp.int32, (objects, rows), 0)
    count = jnp.zeros((objects, rows), jnp.int32)
    for n in range(objects):
        count = jnp.where(owner == n, cnt_ref[n], count)
    local = position - owner * observed
    present = (local >= 0) & (local < observed) & (local < count)
    live = jnp.where(present, jnp.broadcast_to(ow_ref[...], (objects, rows)), 0.0)
    weight = jnp.sum(live, axis=0, keepdims=True)
    misfit = jnp.sum(weight * res * res, axis=1, keepdims=True)
    counted = jnp.sum(
        jnp.sum(jnp.where(present, 1.0, 0.0), axis=0, keepdims=True), axis=1, keepdims=True
    )

    padded[...] = jnp.zeros_like(padded)
    padded[0:1, :rows] = weight
    padded[1:5, :rows] = ci_ref[...].astype(f32)
    padded[5:9, :rows] = cw_ref[...].astype(f32)
    for block in range(padded.shape[1] // NB):
        columns = padded[:, block * NB : (block + 1) * NB].T
        low = block * NB
        while low < min((block + 1) * NB, rows):
            high = min(low + 32, rows)
            here = columns[low - block * NB : high - block * NB]
            weights = here[:, 0:1]
            lanes = lax.broadcasted_iota(jnp.int32, (high - low, width), 1).astype(f32)
            total = jnp.zeros((high - low, width), f32)
            for k in range(4):
                total = total + jnp.where(here[:, 1 + k : 2 + k] == lanes, here[:, 5 + k : 6 + k], 0.0)
            joined = total.astype(bf16)
            for at, value in ((0, joined), (width, gj_ref[low:high, :])):
                scaled = (value.astype(f32) * weights).astype(bf16)
                right[low:high, at : at + width] = value
                right[rows + low : rows + high, at : at + width] = scaled
                left[low:high, at : at + width] = (scaled.astype(f32) * 0.5).astype(bf16)
                left[rows + low : rows + high, at : at + width] = (value.astype(f32) * 0.5).astype(bf16)
            low = high

    jac = lj_ref[...].astype(f32)
    weighted = [jac[a : a + 1, :] * live for a in range(nparams)]
    entries = [[None] * nparams for a in range(nparams)]
    owner8 = lax.broadcasted_iota(jnp.int32, (objects, objects), 0)
    lane8 = lax.broadcasted_iota(jnp.int32, (objects, objects), 1)
    for a in range(nparams):
        for b in range(a + 1):
            value = jnp.sum(weighted[a] * jac[b : b + 1, :], axis=1, keepdims=True)
            if a == b:
                prior = jnp.broadcast_to(lp_ref[a : a + 1, :], (objects, objects))
                value = value + jnp.sum(jnp.where(owner8 == lane8, prior, 0.0), axis=1, keepdims=True)
            entries[a][b] = value
    factor = cholesky_small(entries)
    local_gradient = [jnp.sum(weighted[a] * res, axis=1, keepdims=True) for a in range(nparams)]
    reduced_gradient = forward_small(factor, local_gradient)

    blank = jnp.zeros((8, rows), f32)
    stacked = jnp.concatenate(weighted + [blank], axis=0)
    everything = right[0:rows, :]
    coupling = None
    for piece in pieces(stacked):
        term = nn(piece, everything)
        coupling = term if coupling is None else coupling + term
    reduced = forward_small(factor, [coupling[8 * a : 8 * a + 8] for a in range(nparams)])
    joint = jnp.concatenate(reduced + [jnp.zeros((8, 2 * width), f32)], axis=0)
    red_ref[...] = joint
    r0, r1, r2 = pieces(joint)
    base = 2 * rows
    for at, (one, two) in enumerate(((r0, r0), (r0, r1), (r1, r0), (r1, r1), (r0, r2), (r2, r0))):
        left[base + at * RPAD : base + (at + 1) * RPAD, :] = -one
        right[base + at * RPAD : base + (at + 1) * RPAD, :] = two

    lane = lax.broadcasted_iota(jnp.int32, (objects, NB), 1)
    aux = jnp.zeros((objects, NB), f32)
    at = 0
    for a in range(nparams):
        for b in range(a + 1):
            aux = jnp.where(lane == at, factor[a][b], aux)
            at += 1
    for a in range(nparams):
        aux = jnp.where(lane == at, reduced_gradient[a], aux)
        at += 1
    aux_ref[...] = aux

    first, second, third = pieces(res)
    lhs = jnp.concatenate(
        [first.astype(f32), second.astype(f32), third.astype(f32), jnp.zeros((13, rows), f32)], axis=0
    ).astype(bf16)
    gradient = jnp.sum(nn(lhs, right[rows : 2 * rows, :]), axis=0, keepdims=True)
    for a in range(nparams):
        gradient = gradient - jnp.sum(reduced_gradient[a] * reduced[a], axis=0, keepdims=True)
    for at in range(8):
        main_ref[TRI + at : TRI + at + 1, :] = gradient[:, at * NB : (at + 1) * NB]

    row_lane = lax.broadcasted_iota(jnp.int32, (8, NB), 1)
    scalars = jnp.where(row_lane == 0, misfit, jnp.where(row_lane == 1, counted, 0.0))
    for part in range(REG_PARTS):
        gg_ref[part * PART_ROWS + PART : (part + 1) * PART_ROWS, :] = scalars
    for i in range(NBLK):
        for half in range(2):
            at = half * width
            value = tn(left[:, at + i * NB : at + (i + 1) * NB], right[:, at + i * NB : at + width])
            for j in range(i, NBLK):
                block = value[:, (j - i) * NB : (j - i + 1) * NB]
                slot = SLOT[i, j]
                if half == 0:
                    main_ref[slot * NB : (slot + 1) * NB, :] = block
                else:
                    store_split(gg_ref, slot, block)
        value = 2.0 * tn(left[0:rows, i * NB : (i + 1) * NB], right[0:rows, width:]) + tn(
            left[base:, i * NB : (i + 1) * NB], right[base:, width:]
        )
        for c in range(NBLK):
            rg_ref[c * width + i * NB : c * width + (i + 1) * NB, :] = value[:, c * NB : (c + 1) * NB]


def spread(value, at):
    return jnp.broadcast_to(value[at : at + 1], (8, 128))


def invert_pivot(ref):
    lane = lax.broadcasted_iota(jnp.int32, (8, 128), 1)
    sub = lax.broadcasted_iota(jnp.int32, (8, 128), 0)
    col = lane & (PB - 1)
    half = lane - col
    tiles = PB // 16

    def pick(value, index):
        return jnp.take_along_axis(value, index, axis=1)

    def group(g, carry):
        at = pl.multiple_of(8 * lax.rem(g, tiles), 8)
        side = lax.div(g, tiles) * PB
        base = 8 * g
        source = ref[pl.ds(at, 8), :]
        panel = pick(source, col + side)
        columns = [pick(source, jnp.full((8, 128), side + base + j, jnp.int32)) for j in range(8)]
        for k in range(0, 8, 2):
            c0, c1 = columns[k], columns[k + 1]
            a, b, c = spread(c0, k), spread(c1, k), spread(c1, k + 1)
            q = 1.0 / (a * c - b * b)
            pa, pb, pc = c * q, b * q, a * q
            s0, s1 = sub == k, sub == k + 1
            m0, m1 = col == base + k, col == base + k + 1
            r0 = jnp.where(m0, 1.0, jnp.where(m1, 0.0, spread(panel, k)))
            r1 = jnp.where(m1, 1.0, jnp.where(m0, 0.0, spread(panel, k + 1)))
            n0 = pa * r0 - pb * r1
            n1 = pc * r1 - pb * r0
            rest = jnp.where(m0 | m1, 0.0, panel) - c0 * n0 - c1 * n1
            panel = jnp.where(s0, n0, jnp.where(s1, n1, rest))
            for j in range(k + 2, 8):
                r0, r1 = spread(columns[j], k), spread(columns[j], k + 1)
                n0 = pa * r0 - pb * r1
                n1 = pc * r1 - pb * r0
                columns[j] = jnp.where(s0, n0, jnp.where(s1, n1, columns[j] - c0 * n0 - c1 * n1))
        rows = [spread(panel, i) for i in range(8)]
        inside = (col >= base) & (col < base + 8)
        for t in range(tiles):
            tile = ref[8 * t : 8 * t + 8, :]
            terms = [pick(tile, half + (base + i)) * rows[i] for i in range(8)]
            kept = jnp.where(inside, 0.0, tile) - terms[0]
            ref[8 * t : 8 * t + 8, :] = (kept - terms[1] - (terms[2] + terms[3])) - (
                (terms[4] + terms[5]) + (terms[6] + terms[7])
            )
        here = ref[pl.ds(at, 8), :]
        ref[pl.ds(at, 8), :] = jnp.where(half == side, panel, here)
        return carry

    lax.fori_loop(0, PB // 8, group, 0)


def split_product(a, b):
    a0, a1, a2 = pieces(a)
    b0, b1, b2 = pieces(b)
    left = jnp.concatenate([a0, a0, a1, a1, a0, a2], axis=0)
    right = jnp.concatenate([b0, b1, b0, b1, b2, b0], axis=0)
    return tn(left, right)


def eliminate(a, packed, lower_ref, pivot_ref):
    size = NBLK * NB
    lane = lax.broadcasted_iota(jnp.int32, (PB, size), 1)
    sub = lax.broadcasted_iota(jnp.int32, (PB, size), 0)
    lane32 = lax.broadcasted_iota(jnp.int32, (PB // 2, 128), 1)
    first = lane32 < PB
    for p in range(size // PB):
        r0 = PB * p
        c0 = 128 * (p // 2)
        odd = p % 2 == 1
        row = a[r0 : r0 + PB, :]
        tile = row[:, c0 : c0 + 128]
        turned = pltpu.roll(tile, PB, 1)
        one, two = (turned, tile) if odd else (tile, turned)
        packed[...] = jnp.where(first, one[: PB // 2], two[PB // 2 :])
        invert_pivot(packed)
        inverse = packed[...]
        moved = pltpu.roll(inverse, PB, 1)
        pivot = jnp.concatenate([jnp.where(first, inverse, 0.0), jnp.where(first, moved, 0.0)], axis=0)
        if odd:
            placed = jnp.concatenate([jnp.where(first, 0.0, moved), jnp.where(first, 0.0, inverse)], axis=0)
        else:
            placed = pivot
        pivot_ref[r0 : r0 + PB, :] = placed
        unit = jnp.where(lane == sub + r0, 1.0, 0.0)
        lower_ref[r0 : r0 + PB, :] = jnp.where(lane < r0, row, unit)
        if r0 + PB < size:
            inside = (lane >= r0) & (lane < r0 + PB)
            scaled = split_product(pivot[:, :PB], jnp.where(inside, unit, row))
            c1 = 128 * ((p + 1) // 2)
            below = jnp.where(lane >= r0 + PB, row, 0.0)[:, c1:]
            change = split_product(below, scaled)
            wide = lax.broadcasted_iota(jnp.int32, (size - c1, 128), 1)
            own = (wide >= r0 - c0) & (wide < r0 - c0 + PB)
            a[c1:, c0 : c0 + 128] = jnp.where(own, 0.0, a[c1:, c0 : c0 + 128])
            a[c1:, :] = a[c1:, :] - change


def damped(block, damping, profile):
    row = lax.broadcasted_iota(jnp.int32, (NB, NB), 0)
    col = lax.broadcasted_iota(jnp.int32, (NB, NB), 1)
    return block + jnp.where(row == col, damping * profile, 0.0)


def unpack(source, a, damping, profile):
    a[...] = jnp.zeros_like(a)
    for (i, j), slot in SLOT.items():
        block = source[slot * NB : (slot + 1) * NB, :]
        if i == j:
            block = damped(block, damping, profile[:, i * NB : (i + 1) * NB])
        a[i * NB : (i + 1) * NB, j * NB : (j + 1) * NB] = block


def read_damping(main_ref):
    scal = main_ref[SUM_AT + PART : SUM_AT + PART + 8, :]
    return scal[0:1, 0:1] / scal[0:1, 1:2]


def by_row(matrix, row):
    return jnp.sum(matrix * row, axis=1, keepdims=True)


def by_column(matrix, column):
    return jnp.sum(matrix * column, axis=0, keepdims=True)


def turn(row):
    return jnp.broadcast_to(row, (8, NB)).T


def wide_row(ref, at):
    return jnp.concatenate([ref[at + c : at + c + 1, :] for c in range(NBLK)], axis=1)


def regional_kernel(main_ref, prior_ref, lower_ref, pivot_ref, a, packed):
    unpack(main_ref, a, read_damping(main_ref), prior_ref[0:1, : NBLK * NB])
    eliminate(a, packed, lower_ref, pivot_ref)


def coupling_kernel(main_ref, rg_ref, lower_ref, pivot_ref, out_ref, scaled_ref, q_ref, b, u, w):
    width = NBLK * NB
    for c in range(NBLK):
        b[:, c * NB : (c + 1) * NB] = rg_ref[c * width : (c + 1) * width, :]
    b[:, width:] = jnp.zeros((width, NB), f32)
    for i in range(NBLK):
        b[i * NB : (i + 1) * NB, width : width + 8] = turn(main_ref[TRI + i : TRI + i + 1, :])
    for i in range(NBLK):
        rows = slice(i * NB, (i + 1) * NB)
        value = nn(lower_ref[rows, : (i + 1) * NB], b[: (i + 1) * NB, :], HIGHEST)
        u[rows, :] = value[:, :width]
        w[rows, :] = nn(pivot_ref[rows, :], value, HIGHEST)
    scaled_ref[...] = w[:, :width]
    q_ref[...] = w[:, width:]
    sub = lax.broadcasted_iota(jnp.int32, (8, NB), 0)
    tail = jnp.zeros((8, NB), f32)
    for i in range(NBLK):
        value = tn(u[:, i * NB : (i + 1) * NB], w[:, i * NB :], HIGHEST)
        for j in range(i, NBLK):
            store_split(out_ref, SLOT[i, j], value[:, (j - i) * NB : (j - i + 1) * NB])
        line = TRI + NBLK + i
        rest = jnp.broadcast_to(main_ref[line : line + 1, :], (8, NB)) - value[:, width - i * NB :].T[:8]
        tail = jnp.where(sub == i, jnp.broadcast_to(rest[0:1], (8, NB)), tail)
    for part in range(REG_PARTS):
        out_ref[part * PART_ROWS + PART : (part + 1) * PART_ROWS, :] = tail


def finish_kernel(
    g_ref, v_ref, main_ref, prior_ref, flower_ref, scaled_ref, q_ref, red_ref, aux_ref,
    local_ref, regional_ref, global_ref,
    a, packed, lower, pivot,
):
    nparams = local_ref.shape[0]
    width = NBLK * NB
    unpack(g_ref, a, read_damping(main_ref), prior_ref[0:1, width:])
    eliminate(a, packed, lower, pivot)
    whole = lower[...]
    forward = by_row(whole, wide_row(v_ref, 0))
    forward = jnp.concatenate(
        [
            turn(by_column(pivot[i * NB : (i + 1) * NB, :], forward[i * NB : (i + 1) * NB]))[:, 0:1]
            for i in range(NBLK)
        ],
        axis=0,
    )
    global_step = by_column(whole, forward)
    rest = q_ref[:, 0:1] - by_row(scaled_ref[...], global_step)
    regional_step = by_column(flower_ref[...], rest)
    regional_ref[...] = regional_step
    global_ref[...] = global_step

    aux = aux_ref[...]
    at = 0
    factor = [[None] * nparams for i in range(nparams)]
    for i in range(nparams):
        for c in range(i + 1):
            factor[i][c] = aux[:, at : at + 1]
            at += 1
    update = jnp.concatenate([regional_step, global_step], axis=1)
    target = []
    for i in range(nparams):
        target.append(
            aux[:, at : at + 1] - jnp.sum(red_ref[8 * i : 8 * i + 8, :] * update, axis=1, keepdims=True)
        )
        at += 1
    found = backward_small(factor, target)
    sub = lax.broadcasted_iota(jnp.int32, (8, 8), 0)
    lane = lax.broadcasted_iota(jnp.int32, (8, 8), 1)
    for i in range(nparams):
        local_ref[i : i + 1, :] = jnp.sum(jnp.where(sub == lane, found[i], 0.0), axis=0, keepdims=True)


def shape(*dims, dtype=f32):
    return jax.ShapeDtypeStruct(dims, dtype)


VMEM = pl.BlockSpec(memory_space=pltpu.VMEM)
SMEM = pl.BlockSpec(memory_space=pltpu.SMEM)


def whole_block(dims):
    return pl.BlockSpec(dims, lambda i: (0,) * len(dims))


def call(kernel, out_shape, scratch, specs, flops, grid=(), limit=16):
    return pl.pallas_call(
        kernel,
        grid=grid,
        out_shape=out_shape,
        in_specs=specs,
        out_specs=[VMEM] * len(out_shape),
        scratch_shapes=scratch,
        name=kernel.__name__,
        compiler_params=pltpu.CompilerParams(vmem_limit_bytes=limit * 1024 * 1024),
        cost_estimate=pl.CostEstimate(flops=flops, bytes_accessed=4_000_000, transcendentals=0),
    )


def part_sums(value, axis, parts):
    moved = lax.all_to_all(value, axis, 0, 0, tiled=True)
    return jnp.sum(moved.reshape((parts, value.shape[0] // parts) + value.shape[1:]), axis=0)


def copies_back(piece, axis, parts):
    copies = jnp.broadcast_to(piece[None], (parts,) + piece.shape).reshape((-1,) + piece.shape[1:])
    return lax.all_to_all(copies, axis, 0, 0, tiled=True)


def body(
    local_jac,
    global_jac,
    coeff_index,
    coeff_weight,
    residual,
    obs_weight,
    obs_count,
    local_prior,
    regional_prior,
    global_prior,
):
    nx, nz = lax.axis_size("x"), lax.axis_size("z")
    rows = residual.shape[0]
    nparams = local_jac.shape[0]
    width = global_jac.shape[1]
    stack = 2 * rows + 6 * RPAD
    gg, main, rg, red, aux, prior = call(
        assemble_kernel,
        [
            shape(REG_PARTS * PART_ROWS, NB),
            shape(SUM_AT, NB),
            shape(NBLK * width, NB),
            shape(RPAD, 2 * width),
            shape(8, NB),
            shape(8, 2 * width),
        ],
        [
            pltpu.VMEM((stack, 2 * width), bf16),
            pltpu.VMEM((stack, 2 * width), bf16),
            pltpu.VMEM((NB, 512), f32),
        ],
        [
            whole_block(local_jac.shape), whole_block(global_jac.shape), whole_block(coeff_index.shape),
            whole_block(coeff_weight.shape), whole_block((1, rows)), whole_block((1, rows)), SMEM,
            whole_block(local_prior.shape), whole_block((1, width)), whole_block((1, width)),
        ],
        2_000_000_000,
        grid=(1,),
        limit=60,
    )(
        local_jac, global_jac, coeff_index, coeff_weight, residual[None], obs_weight[None],
        obs_count, local_prior, regional_prior, global_prior[None],
    )
    share = part_sums(gg, GROUPS, REG_PARTS)
    rg = lax.psum_scatter(rg, "x", scatter_dimension=0, tiled=True)
    main = jnp.concatenate([main, share, jnp.zeros((MAIN_ROWS - SUM_AT - PART_ROWS, NB), f32)], axis=0)
    main = part_sums(main, "x", nx)
    both = part_sums(jnp.concatenate([main, rg], axis=0), "z", nz)
    both = copies_back(both, "z", nz)
    main = lax.all_gather(both[: MAIN_ROWS // nx], "x", axis=0, tiled=True)
    main, rg = lax.optimization_barrier((main, both[MAIN_ROWS // nx :]))
    rg = copies_back(rg, "x", nx)
    lower, pivot = call(
        regional_kernel,
        [shape(width, width), shape(width, NB)],
        [pltpu.VMEM((width, width), f32), pltpu.VMEM((PB // 2, 128), f32)],
        [VMEM] * 2,
        20_000_000_000,
    )(main, prior)
    outer, scaled, q = call(
        coupling_kernel,
        [shape(REG_PARTS * PART_ROWS, NB), shape(width, width), shape(width, NB)],
        [
            pltpu.VMEM((width, width + NB), f32),
            pltpu.VMEM((width, width), f32),
            pltpu.VMEM((width, width + NB), f32),
        ],
        [VMEM] * 4,
        4_000_000_000,
    )(main, rg, lower, pivot)
    outer = part_sums(outer, GROUPS, REG_PARTS)
    mine = main[SUM_AT : SUM_AT + PART] - outer[:PART]
    matrix = lax.all_gather(mine, GROUPS, axis=0, tiled=True)
    local_step, regional_step, global_step = call(
        finish_kernel,
        [shape(nparams, 8), shape(1, width), shape(1, width)],
        [
            pltpu.VMEM((width, width), f32),
            pltpu.VMEM((PB // 2, 128), f32),
            pltpu.VMEM((width, width), f32),
            pltpu.VMEM((width, NB), f32),
        ],
        [VMEM] * 9,
        20_000_000_000,
    )(matrix, outer[PART:], main, prior, lower, scaled, q, red, aux)
    return local_step, regional_step, global_step[0]


def solution(mesh):
    devices = mesh.devices.reshape(4, 2, 4, 16)
    split = Mesh(devices, ("y", "core", "x", "z"))
    both = GROUPS + LAYERS
    return jax.shard_map(
        body,
        mesh=split,
        in_specs=(
            P(None, both),
            P(both, None),
            P(None, both),
            P(None, both),
            P(both),
            P(both),
            P(both),
            P(None, both),
            P(GROUPS, None),
            P(),
        ),
        out_specs=(P(None, both), P(GROUPS, None), P()),
        check_vma=False,
    )
```

```python
import jax
import jax.numpy as jnp
from jax import lax
from jax.experimental import pallas as pl
from jax.experimental.pallas import tpu as pltpu
from jax.sharding import Mesh, PartitionSpec as P

f32 = jnp.float32
bf16 = jnp.bfloat16
HIGHEST = lax.Precision.HIGHEST

NB = 128
NBLK = 4
PB = 64
PAIRS = [(i, j) for i in range(NBLK) for j in range(i, NBLK)]
SLOT = {pair: at for at, pair in enumerate(PAIRS)}
TRI = len(PAIRS) * NB
REG_PARTS = 8
PART = TRI // REG_PARTS
PART_ROWS = PART + 8
MAIN_ROWS = 1536
SUM_AT = TRI + 8
CHUNK = 48
RPAD = 64

LAYERS = ("x", "z")
GROUPS = ("y", "core")


def tn(a, b, precision=None):
    return lax.dot_general(
        a, b, (((0,), (0,)), ((), ())), precision=precision, preferred_element_type=f32
    )


def nt(a, b, precision=None):
    return lax.dot_general(
        a, b, (((1,), (1,)), ((), ())), precision=precision, preferred_element_type=f32
    )


def nn(a, b, precision=None):
    return jnp.dot(a, b, precision=precision, preferred_element_type=f32)


def pieces(value):
    first = value.astype(bf16)
    rest = value - first.astype(f32)
    second = rest.astype(bf16)
    third = (rest - second.astype(f32)).astype(bf16)
    return first, second, third


def cholesky_small(entries):
    order = len(entries)
    factor = [[None] * order for i in range(order)]
    for j in range(order):
        diagonal = entries[j][j]
        for k in range(j):
            diagonal = diagonal - factor[j][k] * factor[j][k]
        factor[j][j] = jnp.sqrt(diagonal)
        for i in range(j + 1, order):
            current = entries[i][j]
            for k in range(j):
                current = current - factor[i][k] * factor[j][k]
            factor[i][j] = current / factor[j][j]
    return factor


def forward_small(factor, target):
    result = []
    for a in range(len(target)):
        current = target[a]
        for k in range(a):
            current = current - factor[a][k] * result[k]
        result.append(current / factor[a][a])
    return result


def backward_small(factor, target):
    order = len(target)
    result = [None] * order
    for a in reversed(range(order)):
        current = target[a]
        for k in range(a + 1, order):
            current = current - factor[k][a] * result[k]
        result[a] = current / factor[a][a]
    return result


def store_split(ref, slot, block):
    done = 0
    while done < NB:
        flat = slot * NB + done
        part, off = flat // PART, flat % PART
        take = min(NB - done, PART - off)
        start = part * PART_ROWS + off
        ref[start : start + take, :] = block[done : done + take]
        done += take


def assemble_kernel(
    lj_ref, gj_ref, ci_ref, cw_ref, res_ref, ow_ref, cnt_ref, lp_ref, rp_ref, gp_ref,
    gg_ref, main_ref, rg_ref, red_ref, aux_ref, prior_ref,
    left, right, padded,
):
    rows = gj_ref.shape[0]
    nparams = lj_ref.shape[0]
    objects = 8
    observed = rows // objects
    width = gj_ref.shape[1]
    res = res_ref[...]
    prior_ref[:, :width] = jnp.broadcast_to(rp_ref[...], (8, width))
    prior_ref[:, width:] = jnp.broadcast_to(gp_ref[...], (8, width))
    position = lax.broadcasted_iota(jnp.int32, (objects, rows), 1)
    owner = lax.broadcasted_iota(jnp.int32, (objects, rows), 0)
    count = jnp.zeros((objects, rows), jnp.int32)
    for n in range(objects):
        count = jnp.where(owner == n, cnt_ref[n], count)
    local = position - owner * observed
    present = (local >= 0) & (local < observed) & (local < count)
    live = jnp.where(present, jnp.broadcast_to(ow_ref[...], (objects, rows)), 0.0)
    weight = jnp.sum(live, axis=0, keepdims=True)
    misfit = jnp.sum(weight * res * res, axis=1, keepdims=True)
    counted = jnp.sum(
        jnp.sum(jnp.where(present, 1.0, 0.0), axis=0, keepdims=True), axis=1, keepdims=True
    )

    padded[...] = jnp.zeros_like(padded)
    padded[0:1, :rows] = weight
    padded[1:5, :rows] = ci_ref[...].astype(f32)
    padded[5:9, :rows] = cw_ref[...].astype(f32)
    for block in range(padded.shape[1] // NB):
        columns = padded[:, block * NB : (block + 1) * NB].T
        low = block * NB
        while low < min((block + 1) * NB, rows):
            high = min(low + 32, rows)
            here = columns[low - block * NB : high - block * NB]
            weights = here[:, 0:1]
            lanes = lax.broadcasted_iota(jnp.int32, (high - low, width), 1).astype(f32)
            total = jnp.zeros((high - low, width), f32)
            for k in range(4):
                total = total + jnp.where(here[:, 1 + k : 2 + k] == lanes, here[:, 5 + k : 6 + k], 0.0)
            joined = total.astype(bf16)
            for at, value in ((0, joined), (width, gj_ref[low:high, :])):
                scaled = (value.astype(f32) * weights).astype(bf16)
                right[low:high, at : at + width] = value
                right[rows + low : rows + high, at : at + width] = scaled
                left[low:high, at : at + width] = (scaled.astype(f32) * 0.5).astype(bf16)
                left[rows + low : rows + high, at : at + width] = (value.astype(f32) * 0.5).astype(bf16)
            low = high

    jac = lj_ref[...].astype(f32)
    weighted = [jac[a : a + 1, :] * live for a in range(nparams)]
    entries = [[None] * nparams for a in range(nparams)]
    owner8 = lax.broadcasted_iota(jnp.int32, (objects, objects), 0)
    lane8 = lax.broadcasted_iota(jnp.int32, (objects, objects), 1)
    for a in range(nparams):
        for b in range(a + 1):
            value = jnp.sum(weighted[a] * jac[b : b + 1, :], axis=1, keepdims=True)
            if a == b:
                prior = jnp.broadcast_to(lp_ref[a : a + 1, :], (objects, objects))
                value = value + jnp.sum(jnp.where(owner8 == lane8, prior, 0.0), axis=1, keepdims=True)
            entries[a][b] = value
    factor = cholesky_small(entries)
    local_gradient = [jnp.sum(weighted[a] * res, axis=1, keepdims=True) for a in range(nparams)]
    reduced_gradient = forward_small(factor, local_gradient)

    blank = jnp.zeros((8, rows), f32)
    stacked = jnp.concatenate(weighted + [blank], axis=0)
    everything = right[0:rows, :]
    coupling = None
    for piece in pieces(stacked):
        term = nn(piece, everything)
        coupling = term if coupling is None else coupling + term
    reduced = forward_small(factor, [coupling[8 * a : 8 * a + 8] for a in range(nparams)])
    joint = jnp.concatenate(reduced + [jnp.zeros((8, 2 * width), f32)], axis=0)
    red_ref[...] = joint
    r0, r1, r2 = pieces(joint)
    base = 2 * rows
    for at, (one, two) in enumerate(((r0, r0), (r0, r1), (r1, r0), (r1, r1), (r0, r2), (r2, r0))):
        left[base + at * RPAD : base + (at + 1) * RPAD, :] = -one
        right[base + at * RPAD : base + (at + 1) * RPAD, :] = two

    lane = lax.broadcasted_iota(jnp.int32, (objects, NB), 1)
    aux = jnp.zeros((objects, NB), f32)
    at = 0
    for a in range(nparams):
        for b in range(a + 1):
            aux = jnp.where(lane == at, factor[a][b], aux)
            at += 1
    for a in range(nparams):
        aux = jnp.where(lane == at, reduced_gradient[a], aux)
        at += 1
    aux_ref[...] = aux

    first, second, third = pieces(res)
    lhs = jnp.concatenate(
        [first.astype(f32), second.astype(f32), third.astype(f32), jnp.zeros((13, rows), f32)], axis=0
    ).astype(bf16)
    gradient = jnp.sum(nn(lhs, right[rows : 2 * rows, :]), axis=0, keepdims=True)
    for a in range(nparams):
        gradient = gradient - jnp.sum(reduced_gradient[a] * reduced[a], axis=0, keepdims=True)
    for at in range(8):
        main_ref[TRI + at : TRI + at + 1, :] = gradient[:, at * NB : (at + 1) * NB]

    row_lane = lax.broadcasted_iota(jnp.int32, (8, NB), 1)
    scalars = jnp.where(row_lane == 0, misfit, jnp.where(row_lane == 1, counted, 0.0))
    for part in range(REG_PARTS):
        gg_ref[part * PART_ROWS + PART : (part + 1) * PART_ROWS, :] = scalars
    for i in range(NBLK):
        for half in range(2):
            at = half * width
            value = tn(left[:, at + i * NB : at + (i + 1) * NB], right[:, at + i * NB : at + width])
            for j in range(i, NBLK):
                block = value[:, (j - i) * NB : (j - i + 1) * NB]
                slot = SLOT[i, j]
                if half == 0:
                    main_ref[slot * NB : (slot + 1) * NB, :] = block
                else:
                    store_split(gg_ref, slot, block)
        value = 2.0 * tn(left[0:rows, i * NB : (i + 1) * NB], right[0:rows, width:]) + tn(
            left[base:, i * NB : (i + 1) * NB], right[base:, width:]
        )
        for c in range(NBLK):
            rg_ref[c * width + i * NB : c * width + (i + 1) * NB, :] = value[:, c * NB : (c + 1) * NB]


def spread(value, at):
    return jnp.broadcast_to(value[at : at + 1], (8, 128))


def invert_pivot(ref):
    lane = lax.broadcasted_iota(jnp.int32, (8, 128), 1)
    sub = lax.broadcasted_iota(jnp.int32, (8, 128), 0)
    col = lane & (PB - 1)
    half = lane - col
    tiles = PB // 16

    def pick(value, index):
        return jnp.take_along_axis(value, index, axis=1)

    def group(g, carry):
        at = pl.multiple_of(8 * lax.rem(g, tiles), 8)
        side = lax.div(g, tiles) * PB
        base = 8 * g
        source = ref[pl.ds(at, 8), :]
        panel = pick(source, col + side)
        columns = [pick(source, jnp.full((8, 128), side + base + j, jnp.int32)) for j in range(8)]
        for k in range(0, 8, 2):
            c0, c1 = columns[k], columns[k + 1]
            a, b, c = spread(c0, k), spread(c1, k), spread(c1, k + 1)
            q = pltpu.reciprocal(a * c - b * b, approx=True)
            pa, pb, pc = c * q, b * q, a * q
            s0, s1 = sub == k, sub == k + 1
            m0, m1 = col == base + k, col == base + k + 1
            r0 = jnp.where(m0, 1.0, jnp.where(m1, 0.0, spread(panel, k)))
            r1 = jnp.where(m1, 1.0, jnp.where(m0, 0.0, spread(panel, k + 1)))
            n0 = pa * r0 - pb * r1
            n1 = pc * r1 - pb * r0
            rest = jnp.where(m0 | m1, 0.0, panel) - c0 * n0 - c1 * n1
            panel = jnp.where(s0, n0, jnp.where(s1, n1, rest))
            for j in range(k + 2, 8):
                r0, r1 = spread(columns[j], k), spread(columns[j], k + 1)
                n0 = pa * r0 - pb * r1
                n1 = pc * r1 - pb * r0
                columns[j] = jnp.where(s0, n0, jnp.where(s1, n1, columns[j] - c0 * n0 - c1 * n1))
        rows = [spread(panel, i) for i in range(8)]
        inside = (col >= base) & (col < base + 8)
        for t in range(tiles):
            tile = ref[8 * t : 8 * t + 8, :]
            terms = [pick(tile, half + (base + i)) * rows[i] for i in range(8)]
            kept = jnp.where(inside, 0.0, tile) - terms[0]
            ref[8 * t : 8 * t + 8, :] = (kept - terms[1] - (terms[2] + terms[3])) - (
                (terms[4] + terms[5]) + (terms[6] + terms[7])
            )
        here = ref[pl.ds(at, 8), :]
        ref[pl.ds(at, 8), :] = jnp.where(half == side, panel, here)
        return carry

    lax.fori_loop(0, PB // 8, group, 0)


def halves(value):
    first = value.astype(bf16)
    return first, (value - first.astype(f32)).astype(bf16)


def split_product(a, b):
    a0, a1 = halves(a)
    b0, b1 = halves(b)
    return tn(jnp.concatenate([a0, a0, a1], axis=0), jnp.concatenate([b0, b1, b0], axis=0))


def three(dot, a, b):
    return dot(a[0], b[0]) + (dot(a[0], b[1]) + dot(a[1], b[0]))


def eliminate(a, packed, lower_ref, pivot_ref):
    size = NBLK * NB
    lane = lax.broadcasted_iota(jnp.int32, (PB, size), 1)
    sub = lax.broadcasted_iota(jnp.int32, (PB, size), 0)
    lane32 = lax.broadcasted_iota(jnp.int32, (PB // 2, 128), 1)
    first = lane32 < PB
    for p in range(size // PB):
        r0 = PB * p
        c0 = 128 * (p // 2)
        odd = p % 2 == 1
        row = a[r0 : r0 + PB, :]
        tile = row[:, c0 : c0 + 128]
        turned = pltpu.roll(tile, PB, 1)
        one, two = (turned, tile) if odd else (tile, turned)
        packed[...] = jnp.where(first, one[: PB // 2], two[PB // 2 :])
        invert_pivot(packed)
        inverse = packed[...]
        moved = pltpu.roll(inverse, PB, 1)
        pivot = jnp.concatenate([jnp.where(first, inverse, 0.0), jnp.where(first, moved, 0.0)], axis=0)
        if odd:
            placed = jnp.concatenate([jnp.where(first, 0.0, moved), jnp.where(first, 0.0, inverse)], axis=0)
        else:
            placed = pivot
        pivot_ref[r0 : r0 + PB, :] = placed
        unit = jnp.where(lane == sub + r0, 1.0, 0.0)
        lower_ref[r0 : r0 + PB, :] = jnp.where(lane < r0, row, unit)
        if r0 + PB < size:
            inside = (lane >= r0) & (lane < r0 + PB)
            scaled = split_product(pivot[:, :PB], jnp.where(inside, unit, row))
            c1 = 128 * ((p + 1) // 2)
            below = jnp.where(lane >= r0 + PB, row, 0.0)[:, c1:]
            change = split_product(below, scaled)
            wide = lax.broadcasted_iota(jnp.int32, (size - c1, 128), 1)
            own = (wide >= r0 - c0) & (wide < r0 - c0 + PB)
            a[c1:, c0 : c0 + 128] = jnp.where(own, 0.0, a[c1:, c0 : c0 + 128])
            a[c1:, :] = a[c1:, :] - change


def damped(block, damping, profile):
    row = lax.broadcasted_iota(jnp.int32, (NB, NB), 0)
    col = lax.broadcasted_iota(jnp.int32, (NB, NB), 1)
    return block + jnp.where(row == col, damping * profile, 0.0)


def unpack(source, a, damping, profile):
    a[...] = jnp.zeros_like(a)
    for (i, j), slot in SLOT.items():
        block = source[slot * NB : (slot + 1) * NB, :]
        if i == j:
            block = damped(block, damping, profile[:, i * NB : (i + 1) * NB])
        a[i * NB : (i + 1) * NB, j * NB : (j + 1) * NB] = block


def read_damping(main_ref):
    scal = main_ref[SUM_AT + PART : SUM_AT + PART + 8, :]
    return scal[0:1, 0:1] / scal[0:1, 1:2]


def by_row(matrix, row):
    return jnp.sum(matrix * row, axis=1, keepdims=True)


def by_column(matrix, column):
    return jnp.sum(matrix * column, axis=0, keepdims=True)


def turn(row):
    return jnp.broadcast_to(row, (8, NB)).T


def wide_row(ref, at):
    return jnp.concatenate([ref[at + c : at + c + 1, :] for c in range(NBLK)], axis=1)


def regional_kernel(main_ref, prior_ref, lower_ref, pivot_ref, a, packed):
    unpack(main_ref, a, read_damping(main_ref), prior_ref[0:1, : NBLK * NB])
    eliminate(a, packed, lower_ref, pivot_ref)


def coupling_kernel(main_ref, rg_ref, lower_ref, pivot_ref, out_ref, scaled_ref, q_ref, b0, b1, u0, u1, w0, w1):
    width = NBLK * NB
    for c in range(NBLK):
        lanes = slice(c * NB, (c + 1) * NB)
        b0[:, lanes], b1[:, lanes] = halves(rg_ref[c * width : (c + 1) * width, :])
        column = turn(main_ref[TRI + c : TRI + c + 1, :])
        column = jnp.concatenate([column, jnp.zeros((NB, NB - 8), f32)], axis=1)
        b0[lanes, width:], b1[lanes, width:] = halves(column)
    for i in range(NBLK):
        rows = slice(i * NB, (i + 1) * NB)
        depth = slice(0, (i + 1) * NB)
        value = three(nn, halves(lower_ref[rows, depth]), (b0[depth, :], b1[depth, :]))
        parts = halves(value)
        u0[rows, :], u1[rows, :] = parts[0][:, :width], parts[1][:, :width]
        value = three(nn, halves(pivot_ref[rows, :]), parts)
        scaled_ref[rows, :] = value[:, :width]
        q_ref[rows, :] = value[:, width:]
        w0[rows, :], w1[rows, :] = halves(value)
    sub = lax.broadcasted_iota(jnp.int32, (8, NB), 0)
    tail = jnp.zeros((8, NB), f32)
    for i in range(NBLK):
        lanes = slice(i * NB, (i + 1) * NB)
        value = three(tn, (u0[:, lanes], u1[:, lanes]), (w0[:, i * NB :], w1[:, i * NB :]))
        for j in range(i, NBLK):
            store_split(out_ref, SLOT[i, j], value[:, (j - i) * NB : (j - i + 1) * NB])
        line = TRI + NBLK + i
        rest = jnp.broadcast_to(main_ref[line : line + 1, :], (8, NB)) - value[:, width - i * NB :].T[:8]
        tail = jnp.where(sub == i, jnp.broadcast_to(rest[0:1], (8, NB)), tail)
    for part in range(REG_PARTS):
        out_ref[part * PART_ROWS + PART : (part + 1) * PART_ROWS, :] = tail


def finish_kernel(
    g_ref, v_ref, main_ref, prior_ref, flower_ref, scaled_ref, q_ref, red_ref, aux_ref,
    local_ref, regional_ref, global_ref,
    a, packed, lower, pivot,
):
    nparams = local_ref.shape[0]
    width = NBLK * NB
    unpack(g_ref, a, read_damping(main_ref), prior_ref[0:1, width:])
    eliminate(a, packed, lower, pivot)
    whole = lower[...]
    forward = by_row(whole, wide_row(v_ref, 0))
    forward = jnp.concatenate(
        [
            turn(by_column(pivot[i * NB : (i + 1) * NB, :], forward[i * NB : (i + 1) * NB]))[:, 0:1]
            for i in range(NBLK)
        ],
        axis=0,
    )
    global_step = by_column(whole, forward)
    rest = q_ref[:, 0:1] - by_row(scaled_ref[...], global_step)
    regional_step = by_column(flower_ref[...], rest)
    regional_ref[...] = regional_step
    global_ref[...] = global_step

    aux = aux_ref[...]
    at = 0
    factor = [[None] * nparams for i in range(nparams)]
    for i in range(nparams):
        for c in range(i + 1):
            factor[i][c] = aux[:, at : at + 1]
            at += 1
    update = jnp.concatenate([regional_step, global_step], axis=1)
    target = []
    for i in range(nparams):
        target.append(
            aux[:, at : at + 1] - jnp.sum(red_ref[8 * i : 8 * i + 8, :] * update, axis=1, keepdims=True)
        )
        at += 1
    found = backward_small(factor, target)
    sub = lax.broadcasted_iota(jnp.int32, (8, 8), 0)
    lane = lax.broadcasted_iota(jnp.int32, (8, 8), 1)
    for i in range(nparams):
        local_ref[i : i + 1, :] = jnp.sum(jnp.where(sub == lane, found[i], 0.0), axis=0, keepdims=True)


def join_kernel(parts_ref, rest_ref, out_ref, total, sems):
    parts = total.shape[0]
    aside = pltpu.make_async_copy(rest_ref, out_ref.at[pl.ds(parts, rest_ref.shape[0])], sems.at[0])
    aside.start()
    total[...] = jnp.sum(parts_ref[...], axis=0)
    copy = pltpu.make_async_copy(total, out_ref.at[pl.ds(0, parts)], sems.at[1])
    copy.start()
    copy.wait()
    aside.wait()


def sum_kernel(parts_ref, out_ref, total, sem):
    total[...] = jnp.sum(parts_ref[...], axis=0)
    copy = pltpu.make_async_copy(total, out_ref, sem)
    copy.start()
    copy.wait()


def shape(*dims, dtype=f32):
    return jax.ShapeDtypeStruct(dims, dtype)


VMEM = pl.BlockSpec(memory_space=pltpu.VMEM)
SMEM = pl.BlockSpec(memory_space=pltpu.SMEM)
HBM = pl.BlockSpec(memory_space=pltpu.HBM)


def whole_block(dims):
    return pl.BlockSpec(dims, lambda i: (0,) * len(dims))


def call(kernel, out_shape, scratch, specs, flops, grid=(), limit=16, out=VMEM):
    return pl.pallas_call(
        kernel,
        grid=grid,
        out_shape=out_shape,
        in_specs=specs,
        out_specs=[out] * len(out_shape),
        scratch_shapes=scratch,
        name=kernel.__name__,
        compiler_params=pltpu.CompilerParams(vmem_limit_bytes=limit * 1024 * 1024),
        cost_estimate=pl.CostEstimate(flops=flops, bytes_accessed=4_000_000, transcendentals=0),
    )


def part_sums(value, axis, parts):
    moved = lax.all_to_all(value, axis, 0, 0, tiled=True)
    return jnp.sum(moved.reshape((parts, value.shape[0] // parts) + value.shape[1:]), axis=0)


def copies_back(piece, axis, parts):
    copies = jnp.broadcast_to(piece[None], (parts,) + piece.shape).reshape((-1,) + piece.shape[1:])
    return lax.all_to_all(copies, axis, 0, 0, tiled=True)


def body(
    local_jac,
    global_jac,
    coeff_index,
    coeff_weight,
    residual,
    obs_weight,
    obs_count,
    local_prior,
    regional_prior,
    global_prior,
):
    nx, nz = lax.axis_size("x"), lax.axis_size("z")
    rows = residual.shape[0]
    nparams = local_jac.shape[0]
    width = global_jac.shape[1]
    stack = 2 * rows + 6 * RPAD
    gg, main, rg, red, aux, prior = call(
        assemble_kernel,
        [
            shape(REG_PARTS * PART_ROWS, NB),
            shape(SUM_AT, NB),
            shape(NBLK * width, NB),
            shape(RPAD, 2 * width),
            shape(8, NB),
            shape(8, 2 * width),
        ],
        [
            pltpu.VMEM((stack, 2 * width), bf16),
            pltpu.VMEM((stack, 2 * width), bf16),
            pltpu.VMEM((NB, 512), f32),
        ],
        [
            whole_block(local_jac.shape), whole_block(global_jac.shape), whole_block(coeff_index.shape),
            whole_block(coeff_weight.shape), whole_block((1, rows)), whole_block((1, rows)), SMEM,
            whole_block(local_prior.shape), whole_block((1, width)), whole_block((1, width)),
        ],
        2_000_000_000,
        grid=(1,),
        limit=60,
    )(
        local_jac, global_jac, coeff_index, coeff_weight, residual[None], obs_weight[None],
        obs_count, local_prior, regional_prior, global_prior[None],
    )
    share = part_sums(gg, GROUPS, REG_PARTS)
    rg = lax.psum_scatter(rg, "x", scatter_dimension=0, tiled=True)
    main = jnp.concatenate([main, share, jnp.zeros((MAIN_ROWS - SUM_AT - PART_ROWS, NB), f32)], axis=0)
    main = lax.all_to_all(main, "x", 0, 0, tiled=True).reshape(nx, -1, NB)
    count = main.shape[1] + rg.shape[0]
    both = call(
        join_kernel,
        [shape(count, NB)],
        [pltpu.VMEM(main.shape[1:], f32), pltpu.SemaphoreType.DMA((2,))],
        [whole_block(main.shape), HBM],
        1_000_000,
        grid=(1,),
        limit=60,
        out=HBM,
    )(main, rg)[0]
    both = lax.all_to_all(both, "z", 0, 0, tiled=True).reshape(nz, -1, NB)
    both = call(
        sum_kernel,
        [shape(*both.shape[1:])],
        [pltpu.VMEM(both.shape[1:], f32), pltpu.SemaphoreType.DMA],
        [whole_block(both.shape)],
        1_000_000,
        grid=(1,),
        limit=60,
        out=HBM,
    )(both)[0]
    both = lax.all_gather(both, "z", axis=0, tiled=True)
    main = lax.all_gather(both[: MAIN_ROWS // nx], "x", axis=0, tiled=True)
    main, rg = lax.optimization_barrier((main, both[MAIN_ROWS // nx :]))
    rg = copies_back(rg, "x", nx)
    lower, pivot = call(
        regional_kernel,
        [shape(width, width), shape(width, NB)],
        [pltpu.VMEM((width, width), f32), pltpu.VMEM((PB // 2, 128), f32)],
        [VMEM] * 2,
        20_000_000_000,
    )(main, prior)
    outer, scaled, q = call(
        coupling_kernel,
        [shape(REG_PARTS * PART_ROWS, NB), shape(width, width), shape(width, NB)],
        [
            pltpu.VMEM((width, width + NB), bf16),
            pltpu.VMEM((width, width + NB), bf16),
            pltpu.VMEM((width, width), bf16),
            pltpu.VMEM((width, width), bf16),
            pltpu.VMEM((width, width + NB), bf16),
            pltpu.VMEM((width, width + NB), bf16),
        ],
        [VMEM] * 4,
        4_000_000_000,
    )(main, rg, lower, pivot)
    outer = part_sums(outer, GROUPS, REG_PARTS)
    mine = main[SUM_AT : SUM_AT + PART] - outer[:PART]
    matrix = lax.all_gather(mine, GROUPS, axis=0, tiled=True)
    local_step, regional_step, global_step = call(
        finish_kernel,
        [shape(nparams, 8), shape(1, width), shape(1, width)],
        [
            pltpu.VMEM((width, width), f32),
            pltpu.VMEM((PB // 2, 128), f32),
            pltpu.VMEM((width, width), f32),
            pltpu.VMEM((width, NB), f32),
        ],
        [VMEM] * 9,
        20_000_000_000,
    )(matrix, outer[PART:], main, prior, lower, scaled, q, red, aux)
    return local_step, regional_step, global_step[0]


def solution(mesh):
    devices = mesh.devices.reshape(4, 2, 4, 16)
    split = Mesh(devices, ("y", "core", "x", "z"))
    both = GROUPS + LAYERS
    return jax.shard_map(
        body,
        mesh=split,
        in_specs=(
            P(None, both),
            P(both, None),
            P(None, both),
            P(None, both),
            P(both),
            P(both),
            P(both),
            P(None, both),
            P(GROUPS, None),
            P(),
        ),
        out_specs=(P(None, both), P(GROUPS, None), P()),
        check_vma=False,
    )
```

```python
import jax
import jax.numpy as jnp
from jax import lax
from jax.experimental import pallas as pl
from jax.experimental.pallas import tpu as pltpu
from jax.sharding import Mesh, PartitionSpec as P

f32 = jnp.float32
bf16 = jnp.bfloat16
HIGHEST = lax.Precision.HIGHEST

NB = 128
NBLK = 4
PB = 64
PAIRS = [(i, j) for i in range(NBLK) for j in range(i, NBLK)]
SLOT = {pair: at for at, pair in enumerate(PAIRS)}
TRI = len(PAIRS) * NB
REG_PARTS = 8
PART = TRI // REG_PARTS
PART_ROWS = PART + 8
MAIN_ROWS = 1536
SUM_AT = TRI + 8
CHUNK = 48
RPAD = 64

LAYERS = ("x", "z")
GROUPS = ("y", "core")


def tn(a, b, precision=None):
    return lax.dot_general(
        a, b, (((0,), (0,)), ((), ())), precision=precision, preferred_element_type=f32
    )


def nt(a, b, precision=None):
    return lax.dot_general(
        a, b, (((1,), (1,)), ((), ())), precision=precision, preferred_element_type=f32
    )


def nn(a, b, precision=None):
    return jnp.dot(a, b, precision=precision, preferred_element_type=f32)


def pieces(value):
    first = value.astype(bf16)
    rest = value - first.astype(f32)
    second = rest.astype(bf16)
    third = (rest - second.astype(f32)).astype(bf16)
    return first, second, third


def cholesky_small(entries):
    order = len(entries)
    factor = [[None] * order for i in range(order)]
    for j in range(order):
        diagonal = entries[j][j]
        for k in range(j):
            diagonal = diagonal - factor[j][k] * factor[j][k]
        factor[j][j] = jnp.sqrt(diagonal)
        for i in range(j + 1, order):
            current = entries[i][j]
            for k in range(j):
                current = current - factor[i][k] * factor[j][k]
            factor[i][j] = current / factor[j][j]
    return factor


def forward_small(factor, target):
    result = []
    for a in range(len(target)):
        current = target[a]
        for k in range(a):
            current = current - factor[a][k] * result[k]
        result.append(current / factor[a][a])
    return result


def backward_small(factor, target):
    order = len(target)
    result = [None] * order
    for a in reversed(range(order)):
        current = target[a]
        for k in range(a + 1, order):
            current = current - factor[k][a] * result[k]
        result[a] = current / factor[a][a]
    return result


def store_split(ref, slot, block):
    done = 0
    while done < NB:
        flat = slot * NB + done
        part, off = flat // PART, flat % PART
        take = min(NB - done, PART - off)
        start = part * PART_ROWS + off
        ref[start : start + take, :] = block[done : done + take]
        done += take


def assemble_kernel(
    lj_ref, gj_ref, ci_ref, cw_ref, res_ref, ow_ref, cnt_ref, lp_ref, rp_ref, gp_ref,
    gg_ref, main_ref, rg_ref, red_ref, aux_ref, prior_ref,
    left, right, padded,
):
    rows = gj_ref.shape[0]
    nparams = lj_ref.shape[0]
    objects = 8
    observed = rows // objects
    width = gj_ref.shape[1]
    res = res_ref[...]
    prior_ref[:, :width] = jnp.broadcast_to(rp_ref[...], (8, width))
    prior_ref[:, width:] = jnp.broadcast_to(gp_ref[...], (8, width))
    position = lax.broadcasted_iota(jnp.int32, (objects, rows), 1)
    owner = lax.broadcasted_iota(jnp.int32, (objects, rows), 0)
    count = jnp.zeros((objects, rows), jnp.int32)
    for n in range(objects):
        count = jnp.where(owner == n, cnt_ref[n], count)
    local = position - owner * observed
    present = (local >= 0) & (local < observed) & (local < count)
    live = jnp.where(present, jnp.broadcast_to(ow_ref[...], (objects, rows)), 0.0)
    weight = jnp.sum(live, axis=0, keepdims=True)
    misfit = jnp.sum(weight * res * res, axis=1, keepdims=True)
    counted = jnp.sum(
        jnp.sum(jnp.where(present, 1.0, 0.0), axis=0, keepdims=True), axis=1, keepdims=True
    )

    padded[...] = jnp.zeros_like(padded)
    padded[0:1, :rows] = weight
    padded[1:5, :rows] = ci_ref[...].astype(f32)
    padded[5:9, :rows] = cw_ref[...].astype(f32)
    for block in range(padded.shape[1] // NB):
        columns = padded[:, block * NB : (block + 1) * NB].T
        low = block * NB
        while low < min((block + 1) * NB, rows):
            high = min(low + 32, rows)
            here = columns[low - block * NB : high - block * NB]
            weights = here[:, 0:1]
            lanes = lax.broadcasted_iota(jnp.int32, (high - low, width), 1).astype(f32)
            total = jnp.zeros((high - low, width), f32)
            for k in range(4):
                total = total + jnp.where(here[:, 1 + k : 2 + k] == lanes, here[:, 5 + k : 6 + k], 0.0)
            joined = total.astype(bf16)
            for at, value in ((0, joined), (width, gj_ref[low:high, :])):
                scaled = (value.astype(f32) * weights).astype(bf16)
                right[low:high, at : at + width] = value
                right[rows + low : rows + high, at : at + width] = scaled
                left[low:high, at : at + width] = (scaled.astype(f32) * 0.5).astype(bf16)
                left[rows + low : rows + high, at : at + width] = (value.astype(f32) * 0.5).astype(bf16)
            low = high

    jac = lj_ref[...].astype(f32)
    weighted = [jac[a : a + 1, :] * live for a in range(nparams)]
    entries = [[None] * nparams for a in range(nparams)]
    owner8 = lax.broadcasted_iota(jnp.int32, (objects, objects), 0)
    lane8 = lax.broadcasted_iota(jnp.int32, (objects, objects), 1)
    for a in range(nparams):
        for b in range(a + 1):
            value = jnp.sum(weighted[a] * jac[b : b + 1, :], axis=1, keepdims=True)
            if a == b:
                prior = jnp.broadcast_to(lp_ref[a : a + 1, :], (objects, objects))
                value = value + jnp.sum(jnp.where(owner8 == lane8, prior, 0.0), axis=1, keepdims=True)
            entries[a][b] = value
    factor = cholesky_small(entries)
    local_gradient = [jnp.sum(weighted[a] * res, axis=1, keepdims=True) for a in range(nparams)]
    reduced_gradient = forward_small(factor, local_gradient)

    blank = jnp.zeros((8, rows), f32)
    stacked = jnp.concatenate(weighted + [blank], axis=0)
    everything = right[0:rows, :]
    coupling = None
    for piece in pieces(stacked):
        term = nn(piece, everything)
        coupling = term if coupling is None else coupling + term
    reduced = forward_small(factor, [coupling[8 * a : 8 * a + 8] for a in range(nparams)])
    joint = jnp.concatenate(reduced + [jnp.zeros((8, 2 * width), f32)], axis=0)
    red_ref[...] = joint
    r0, r1, r2 = pieces(joint)
    base = 2 * rows
    for at, (one, two) in enumerate(((r0, r0), (r0, r1), (r1, r0), (r1, r1), (r0, r2), (r2, r0))):
        left[base + at * RPAD : base + (at + 1) * RPAD, :] = -one
        right[base + at * RPAD : base + (at + 1) * RPAD, :] = two

    lane = lax.broadcasted_iota(jnp.int32, (objects, NB), 1)
    aux = jnp.zeros((objects, NB), f32)
    at = 0
    for a in range(nparams):
        for b in range(a + 1):
            aux = jnp.where(lane == at, factor[a][b], aux)
            at += 1
    for a in range(nparams):
        aux = jnp.where(lane == at, reduced_gradient[a], aux)
        at += 1
    aux_ref[...] = aux

    first, second, third = pieces(res)
    lhs = jnp.concatenate(
        [first.astype(f32), second.astype(f32), third.astype(f32), jnp.zeros((13, rows), f32)], axis=0
    ).astype(bf16)
    gradient = jnp.sum(nn(lhs, right[rows : 2 * rows, :]), axis=0, keepdims=True)
    for a in range(nparams):
        gradient = gradient - jnp.sum(reduced_gradient[a] * reduced[a], axis=0, keepdims=True)
    for at in range(8):
        main_ref[TRI + at : TRI + at + 1, :] = gradient[:, at * NB : (at + 1) * NB]

    row_lane = lax.broadcasted_iota(jnp.int32, (8, NB), 1)
    scalars = jnp.where(row_lane == 0, misfit, jnp.where(row_lane == 1, counted, 0.0))
    for part in range(REG_PARTS):
        gg_ref[part * PART_ROWS + PART : (part + 1) * PART_ROWS, :] = scalars
    for i in range(NBLK):
        for half in range(2):
            at = half * width
            value = tn(left[:, at + i * NB : at + (i + 1) * NB], right[:, at + i * NB : at + width])
            for j in range(i, NBLK):
                block = value[:, (j - i) * NB : (j - i + 1) * NB]
                slot = SLOT[i, j]
                if half == 0:
                    main_ref[slot * NB : (slot + 1) * NB, :] = block
                else:
                    store_split(gg_ref, slot, block)
        value = 2.0 * tn(left[0:rows, i * NB : (i + 1) * NB], right[0:rows, width:]) + tn(
            left[base:, i * NB : (i + 1) * NB], right[base:, width:]
        )
        for c in range(NBLK):
            rg_ref[c * width + i * NB : c * width + (i + 1) * NB, :] = value[:, c * NB : (c + 1) * NB]


def spread(value, at):
    return jnp.broadcast_to(value[at : at + 1], (8, 128))


def invert_pivot(ref):
    lane = lax.broadcasted_iota(jnp.int32, (8, 128), 1)
    sub = lax.broadcasted_iota(jnp.int32, (8, 128), 0)
    col = lane & (PB - 1)
    half = lane - col
    tiles = PB // 16

    def pick(value, index):
        return jnp.take_along_axis(value, index, axis=1)

    def group(g, carry):
        at = pl.multiple_of(8 * lax.rem(g, tiles), 8)
        side = lax.div(g, tiles) * PB
        base = 8 * g
        source = ref[pl.ds(at, 8), :]
        panel = pick(source, col + side)
        columns = [pick(source, jnp.full((8, 128), side + base + j, jnp.int32)) for j in range(8)]
        for k in range(0, 8, 2):
            c0, c1 = columns[k], columns[k + 1]
            a, b, c = spread(c0, k), spread(c1, k), spread(c1, k + 1)
            q = 1.0 / (a * c - b * b)
            pa, pb, pc = c * q, b * q, a * q
            s0, s1 = sub == k, sub == k + 1
            m0, m1 = col == base + k, col == base + k + 1
            r0 = jnp.where(m0, 1.0, jnp.where(m1, 0.0, spread(panel, k)))
            r1 = jnp.where(m1, 1.0, jnp.where(m0, 0.0, spread(panel, k + 1)))
            n0 = pa * r0 - pb * r1
            n1 = pc * r1 - pb * r0
            rest = jnp.where(m0 | m1, 0.0, panel) - c0 * n0 - c1 * n1
            panel = jnp.where(s0, n0, jnp.where(s1, n1, rest))
            for j in range(k + 2, 8):
                r0, r1 = spread(columns[j], k), spread(columns[j], k + 1)
                n0 = pa * r0 - pb * r1
                n1 = pc * r1 - pb * r0
                columns[j] = jnp.where(s0, n0, jnp.where(s1, n1, columns[j] - c0 * n0 - c1 * n1))
        rows = [spread(panel, i) for i in range(8)]
        inside = (col >= base) & (col < base + 8)
        for t in range(tiles):
            tile = ref[8 * t : 8 * t + 8, :]
            terms = [pick(tile, half + (base + i)) * rows[i] for i in range(8)]
            kept = jnp.where(inside, 0.0, tile) - terms[0]
            ref[8 * t : 8 * t + 8, :] = (kept - terms[1] - (terms[2] + terms[3])) - (
                (terms[4] + terms[5]) + (terms[6] + terms[7])
            )
        here = ref[pl.ds(at, 8), :]
        ref[pl.ds(at, 8), :] = jnp.where(half == side, panel, here)
        return carry

    lax.fori_loop(0, PB // 8, group, 0)


def split_product(a, b):
    a0, a1, a2 = pieces(a)
    b0, b1, b2 = pieces(b)
    left = jnp.concatenate([a0, a0, a1, a1, a0, a2], axis=0)
    right = jnp.concatenate([b0, b1, b0, b1, b2, b0], axis=0)
    return tn(left, right)


def halves(value):
    first = value.astype(bf16)
    return first, (value - first.astype(f32)).astype(bf16)


def three(dot, a, b):
    return dot(a[0], b[0]) + (dot(a[0], b[1]) + dot(a[1], b[0]))


def eliminate(a, packed, lower_ref, pivot_ref):
    size = NBLK * NB
    lane = lax.broadcasted_iota(jnp.int32, (PB, size), 1)
    sub = lax.broadcasted_iota(jnp.int32, (PB, size), 0)
    lane32 = lax.broadcasted_iota(jnp.int32, (PB // 2, 128), 1)
    first = lane32 < PB
    for p in range(size // PB):
        r0 = PB * p
        c0 = 128 * (p // 2)
        odd = p % 2 == 1
        row = a[r0 : r0 + PB, :]
        tile = row[:, c0 : c0 + 128]
        turned = pltpu.roll(tile, PB, 1)
        one, two = (turned, tile) if odd else (tile, turned)
        packed[...] = jnp.where(first, one[: PB // 2], two[PB // 2 :])
        invert_pivot(packed)
        inverse = packed[...]
        moved = pltpu.roll(inverse, PB, 1)
        pivot = jnp.concatenate([jnp.where(first, inverse, 0.0), jnp.where(first, moved, 0.0)], axis=0)
        if odd:
            placed = jnp.concatenate([jnp.where(first, 0.0, moved), jnp.where(first, 0.0, inverse)], axis=0)
        else:
            placed = pivot
        pivot_ref[r0 : r0 + PB, :] = placed
        unit = jnp.where(lane == sub + r0, 1.0, 0.0)
        lower_ref[r0 : r0 + PB, :] = jnp.where(lane < r0, row, unit)
        if r0 + PB < size:
            inside = (lane >= r0) & (lane < r0 + PB)
            scaled = split_product(pivot[:, :PB], jnp.where(inside, unit, row))
            c1 = 128 * ((p + 1) // 2)
            below = jnp.where(lane >= r0 + PB, row, 0.0)[:, c1:]
            change = split_product(below, scaled)
            wide = lax.broadcasted_iota(jnp.int32, (size - c1, 128), 1)
            own = (wide >= r0 - c0) & (wide < r0 - c0 + PB)
            a[c1:, c0 : c0 + 128] = jnp.where(own, 0.0, a[c1:, c0 : c0 + 128])
            a[c1:, :] = a[c1:, :] - change


def damped(block, damping, profile):
    row = lax.broadcasted_iota(jnp.int32, (NB, NB), 0)
    col = lax.broadcasted_iota(jnp.int32, (NB, NB), 1)
    return block + jnp.where(row == col, damping * profile, 0.0)


def unpack(source, a, damping, profile):
    a[...] = jnp.zeros_like(a)
    for (i, j), slot in SLOT.items():
        block = source[slot * NB : (slot + 1) * NB, :]
        if i == j:
            block = damped(block, damping, profile[:, i * NB : (i + 1) * NB])
        a[i * NB : (i + 1) * NB, j * NB : (j + 1) * NB] = block


def read_damping(main_ref):
    scal = main_ref[SUM_AT + PART : SUM_AT + PART + 8, :]
    return scal[0:1, 0:1] / scal[0:1, 1:2]


def by_row(matrix, row):
    return jnp.sum(matrix * row, axis=1, keepdims=True)


def by_column(matrix, column):
    return jnp.sum(matrix * column, axis=0, keepdims=True)


def turn(row):
    return jnp.broadcast_to(row, (8, NB)).T


def wide_row(ref, at):
    return jnp.concatenate([ref[at + c : at + c + 1, :] for c in range(NBLK)], axis=1)


def regional_kernel(main_ref, prior_ref, lower_ref, pivot_ref, a, packed):
    unpack(main_ref, a, read_damping(main_ref), prior_ref[0:1, : NBLK * NB])
    eliminate(a, packed, lower_ref, pivot_ref)


def coupling_kernel(main_ref, rg_ref, lower_ref, pivot_ref, out_ref, scaled_ref, q_ref, b0, b1, u0, u1, w0, w1):
    width = NBLK * NB
    for c in range(NBLK):
        lanes = slice(c * NB, (c + 1) * NB)
        b0[:, lanes], b1[:, lanes] = halves(rg_ref[c * width : (c + 1) * width, :])
        column = turn(main_ref[TRI + c : TRI + c + 1, :])
        column = jnp.concatenate([column, jnp.zeros((NB, NB - 8), f32)], axis=1)
        b0[lanes, width:], b1[lanes, width:] = halves(column)
    for i in range(NBLK):
        rows = slice(i * NB, (i + 1) * NB)
        depth = slice(0, (i + 1) * NB)
        value = three(nn, halves(lower_ref[rows, depth]), (b0[depth, :], b1[depth, :]))
        parts = halves(value)
        u0[rows, :], u1[rows, :] = parts[0][:, :width], parts[1][:, :width]
        value = three(nn, halves(pivot_ref[rows, :]), parts)
        scaled_ref[rows, :] = value[:, :width]
        q_ref[rows, :] = value[:, width:]
        w0[rows, :], w1[rows, :] = halves(value)
    sub = lax.broadcasted_iota(jnp.int32, (8, NB), 0)
    tail = jnp.zeros((8, NB), f32)
    for i in range(NBLK):
        lanes = slice(i * NB, (i + 1) * NB)
        value = three(tn, (u0[:, lanes], u1[:, lanes]), (w0[:, i * NB :], w1[:, i * NB :]))
        for j in range(i, NBLK):
            store_split(out_ref, SLOT[i, j], value[:, (j - i) * NB : (j - i + 1) * NB])
        line = TRI + NBLK + i
        rest = jnp.broadcast_to(main_ref[line : line + 1, :], (8, NB)) - value[:, width - i * NB :].T[:8]
        tail = jnp.where(sub == i, jnp.broadcast_to(rest[0:1], (8, NB)), tail)
    for part in range(REG_PARTS):
        out_ref[part * PART_ROWS + PART : (part + 1) * PART_ROWS, :] = tail


def finish_kernel(
    g_ref, v_ref, main_ref, prior_ref, flower_ref, scaled_ref, q_ref, red_ref, aux_ref,
    local_ref, regional_ref, global_ref,
    a, packed, lower, pivot,
):
    nparams = local_ref.shape[0]
    width = NBLK * NB
    unpack(g_ref, a, read_damping(main_ref), prior_ref[0:1, width:])
    eliminate(a, packed, lower, pivot)
    whole = lower[...]
    forward = by_row(whole, wide_row(v_ref, 0))
    forward = jnp.concatenate(
        [
            turn(by_column(pivot[i * NB : (i + 1) * NB, :], forward[i * NB : (i + 1) * NB]))[:, 0:1]
            for i in range(NBLK)
        ],
        axis=0,
    )
    global_step = by_column(whole, forward)
    rest = q_ref[:, 0:1] - by_row(scaled_ref[...], global_step)
    regional_step = by_column(flower_ref[...], rest)
    regional_ref[...] = regional_step
    global_ref[...] = global_step

    aux = aux_ref[...]
    at = 0
    factor = [[None] * nparams for i in range(nparams)]
    for i in range(nparams):
        for c in range(i + 1):
            factor[i][c] = aux[:, at : at + 1]
            at += 1
    update = jnp.concatenate([regional_step, global_step], axis=1)
    target = []
    for i in range(nparams):
        target.append(
            aux[:, at : at + 1] - jnp.sum(red_ref[8 * i : 8 * i + 8, :] * update, axis=1, keepdims=True)
        )
        at += 1
    found = backward_small(factor, target)
    sub = lax.broadcasted_iota(jnp.int32, (8, 8), 0)
    lane = lax.broadcasted_iota(jnp.int32, (8, 8), 1)
    for i in range(nparams):
        local_ref[i : i + 1, :] = jnp.sum(jnp.where(sub == lane, found[i], 0.0), axis=0, keepdims=True)


def shape(*dims, dtype=f32):
    return jax.ShapeDtypeStruct(dims, dtype)


VMEM = pl.BlockSpec(memory_space=pltpu.VMEM)
SMEM = pl.BlockSpec(memory_space=pltpu.SMEM)


def whole_block(dims):
    return pl.BlockSpec(dims, lambda i: (0,) * len(dims))


def call(kernel, out_shape, scratch, specs, flops, grid=(), limit=16):
    return pl.pallas_call(
        kernel,
        grid=grid,
        out_shape=out_shape,
        in_specs=specs,
        out_specs=[VMEM] * len(out_shape),
        scratch_shapes=scratch,
        name=kernel.__name__,
        compiler_params=pltpu.CompilerParams(vmem_limit_bytes=limit * 1024 * 1024),
        cost_estimate=pl.CostEstimate(flops=flops, bytes_accessed=4_000_000, transcendentals=0),
    )


def part_sums(value, axis, parts):
    moved = lax.all_to_all(value, axis, 0, 0, tiled=True)
    return jnp.sum(moved.reshape((parts, value.shape[0] // parts) + value.shape[1:]), axis=0)


def copies_back(piece, axis, parts):
    copies = jnp.broadcast_to(piece[None], (parts,) + piece.shape).reshape((-1,) + piece.shape[1:])
    return lax.all_to_all(copies, axis, 0, 0, tiled=True)


def body(
    local_jac,
    global_jac,
    coeff_index,
    coeff_weight,
    residual,
    obs_weight,
    obs_count,
    local_prior,
    regional_prior,
    global_prior,
):
    nx, nz = lax.axis_size("x"), lax.axis_size("z")
    rows = residual.shape[0]
    nparams = local_jac.shape[0]
    width = global_jac.shape[1]
    stack = 2 * rows + 6 * RPAD
    gg, main, rg, red, aux, prior = call(
        assemble_kernel,
        [
            shape(REG_PARTS * PART_ROWS, NB),
            shape(SUM_AT, NB),
            shape(NBLK * width, NB),
            shape(RPAD, 2 * width),
            shape(8, NB),
            shape(8, 2 * width),
        ],
        [
            pltpu.VMEM((stack, 2 * width), bf16),
            pltpu.VMEM((stack, 2 * width), bf16),
            pltpu.VMEM((NB, 512), f32),
        ],
        [
            whole_block(local_jac.shape), whole_block(global_jac.shape), whole_block(coeff_index.shape),
            whole_block(coeff_weight.shape), whole_block((1, rows)), whole_block((1, rows)), SMEM,
            whole_block(local_prior.shape), whole_block((1, width)), whole_block((1, width)),
        ],
        2_000_000_000,
        grid=(1,),
        limit=60,
    )(
        local_jac, global_jac, coeff_index, coeff_weight, residual[None], obs_weight[None],
        obs_count, local_prior, regional_prior, global_prior[None],
    )
    share = part_sums(gg, GROUPS, REG_PARTS)
    rg = lax.psum_scatter(rg, "x", scatter_dimension=0, tiled=True)
    main = jnp.concatenate([main, share, jnp.zeros((MAIN_ROWS - SUM_AT - PART_ROWS, NB), f32)], axis=0)
    main = part_sums(main, "x", nx)
    both = part_sums(jnp.concatenate([main, rg], axis=0), "z", nz)
    both = copies_back(both, "z", nz)
    main = lax.all_gather(both[: MAIN_ROWS // nx], "x", axis=0, tiled=True)
    main, rg = lax.optimization_barrier((main, both[MAIN_ROWS // nx :]))
    rg = copies_back(rg, "x", nx)
    lower, pivot = call(
        regional_kernel,
        [shape(width, width), shape(width, NB)],
        [pltpu.VMEM((width, width), f32), pltpu.VMEM((PB // 2, 128), f32)],
        [VMEM] * 2,
        20_000_000_000,
    )(main, prior)
    outer, scaled, q = call(
        coupling_kernel,
        [shape(REG_PARTS * PART_ROWS, NB), shape(width, width), shape(width, NB)],
        [
            pltpu.VMEM((width, width + NB), bf16),
            pltpu.VMEM((width, width + NB), bf16),
            pltpu.VMEM((width, width), bf16),
            pltpu.VMEM((width, width), bf16),
            pltpu.VMEM((width, width + NB), bf16),
            pltpu.VMEM((width, width + NB), bf16),
        ],
        [VMEM] * 4,
        4_000_000_000,
    )(main, rg, lower, pivot)
    outer = part_sums(outer, GROUPS, REG_PARTS)
    mine = main[SUM_AT : SUM_AT + PART] - outer[:PART]
    matrix = lax.all_gather(mine, GROUPS, axis=0, tiled=True)
    local_step, regional_step, global_step = call(
        finish_kernel,
        [shape(nparams, 8), shape(1, width), shape(1, width)],
        [
            pltpu.VMEM((width, width), f32),
            pltpu.VMEM((PB // 2, 128), f32),
            pltpu.VMEM((width, width), f32),
            pltpu.VMEM((width, NB), f32),
        ],
        [VMEM] * 9,
        20_000_000_000,
    )(matrix, outer[PART:], main, prior, lower, scaled, q, red, aux)
    return local_step, regional_step, global_step[0]


def solution(mesh):
    devices = mesh.devices.reshape(4, 2, 4, 16)
    split = Mesh(devices, ("y", "core", "x", "z"))
    both = GROUPS + LAYERS
    return jax.shard_map(
        body,
        mesh=split,
        in_specs=(
            P(None, both),
            P(both, None),
            P(None, both),
            P(None, both),
            P(both),
            P(both),
            P(both),
            P(None, both),
            P(GROUPS, None),
            P(),
        ),
        out_specs=(P(None, both), P(GROUPS, None), P()),
        check_vma=False,
    )
```

```python
import jax
import jax.numpy as jnp
from jax import lax
from jax.experimental import pallas as pl
from jax.experimental.pallas import tpu as pltpu
from jax.sharding import Mesh, PartitionSpec as P

f32 = jnp.float32
bf16 = jnp.bfloat16
HIGHEST = lax.Precision.HIGHEST

NB = 128
NBLK = 4
PB = 64
PAIRS = [(i, j) for i in range(NBLK) for j in range(i, NBLK)]
SLOT = {pair: at for at, pair in enumerate(PAIRS)}
TRI = len(PAIRS) * NB
REG_PARTS = 8
PART = TRI // REG_PARTS
PART_ROWS = PART + 8
MAIN_ROWS = 1536
SUM_AT = TRI + 8
CHUNK = 48
RPAD = 64

LAYERS = ("x", "z")
GROUPS = ("y", "core")


def tn(a, b, precision=None):
    return lax.dot_general(
        a, b, (((0,), (0,)), ((), ())), precision=precision, preferred_element_type=f32
    )


def nt(a, b, precision=None):
    return lax.dot_general(
        a, b, (((1,), (1,)), ((), ())), precision=precision, preferred_element_type=f32
    )


def nn(a, b, precision=None):
    return jnp.dot(a, b, precision=precision, preferred_element_type=f32)


def pieces(value):
    first = value.astype(bf16)
    rest = value - first.astype(f32)
    second = rest.astype(bf16)
    third = (rest - second.astype(f32)).astype(bf16)
    return first, second, third


def cholesky_small(entries):
    order = len(entries)
    factor = [[None] * order for i in range(order)]
    for j in range(order):
        diagonal = entries[j][j]
        for k in range(j):
            diagonal = diagonal - factor[j][k] * factor[j][k]
        factor[j][j] = jnp.sqrt(diagonal)
        for i in range(j + 1, order):
            current = entries[i][j]
            for k in range(j):
                current = current - factor[i][k] * factor[j][k]
            factor[i][j] = current / factor[j][j]
    return factor


def forward_small(factor, target):
    result = []
    for a in range(len(target)):
        current = target[a]
        for k in range(a):
            current = current - factor[a][k] * result[k]
        result.append(current / factor[a][a])
    return result


def backward_small(factor, target):
    order = len(target)
    result = [None] * order
    for a in reversed(range(order)):
        current = target[a]
        for k in range(a + 1, order):
            current = current - factor[k][a] * result[k]
        result[a] = current / factor[a][a]
    return result


def store_split(ref, slot, block):
    done = 0
    while done < NB:
        flat = slot * NB + done
        part, off = flat // PART, flat % PART
        take = min(NB - done, PART - off)
        start = part * PART_ROWS + off
        ref[start : start + take, :] = block[done : done + take]
        done += take


def assemble_kernel(
    lj_ref, gj_ref, ci_ref, cw_ref, res_ref, ow_ref, cnt_ref, lp_ref, rp_ref, gp_ref,
    gg_ref, main_ref, rg_ref, red_ref, aux_ref, prior_ref,
    left, right, padded,
):
    rows = gj_ref.shape[0]
    nparams = lj_ref.shape[0]
    objects = 8
    observed = rows // objects
    width = gj_ref.shape[1]
    res = res_ref[...]
    prior_ref[:, :width] = jnp.broadcast_to(rp_ref[...], (8, width))
    prior_ref[:, width:] = jnp.broadcast_to(gp_ref[...], (8, width))
    position = lax.broadcasted_iota(jnp.int32, (objects, rows), 1)
    owner = lax.broadcasted_iota(jnp.int32, (objects, rows), 0)
    count = jnp.zeros((objects, rows), jnp.int32)
    for n in range(objects):
        count = jnp.where(owner == n, cnt_ref[n], count)
    local = position - owner * observed
    present = (local >= 0) & (local < observed) & (local < count)
    live = jnp.where(present, jnp.broadcast_to(ow_ref[...], (objects, rows)), 0.0)
    weight = jnp.sum(live, axis=0, keepdims=True)
    misfit = jnp.sum(weight * res * res, axis=1, keepdims=True)
    counted = jnp.sum(
        jnp.sum(jnp.where(present, 1.0, 0.0), axis=0, keepdims=True), axis=1, keepdims=True
    )

    padded[...] = jnp.zeros_like(padded)
    padded[0:1, :rows] = weight
    padded[1:5, :rows] = ci_ref[...].astype(f32)
    padded[5:9, :rows] = cw_ref[...].astype(f32)
    for block in range(padded.shape[1] // NB):
        columns = padded[:, block * NB : (block + 1) * NB].T
        low = block * NB
        while low < min((block + 1) * NB, rows):
            high = min(low + 32, rows)
            here = columns[low - block * NB : high - block * NB]
            weights = here[:, 0:1]
            lanes = lax.broadcasted_iota(jnp.int32, (high - low, width), 1).astype(f32)
            total = jnp.zeros((high - low, width), f32)
            for k in range(4):
                total = total + jnp.where(here[:, 1 + k : 2 + k] == lanes, here[:, 5 + k : 6 + k], 0.0)
            joined = total.astype(bf16)
            for at, value in ((0, joined), (width, gj_ref[low:high, :])):
                scaled = (value.astype(f32) * weights).astype(bf16)
                right[low:high, at : at + width] = value
                right[rows + low : rows + high, at : at + width] = scaled
                left[low:high, at : at + width] = (scaled.astype(f32) * 0.5).astype(bf16)
                left[rows + low : rows + high, at : at + width] = (value.astype(f32) * 0.5).astype(bf16)
            low = high

    jac = lj_ref[...].astype(f32)
    weighted = [jac[a : a + 1, :] * live for a in range(nparams)]
    entries = [[None] * nparams for a in range(nparams)]
    owner8 = lax.broadcasted_iota(jnp.int32, (objects, objects), 0)
    lane8 = lax.broadcasted_iota(jnp.int32, (objects, objects), 1)
    for a in range(nparams):
        for b in range(a + 1):
            value = jnp.sum(weighted[a] * jac[b : b + 1, :], axis=1, keepdims=True)
            if a == b:
                prior = jnp.broadcast_to(lp_ref[a : a + 1, :], (objects, objects))
                value = value + jnp.sum(jnp.where(owner8 == lane8, prior, 0.0), axis=1, keepdims=True)
            entries[a][b] = value
    factor = cholesky_small(entries)
    local_gradient = [jnp.sum(weighted[a] * res, axis=1, keepdims=True) for a in range(nparams)]
    reduced_gradient = forward_small(factor, local_gradient)

    blank = jnp.zeros((8, rows), f32)
    stacked = jnp.concatenate(weighted + [blank], axis=0)
    everything = right[0:rows, :]
    coupling = None
    for piece in pieces(stacked):
        term = nn(piece, everything)
        coupling = term if coupling is None else coupling + term
    reduced = forward_small(factor, [coupling[8 * a : 8 * a + 8] for a in range(nparams)])
    joint = jnp.concatenate(reduced + [jnp.zeros((8, 2 * width), f32)], axis=0)
    red_ref[...] = joint
    r0, r1, r2 = pieces(joint)
    base = 2 * rows
    for at, (one, two) in enumerate(((r0, r0), (r0, r1), (r1, r0), (r1, r1), (r0, r2), (r2, r0))):
        left[base + at * RPAD : base + (at + 1) * RPAD, :] = -one
        right[base + at * RPAD : base + (at + 1) * RPAD, :] = two

    lane = lax.broadcasted_iota(jnp.int32, (objects, NB), 1)
    aux = jnp.zeros((objects, NB), f32)
    at = 0
    for a in range(nparams):
        for b in range(a + 1):
            aux = jnp.where(lane == at, factor[a][b], aux)
            at += 1
    for a in range(nparams):
        aux = jnp.where(lane == at, reduced_gradient[a], aux)
        at += 1
    aux_ref[...] = aux

    first, second, third = pieces(res)
    lhs = jnp.concatenate(
        [first.astype(f32), second.astype(f32), third.astype(f32), jnp.zeros((13, rows), f32)], axis=0
    ).astype(bf16)
    gradient = jnp.sum(nn(lhs, right[rows : 2 * rows, :]), axis=0, keepdims=True)
    for a in range(nparams):
        gradient = gradient - jnp.sum(reduced_gradient[a] * reduced[a], axis=0, keepdims=True)
    for at in range(8):
        main_ref[TRI + at : TRI + at + 1, :] = gradient[:, at * NB : (at + 1) * NB]

    row_lane = lax.broadcasted_iota(jnp.int32, (8, NB), 1)
    scalars = jnp.where(row_lane == 0, misfit, jnp.where(row_lane == 1, counted, 0.0))
    for part in range(REG_PARTS):
        gg_ref[part * PART_ROWS + PART : (part + 1) * PART_ROWS, :] = scalars
    for i in range(NBLK):
        for half in range(2):
            at = half * width
            value = tn(left[:, at + i * NB : at + (i + 1) * NB], right[:, at + i * NB : at + width])
            for j in range(i, NBLK):
                block = value[:, (j - i) * NB : (j - i + 1) * NB]
                slot = SLOT[i, j]
                if half == 0:
                    main_ref[slot * NB : (slot + 1) * NB, :] = block
                else:
                    store_split(gg_ref, slot, block)
        value = 2.0 * tn(left[0:rows, i * NB : (i + 1) * NB], right[0:rows, width:]) + tn(
            left[base:, i * NB : (i + 1) * NB], right[base:, width:]
        )
        for c in range(NBLK):
            rg_ref[c * width + i * NB : c * width + (i + 1) * NB, :] = value[:, c * NB : (c + 1) * NB]


def spread(value, at):
    return jnp.broadcast_to(value[at : at + 1], (8, 128))


def invert_pivot(ref):
    lane = lax.broadcasted_iota(jnp.int32, (8, 128), 1)
    sub = lax.broadcasted_iota(jnp.int32, (8, 128), 0)
    col = lane & (PB - 1)
    half = lane - col
    tiles = PB // 16

    def pick(value, index):
        return jnp.take_along_axis(value, index, axis=1)

    def group(g, carry):
        at = pl.multiple_of(8 * lax.rem(g, tiles), 8)
        side = lax.div(g, tiles) * PB
        base = 8 * g
        source = ref[pl.ds(at, 8), :]
        panel = pick(source, col + side)
        columns = [pick(source, jnp.full((8, 128), side + base + j, jnp.int32)) for j in range(8)]
        for k in range(0, 8, 2):
            c0, c1 = columns[k], columns[k + 1]
            a, b, c = spread(c0, k), spread(c1, k), spread(c1, k + 1)
            q = 1.0 / (a * c - b * b)
            pa, pb, pc = c * q, b * q, a * q
            s0, s1 = sub == k, sub == k + 1
            m0, m1 = col == base + k, col == base + k + 1
            r0 = jnp.where(m0, 1.0, jnp.where(m1, 0.0, spread(panel, k)))
            r1 = jnp.where(m1, 1.0, jnp.where(m0, 0.0, spread(panel, k + 1)))
            n0 = pa * r0 - pb * r1
            n1 = pc * r1 - pb * r0
            rest = jnp.where(m0 | m1, 0.0, panel) - c0 * n0 - c1 * n1
            panel = jnp.where(s0, n0, jnp.where(s1, n1, rest))
            for j in range(k + 2, 8):
                r0, r1 = spread(columns[j], k), spread(columns[j], k + 1)
                n0 = pa * r0 - pb * r1
                n1 = pc * r1 - pb * r0
                columns[j] = jnp.where(s0, n0, jnp.where(s1, n1, columns[j] - c0 * n0 - c1 * n1))
        rows = [spread(panel, i) for i in range(8)]
        inside = (col >= base) & (col < base + 8)
        for t in range(tiles):
            tile = ref[8 * t : 8 * t + 8, :]
            terms = [pick(tile, half + (base + i)) * rows[i] for i in range(8)]
            kept = jnp.where(inside, 0.0, tile) - terms[0]
            ref[8 * t : 8 * t + 8, :] = (kept - terms[1] - (terms[2] + terms[3])) - (
                (terms[4] + terms[5]) + (terms[6] + terms[7])
            )
        here = ref[pl.ds(at, 8), :]
        ref[pl.ds(at, 8), :] = jnp.where(half == side, panel, here)
        return carry

    lax.fori_loop(0, PB // 8, group, 0)


def halves(value):
    first = value.astype(bf16)
    return first, (value - first.astype(f32)).astype(bf16)


def split_product(a, b):
    a0, a1 = halves(a)
    b0, b1 = halves(b)
    return tn(jnp.concatenate([a0, a0, a1], axis=0), jnp.concatenate([b0, b1, b0], axis=0))


def three(dot, a, b):
    return dot(a[0], b[0]) + (dot(a[0], b[1]) + dot(a[1], b[0]))


def eliminate(a, packed, lower_ref, pivot_ref):
    size = NBLK * NB
    lane = lax.broadcasted_iota(jnp.int32, (PB, size), 1)
    sub = lax.broadcasted_iota(jnp.int32, (PB, size), 0)
    lane32 = lax.broadcasted_iota(jnp.int32, (PB // 2, 128), 1)
    first = lane32 < PB
    for p in range(size // PB):
        r0 = PB * p
        c0 = 128 * (p // 2)
        odd = p % 2 == 1
        row = a[r0 : r0 + PB, :]
        tile = row[:, c0 : c0 + 128]
        turned = pltpu.roll(tile, PB, 1)
        one, two = (turned, tile) if odd else (tile, turned)
        packed[...] = jnp.where(first, one[: PB // 2], two[PB // 2 :])
        invert_pivot(packed)
        inverse = packed[...]
        moved = pltpu.roll(inverse, PB, 1)
        pivot = jnp.concatenate([jnp.where(first, inverse, 0.0), jnp.where(first, moved, 0.0)], axis=0)
        if odd:
            placed = jnp.concatenate([jnp.where(first, 0.0, moved), jnp.where(first, 0.0, inverse)], axis=0)
        else:
            placed = pivot
        pivot_ref[r0 : r0 + PB, :] = placed
        unit = jnp.where(lane == sub + r0, 1.0, 0.0)
        lower_ref[r0 : r0 + PB, :] = jnp.where(lane < r0, row, unit)
        if r0 + PB < size:
            inside = (lane >= r0) & (lane < r0 + PB)
            scaled = split_product(pivot[:, :PB], jnp.where(inside, unit, row))
            c1 = 128 * ((p + 1) // 2)
            below = jnp.where(lane >= r0 + PB, row, 0.0)[:, c1:]
            change = split_product(below, scaled)
            wide = lax.broadcasted_iota(jnp.int32, (size - c1, 128), 1)
            own = (wide >= r0 - c0) & (wide < r0 - c0 + PB)
            a[c1:, c0 : c0 + 128] = jnp.where(own, 0.0, a[c1:, c0 : c0 + 128])
            a[c1:, :] = a[c1:, :] - change


def damped(block, damping, profile):
    row = lax.broadcasted_iota(jnp.int32, (NB, NB), 0)
    col = lax.broadcasted_iota(jnp.int32, (NB, NB), 1)
    return block + jnp.where(row == col, damping * profile, 0.0)


def unpack(source, a, damping, profile):
    a[...] = jnp.zeros_like(a)
    for (i, j), slot in SLOT.items():
        block = source[slot * NB : (slot + 1) * NB, :]
        if i == j:
            block = damped(block, damping, profile[:, i * NB : (i + 1) * NB])
        a[i * NB : (i + 1) * NB, j * NB : (j + 1) * NB] = block


def read_damping(main_ref):
    scal = main_ref[SUM_AT + PART : SUM_AT + PART + 8, :]
    return scal[0:1, 0:1] / scal[0:1, 1:2]


def by_row(matrix, row):
    return jnp.sum(matrix * row, axis=1, keepdims=True)


def by_column(matrix, column):
    return jnp.sum(matrix * column, axis=0, keepdims=True)


def turn(row):
    return jnp.broadcast_to(row, (8, NB)).T


def wide_row(ref, at):
    return jnp.concatenate([ref[at + c : at + c + 1, :] for c in range(NBLK)], axis=1)


def regional_kernel(main_ref, prior_ref, lower_ref, pivot_ref, a, packed):
    unpack(main_ref, a, read_damping(main_ref), prior_ref[0:1, : NBLK * NB])
    eliminate(a, packed, lower_ref, pivot_ref)


def coupling_kernel(main_ref, rg_ref, lower_ref, pivot_ref, out_ref, scaled_ref, q_ref, b0, b1, u0, u1, w0, w1):
    width = NBLK * NB
    for c in range(NBLK):
        lanes = slice(c * NB, (c + 1) * NB)
        b0[:, lanes], b1[:, lanes] = halves(rg_ref[c * width : (c + 1) * width, :])
        column = turn(main_ref[TRI + c : TRI + c + 1, :])
        column = jnp.concatenate([column, jnp.zeros((NB, NB - 8), f32)], axis=1)
        b0[lanes, width:], b1[lanes, width:] = halves(column)
    for i in range(NBLK):
        rows = slice(i * NB, (i + 1) * NB)
        depth = slice(0, (i + 1) * NB)
        value = three(nn, halves(lower_ref[rows, depth]), (b0[depth, :], b1[depth, :]))
        parts = halves(value)
        u0[rows, :], u1[rows, :] = parts[0][:, :width], parts[1][:, :width]
        value = three(nn, halves(pivot_ref[rows, :]), parts)
        scaled_ref[rows, :] = value[:, :width]
        q_ref[rows, :] = value[:, width:]
        w0[rows, :], w1[rows, :] = halves(value)
    sub = lax.broadcasted_iota(jnp.int32, (8, NB), 0)
    tail = jnp.zeros((8, NB), f32)
    for i in range(NBLK):
        lanes = slice(i * NB, (i + 1) * NB)
        value = three(tn, (u0[:, lanes], u1[:, lanes]), (w0[:, i * NB :], w1[:, i * NB :]))
        for j in range(i, NBLK):
            store_split(out_ref, SLOT[i, j], value[:, (j - i) * NB : (j - i + 1) * NB])
        line = TRI + NBLK + i
        rest = jnp.broadcast_to(main_ref[line : line + 1, :], (8, NB)) - value[:, width - i * NB :].T[:8]
        tail = jnp.where(sub == i, jnp.broadcast_to(rest[0:1], (8, NB)), tail)
    for part in range(REG_PARTS):
        out_ref[part * PART_ROWS + PART : (part + 1) * PART_ROWS, :] = tail


def finish_kernel(
    g_ref, v_ref, main_ref, prior_ref, flower_ref, scaled_ref, q_ref, red_ref, aux_ref,
    local_ref, regional_ref, global_ref,
    a, packed, lower, pivot,
):
    nparams = local_ref.shape[0]
    width = NBLK * NB
    unpack(g_ref, a, read_damping(main_ref), prior_ref[0:1, width:])
    eliminate(a, packed, lower, pivot)
    whole = lower[...]
    forward = by_row(whole, wide_row(v_ref, 0))
    forward = jnp.concatenate(
        [
            turn(by_column(pivot[i * NB : (i + 1) * NB, :], forward[i * NB : (i + 1) * NB]))[:, 0:1]
            for i in range(NBLK)
        ],
        axis=0,
    )
    global_step = by_column(whole, forward)
    rest = q_ref[:, 0:1] - by_row(scaled_ref[...], global_step)
    regional_step = by_column(flower_ref[...], rest)
    regional_ref[...] = regional_step
    global_ref[...] = global_step

    aux = aux_ref[...]
    at = 0
    factor = [[None] * nparams for i in range(nparams)]
    for i in range(nparams):
        for c in range(i + 1):
            factor[i][c] = aux[:, at : at + 1]
            at += 1
    update = jnp.concatenate([regional_step, global_step], axis=1)
    target = []
    for i in range(nparams):
        target.append(
            aux[:, at : at + 1] - jnp.sum(red_ref[8 * i : 8 * i + 8, :] * update, axis=1, keepdims=True)
        )
        at += 1
    found = backward_small(factor, target)
    sub = lax.broadcasted_iota(jnp.int32, (8, 8), 0)
    lane = lax.broadcasted_iota(jnp.int32, (8, 8), 1)
    for i in range(nparams):
        local_ref[i : i + 1, :] = jnp.sum(jnp.where(sub == lane, found[i], 0.0), axis=0, keepdims=True)


def shape(*dims, dtype=f32):
    return jax.ShapeDtypeStruct(dims, dtype)


VMEM = pl.BlockSpec(memory_space=pltpu.VMEM)
SMEM = pl.BlockSpec(memory_space=pltpu.SMEM)


def whole_block(dims):
    return pl.BlockSpec(dims, lambda i: (0,) * len(dims))


def call(kernel, out_shape, scratch, specs, flops, grid=(), limit=16):
    return pl.pallas_call(
        kernel,
        grid=grid,
        out_shape=out_shape,
        in_specs=specs,
        out_specs=[VMEM] * len(out_shape),
        scratch_shapes=scratch,
        name=kernel.__name__,
        compiler_params=pltpu.CompilerParams(vmem_limit_bytes=limit * 1024 * 1024),
        cost_estimate=pl.CostEstimate(flops=flops, bytes_accessed=4_000_000, transcendentals=0),
    )


def part_sums(value, axis, parts):
    moved = lax.all_to_all(value, axis, 0, 0, tiled=True)
    return jnp.sum(moved.reshape((parts, value.shape[0] // parts) + value.shape[1:]), axis=0)


def copies_back(piece, axis, parts):
    copies = jnp.broadcast_to(piece[None], (parts,) + piece.shape).reshape((-1,) + piece.shape[1:])
    return lax.all_to_all(copies, axis, 0, 0, tiled=True)


def body(
    local_jac,
    global_jac,
    coeff_index,
    coeff_weight,
    residual,
    obs_weight,
    obs_count,
    local_prior,
    regional_prior,
    global_prior,
):
    nx, nz = lax.axis_size("x"), lax.axis_size("z")
    rows = residual.shape[0]
    nparams = local_jac.shape[0]
    width = global_jac.shape[1]
    stack = 2 * rows + 6 * RPAD
    gg, main, rg, red, aux, prior = call(
        assemble_kernel,
        [
            shape(REG_PARTS * PART_ROWS, NB),
            shape(SUM_AT, NB),
            shape(NBLK * width, NB),
            shape(RPAD, 2 * width),
            shape(8, NB),
            shape(8, 2 * width),
        ],
        [
            pltpu.VMEM((stack, 2 * width), bf16),
            pltpu.VMEM((stack, 2 * width), bf16),
            pltpu.VMEM((NB, 512), f32),
        ],
        [
            whole_block(local_jac.shape), whole_block(global_jac.shape), whole_block(coeff_index.shape),
            whole_block(coeff_weight.shape), whole_block((1, rows)), whole_block((1, rows)), SMEM,
            whole_block(local_prior.shape), whole_block((1, width)), whole_block((1, width)),
        ],
        2_000_000_000,
        grid=(1,),
        limit=60,
    )(
        local_jac, global_jac, coeff_index, coeff_weight, residual[None], obs_weight[None],
        obs_count, local_prior, regional_prior, global_prior[None],
    )
    share = part_sums(gg, GROUPS, REG_PARTS)
    rg = lax.psum_scatter(rg, "x", scatter_dimension=0, tiled=True)
    main = jnp.concatenate([main, share, jnp.zeros((MAIN_ROWS - SUM_AT - PART_ROWS, NB), f32)], axis=0)
    main = part_sums(main, "x", nx)
    both = part_sums(jnp.concatenate([main, rg], axis=0), "z", nz)
    both = copies_back(both, "z", nz)
    main = lax.all_gather(both[: MAIN_ROWS // nx], "x", axis=0, tiled=True)
    main, rg = lax.optimization_barrier((main, both[MAIN_ROWS // nx :]))
    rg = copies_back(rg, "x", nx)
    lower, pivot = call(
        regional_kernel,
        [shape(width, width), shape(width, NB)],
        [pltpu.VMEM((width, width), f32), pltpu.VMEM((PB // 2, 128), f32)],
        [VMEM] * 2,
        20_000_000_000,
    )(main, prior)
    outer, scaled, q = call(
        coupling_kernel,
        [shape(REG_PARTS * PART_ROWS, NB), shape(width, width), shape(width, NB)],
        [
            pltpu.VMEM((width, width + NB), bf16),
            pltpu.VMEM((width, width + NB), bf16),
            pltpu.VMEM((width, width), bf16),
            pltpu.VMEM((width, width), bf16),
            pltpu.VMEM((width, width + NB), bf16),
            pltpu.VMEM((width, width + NB), bf16),
        ],
        [VMEM] * 4,
        4_000_000_000,
    )(main, rg, lower, pivot)
    outer = part_sums(outer, GROUPS, REG_PARTS)
    mine = main[SUM_AT : SUM_AT + PART] - outer[:PART]
    matrix = lax.all_gather(mine, GROUPS, axis=0, tiled=True)
    local_step, regional_step, global_step = call(
        finish_kernel,
        [shape(nparams, 8), shape(1, width), shape(1, width)],
        [
            pltpu.VMEM((width, width), f32),
            pltpu.VMEM((PB // 2, 128), f32),
            pltpu.VMEM((width, width), f32),
            pltpu.VMEM((width, NB), f32),
        ],
        [VMEM] * 9,
        20_000_000_000,
    )(matrix, outer[PART:], main, prior, lower, scaled, q, red, aux)
    return local_step, regional_step, global_step[0]


def solution(mesh):
    devices = mesh.devices.reshape(4, 2, 4, 16)
    split = Mesh(devices, ("y", "core", "x", "z"))
    both = GROUPS + LAYERS
    return jax.shard_map(
        body,
        mesh=split,
        in_specs=(
            P(None, both),
            P(both, None),
            P(None, both),
            P(None, both),
            P(both),
            P(both),
            P(both),
            P(None, both),
            P(GROUPS, None),
            P(),
        ),
        out_specs=(P(None, both), P(GROUPS, None), P()),
        check_vma=False,
    )
```

```python
import jax
import jax.numpy as jnp
from jax import lax
from jax.experimental import pallas as pl
from jax.experimental.pallas import tpu as pltpu
from jax.sharding import Mesh, PartitionSpec as P

f32 = jnp.float32
bf16 = jnp.bfloat16
HIGHEST = lax.Precision.HIGHEST

NB = 128
NBLK = 4
PB = 64
PAIRS = [(i, j) for i in range(NBLK) for j in range(i, NBLK)]
SLOT = {pair: at for at, pair in enumerate(PAIRS)}
TRI = len(PAIRS) * NB
REG_PARTS = 8
PART = TRI // REG_PARTS
PART_ROWS = PART + 8
MAIN_ROWS = 1536
SUM_AT = TRI + 8
CHUNK = 48
RPAD = 64

LAYERS = ("x", "z")
GROUPS = ("y", "core")


def tn(a, b, precision=None):
    return lax.dot_general(
        a, b, (((0,), (0,)), ((), ())), precision=precision, preferred_element_type=f32
    )


def nt(a, b, precision=None):
    return lax.dot_general(
        a, b, (((1,), (1,)), ((), ())), precision=precision, preferred_element_type=f32
    )


def nn(a, b, precision=None):
    return jnp.dot(a, b, precision=precision, preferred_element_type=f32)


def pieces(value):
    first = value.astype(bf16)
    rest = value - first.astype(f32)
    second = rest.astype(bf16)
    third = (rest - second.astype(f32)).astype(bf16)
    return first, second, third


def cholesky_small(entries):
    order = len(entries)
    factor = [[None] * order for i in range(order)]
    for j in range(order):
        diagonal = entries[j][j]
        for k in range(j):
            diagonal = diagonal - factor[j][k] * factor[j][k]
        factor[j][j] = jnp.sqrt(diagonal)
        for i in range(j + 1, order):
            current = entries[i][j]
            for k in range(j):
                current = current - factor[i][k] * factor[j][k]
            factor[i][j] = current / factor[j][j]
    return factor


def forward_small(factor, target):
    result = []
    for a in range(len(target)):
        current = target[a]
        for k in range(a):
            current = current - factor[a][k] * result[k]
        result.append(current / factor[a][a])
    return result


def backward_small(factor, target):
    order = len(target)
    result = [None] * order
    for a in reversed(range(order)):
        current = target[a]
        for k in range(a + 1, order):
            current = current - factor[k][a] * result[k]
        result[a] = current / factor[a][a]
    return result


def store_split(ref, slot, block):
    done = 0
    while done < NB:
        flat = slot * NB + done
        part, off = flat // PART, flat % PART
        take = min(NB - done, PART - off)
        start = part * PART_ROWS + off
        ref[start : start + take, :] = block[done : done + take]
        done += take


def assemble_kernel(
    lj_ref, gj_ref, ci_ref, cw_ref, res_ref, ow_ref, cnt_ref, lp_ref, rp_ref, gp_ref,
    gg_ref, main_ref, rg_ref, red_ref, aux_ref, prior_ref,
    left, right, padded,
):
    rows = gj_ref.shape[0]
    nparams = lj_ref.shape[0]
    objects = 8
    observed = rows // objects
    width = gj_ref.shape[1]
    res = res_ref[...]
    prior_ref[:, :width] = jnp.broadcast_to(rp_ref[...], (8, width))
    prior_ref[:, width:] = jnp.broadcast_to(gp_ref[...], (8, width))
    position = lax.broadcasted_iota(jnp.int32, (objects, rows), 1)
    owner = lax.broadcasted_iota(jnp.int32, (objects, rows), 0)
    count = jnp.zeros((objects, rows), jnp.int32)
    for n in range(objects):
        count = jnp.where(owner == n, cnt_ref[n], count)
    local = position - owner * observed
    present = (local >= 0) & (local < observed) & (local < count)
    live = jnp.where(present, jnp.broadcast_to(ow_ref[...], (objects, rows)), 0.0)
    weight = jnp.sum(live, axis=0, keepdims=True)
    misfit = jnp.sum(weight * res * res, axis=1, keepdims=True)
    counted = jnp.sum(
        jnp.sum(jnp.where(present, 1.0, 0.0), axis=0, keepdims=True), axis=1, keepdims=True
    )

    padded[...] = jnp.zeros_like(padded)
    padded[0:1, :rows] = weight
    padded[1:5, :rows] = ci_ref[...].astype(f32)
    padded[5:9, :rows] = cw_ref[...].astype(f32)
    for block in range(padded.shape[1] // NB):
        columns = padded[:, block * NB : (block + 1) * NB].T
        low = block * NB
        while low < min((block + 1) * NB, rows):
            high = min(low + 32, rows)
            here = columns[low - block * NB : high - block * NB]
            weights = here[:, 0:1]
            lanes = lax.broadcasted_iota(jnp.int32, (high - low, width), 1).astype(f32)
            total = jnp.zeros((high - low, width), f32)
            for k in range(4):
                total = total + jnp.where(here[:, 1 + k : 2 + k] == lanes, here[:, 5 + k : 6 + k], 0.0)
            joined = total.astype(bf16)
            for at, value in ((0, joined), (width, gj_ref[low:high, :])):
                scaled = (value.astype(f32) * weights).astype(bf16)
                right[low:high, at : at + width] = value
                right[rows + low : rows + high, at : at + width] = scaled
                left[low:high, at : at + width] = (scaled.astype(f32) * 0.5).astype(bf16)
                left[rows + low : rows + high, at : at + width] = (value.astype(f32) * 0.5).astype(bf16)
            low = high

    jac = lj_ref[...].astype(f32)
    weighted = [jac[a : a + 1, :] * live for a in range(nparams)]
    entries = [[None] * nparams for a in range(nparams)]
    owner8 = lax.broadcasted_iota(jnp.int32, (objects, objects), 0)
    lane8 = lax.broadcasted_iota(jnp.int32, (objects, objects), 1)
    for a in range(nparams):
        for b in range(a + 1):
            value = jnp.sum(weighted[a] * jac[b : b + 1, :], axis=1, keepdims=True)
            if a == b:
                prior = jnp.broadcast_to(lp_ref[a : a + 1, :], (objects, objects))
                value = value + jnp.sum(jnp.where(owner8 == lane8, prior, 0.0), axis=1, keepdims=True)
            entries[a][b] = value
    factor = cholesky_small(entries)
    local_gradient = [jnp.sum(weighted[a] * res, axis=1, keepdims=True) for a in range(nparams)]
    reduced_gradient = forward_small(factor, local_gradient)

    blank = jnp.zeros((8, rows), f32)
    stacked = jnp.concatenate(weighted + [blank], axis=0)
    everything = right[0:rows, :]
    coupling = None
    for piece in pieces(stacked):
        term = nn(piece, everything)
        coupling = term if coupling is None else coupling + term
    reduced = forward_small(factor, [coupling[8 * a : 8 * a + 8] for a in range(nparams)])
    joint = jnp.concatenate(reduced + [jnp.zeros((8, 2 * width), f32)], axis=0)
    red_ref[...] = joint
    r0, r1 = halves(joint)
    base = 2 * rows
    for at, (one, two) in enumerate(((r0, r0), (r0, r1), (r1, r0))):
        left[base + at * RPAD : base + (at + 1) * RPAD, :] = -one
        right[base + at * RPAD : base + (at + 1) * RPAD, :] = two

    lane = lax.broadcasted_iota(jnp.int32, (objects, NB), 1)
    aux = jnp.zeros((objects, NB), f32)
    at = 0
    for a in range(nparams):
        for b in range(a + 1):
            aux = jnp.where(lane == at, factor[a][b], aux)
            at += 1
    for a in range(nparams):
        aux = jnp.where(lane == at, reduced_gradient[a], aux)
        at += 1
    aux_ref[...] = aux

    first, second, third = pieces(res)
    lhs = jnp.concatenate(
        [first.astype(f32), second.astype(f32), third.astype(f32), jnp.zeros((13, rows), f32)], axis=0
    ).astype(bf16)
    gradient = jnp.sum(nn(lhs, right[rows : 2 * rows, :]), axis=0, keepdims=True)
    for a in range(nparams):
        gradient = gradient - jnp.sum(reduced_gradient[a] * reduced[a], axis=0, keepdims=True)
    for at in range(8):
        main_ref[TRI + at : TRI + at + 1, :] = gradient[:, at * NB : (at + 1) * NB]

    row_lane = lax.broadcasted_iota(jnp.int32, (8, NB), 1)
    scalars = jnp.where(row_lane == 0, misfit, jnp.where(row_lane == 1, counted, 0.0))
    for part in range(REG_PARTS):
        gg_ref[part * PART_ROWS + PART : (part + 1) * PART_ROWS, :] = scalars
    for i in range(NBLK):
        for half in range(2):
            at = half * width
            value = tn(left[:, at + i * NB : at + (i + 1) * NB], right[:, at + i * NB : at + width])
            for j in range(i, NBLK):
                block = value[:, (j - i) * NB : (j - i + 1) * NB]
                slot = SLOT[i, j]
                if half == 0:
                    main_ref[slot * NB : (slot + 1) * NB, :] = block
                else:
                    store_split(gg_ref, slot, block)
        value = 2.0 * tn(left[0:rows, i * NB : (i + 1) * NB], right[0:rows, width:]) + tn(
            left[base:, i * NB : (i + 1) * NB], right[base:, width:]
        )
        for c in range(NBLK):
            rg_ref[c * width + i * NB : c * width + (i + 1) * NB, :] = value[:, c * NB : (c + 1) * NB]


def spread(value, at):
    return jnp.broadcast_to(value[at : at + 1], (8, 128))


def invert_pivot(ref):
    lane = lax.broadcasted_iota(jnp.int32, (8, 128), 1)
    sub = lax.broadcasted_iota(jnp.int32, (8, 128), 0)
    col = lane & (PB - 1)
    half = lane - col
    tiles = PB // 16

    def pick(value, index):
        return jnp.take_along_axis(value, index, axis=1)

    def group(g, carry):
        at = pl.multiple_of(8 * lax.rem(g, tiles), 8)
        side = lax.div(g, tiles) * PB
        base = 8 * g
        source = ref[pl.ds(at, 8), :]
        panel = pick(source, col + side)
        columns = [pick(source, jnp.full((8, 128), side + base + j, jnp.int32)) for j in range(8)]
        for k in range(0, 8, 2):
            c0, c1 = columns[k], columns[k + 1]
            a, b, c = spread(c0, k), spread(c1, k), spread(c1, k + 1)
            q = 1.0 / (a * c - b * b)
            pa, pb, pc = c * q, b * q, a * q
            s0, s1 = sub == k, sub == k + 1
            m0, m1 = col == base + k, col == base + k + 1
            r0 = jnp.where(m0, 1.0, jnp.where(m1, 0.0, spread(panel, k)))
            r1 = jnp.where(m1, 1.0, jnp.where(m0, 0.0, spread(panel, k + 1)))
            n0 = pa * r0 - pb * r1
            n1 = pc * r1 - pb * r0
            rest = jnp.where(m0 | m1, 0.0, panel) - c0 * n0 - c1 * n1
            panel = jnp.where(s0, n0, jnp.where(s1, n1, rest))
            for j in range(k + 2, 8):
                r0, r1 = spread(columns[j], k), spread(columns[j], k + 1)
                n0 = pa * r0 - pb * r1
                n1 = pc * r1 - pb * r0
                columns[j] = jnp.where(s0, n0, jnp.where(s1, n1, columns[j] - c0 * n0 - c1 * n1))
        rows = [spread(panel, i) for i in range(8)]
        inside = (col >= base) & (col < base + 8)
        for t in range(tiles):
            tile = ref[8 * t : 8 * t + 8, :]
            terms = [pick(tile, half + (base + i)) * rows[i] for i in range(8)]
            kept = jnp.where(inside, 0.0, tile) - terms[0]
            ref[8 * t : 8 * t + 8, :] = (kept - terms[1] - (terms[2] + terms[3])) - (
                (terms[4] + terms[5]) + (terms[6] + terms[7])
            )
        here = ref[pl.ds(at, 8), :]
        ref[pl.ds(at, 8), :] = jnp.where(half == side, panel, here)
        return carry

    lax.fori_loop(0, PB // 8, group, 0)


def halves(value):
    first = value.astype(bf16)
    return first, (value - first.astype(f32)).astype(bf16)


def split_product(a, b):
    a0, a1 = halves(a)
    b0, b1 = halves(b)
    return tn(jnp.concatenate([a0, a0, a1], axis=0), jnp.concatenate([b0, b1, b0], axis=0))


def three(dot, a, b):
    return dot(a[0], b[0]) + (dot(a[0], b[1]) + dot(a[1], b[0]))


def eliminate(a, packed, lower_ref, pivot_ref):
    size = NBLK * NB
    lane = lax.broadcasted_iota(jnp.int32, (PB, size), 1)
    sub = lax.broadcasted_iota(jnp.int32, (PB, size), 0)
    lane32 = lax.broadcasted_iota(jnp.int32, (PB // 2, 128), 1)
    first = lane32 < PB
    for p in range(size // PB):
        r0 = PB * p
        c0 = 128 * (p // 2)
        odd = p % 2 == 1
        row = a[r0 : r0 + PB, :]
        tile = row[:, c0 : c0 + 128]
        turned = pltpu.roll(tile, PB, 1)
        one, two = (turned, tile) if odd else (tile, turned)
        packed[...] = jnp.where(first, one[: PB // 2], two[PB // 2 :])
        invert_pivot(packed)
        inverse = packed[...]
        moved = pltpu.roll(inverse, PB, 1)
        pivot = jnp.concatenate([jnp.where(first, inverse, 0.0), jnp.where(first, moved, 0.0)], axis=0)
        if odd:
            placed = jnp.concatenate([jnp.where(first, 0.0, moved), jnp.where(first, 0.0, inverse)], axis=0)
        else:
            placed = pivot
        pivot_ref[r0 : r0 + PB, :] = placed
        unit = jnp.where(lane == sub + r0, 1.0, 0.0)
        lower_ref[r0 : r0 + PB, :] = jnp.where(lane < r0, row, unit)
        if r0 + PB < size:
            inside = (lane >= r0) & (lane < r0 + PB)
            scaled = split_product(pivot[:, :PB], jnp.where(inside, unit, row))
            c1 = 128 * ((p + 1) // 2)
            below = jnp.where(lane >= r0 + PB, row, 0.0)[:, c1:]
            change = split_product(below, scaled)
            wide = lax.broadcasted_iota(jnp.int32, (size - c1, 128), 1)
            own = (wide >= r0 - c0) & (wide < r0 - c0 + PB)
            a[c1:, c0 : c0 + 128] = jnp.where(own, 0.0, a[c1:, c0 : c0 + 128])
            a[c1:, :] = a[c1:, :] - change


def damped(block, damping, profile):
    row = lax.broadcasted_iota(jnp.int32, (NB, NB), 0)
    col = lax.broadcasted_iota(jnp.int32, (NB, NB), 1)
    return block + jnp.where(row == col, damping * profile, 0.0)


def unpack(source, a, damping, profile):
    a[...] = jnp.zeros_like(a)
    for (i, j), slot in SLOT.items():
        block = source[slot * NB : (slot + 1) * NB, :]
        if i == j:
            block = damped(block, damping, profile[:, i * NB : (i + 1) * NB])
        a[i * NB : (i + 1) * NB, j * NB : (j + 1) * NB] = block


def read_damping(main_ref):
    scal = main_ref[SUM_AT + PART : SUM_AT + PART + 8, :]
    return scal[0:1, 0:1] / scal[0:1, 1:2]


def by_row(matrix, row):
    return jnp.sum(matrix * row, axis=1, keepdims=True)


def by_column(matrix, column):
    return jnp.sum(matrix * column, axis=0, keepdims=True)


def turn(row):
    return jnp.broadcast_to(row, (8, NB)).T


def wide_row(ref, at):
    return jnp.concatenate([ref[at + c : at + c + 1, :] for c in range(NBLK)], axis=1)


def regional_kernel(main_ref, prior_ref, lower_ref, pivot_ref, a, packed):
    unpack(main_ref, a, read_damping(main_ref), prior_ref[0:1, : NBLK * NB])
    eliminate(a, packed, lower_ref, pivot_ref)


def coupling_kernel(main_ref, rg_ref, lower_ref, pivot_ref, out_ref, scaled_ref, q_ref, b0, b1, u0, u1, w0, w1):
    width = NBLK * NB
    for c in range(NBLK):
        lanes = slice(c * NB, (c + 1) * NB)
        b0[:, lanes], b1[:, lanes] = halves(rg_ref[c * width : (c + 1) * width, :])
        column = turn(main_ref[TRI + c : TRI + c + 1, :])
        column = jnp.concatenate([column, jnp.zeros((NB, NB - 8), f32)], axis=1)
        b0[lanes, width:], b1[lanes, width:] = halves(column)
    for i in range(NBLK):
        rows = slice(i * NB, (i + 1) * NB)
        depth = slice(0, (i + 1) * NB)
        value = three(nn, halves(lower_ref[rows, depth]), (b0[depth, :], b1[depth, :]))
        parts = halves(value)
        u0[rows, :], u1[rows, :] = parts[0][:, :width], parts[1][:, :width]
        value = three(nn, halves(pivot_ref[rows, :]), parts)
        scaled_ref[rows, :] = value[:, :width]
        q_ref[rows, :] = value[:, width:]
        w0[rows, :], w1[rows, :] = halves(value)
    sub = lax.broadcasted_iota(jnp.int32, (8, NB), 0)
    tail = jnp.zeros((8, NB), f32)
    for i in range(NBLK):
        lanes = slice(i * NB, (i + 1) * NB)
        value = three(tn, (u0[:, lanes], u1[:, lanes]), (w0[:, i * NB :], w1[:, i * NB :]))
        for j in range(i, NBLK):
            store_split(out_ref, SLOT[i, j], value[:, (j - i) * NB : (j - i + 1) * NB])
        line = TRI + NBLK + i
        rest = jnp.broadcast_to(main_ref[line : line + 1, :], (8, NB)) - value[:, width - i * NB :].T[:8]
        tail = jnp.where(sub == i, jnp.broadcast_to(rest[0:1], (8, NB)), tail)
    for part in range(REG_PARTS):
        out_ref[part * PART_ROWS + PART : (part + 1) * PART_ROWS, :] = tail


def finish_kernel(
    g_ref, v_ref, main_ref, prior_ref, flower_ref, scaled_ref, q_ref, red_ref, aux_ref,
    local_ref, regional_ref, global_ref,
    a, packed, lower, pivot,
):
    nparams = local_ref.shape[0]
    width = NBLK * NB
    unpack(g_ref, a, read_damping(main_ref), prior_ref[0:1, width:])
    eliminate(a, packed, lower, pivot)
    whole = lower[...]
    forward = by_row(whole, wide_row(v_ref, 0))
    forward = jnp.concatenate(
        [
            turn(by_column(pivot[i * NB : (i + 1) * NB, :], forward[i * NB : (i + 1) * NB]))[:, 0:1]
            for i in range(NBLK)
        ],
        axis=0,
    )
    global_step = by_column(whole, forward)
    rest = q_ref[:, 0:1] - by_row(scaled_ref[...], global_step)
    regional_step = by_column(flower_ref[...], rest)
    regional_ref[...] = regional_step
    global_ref[...] = global_step

    aux = aux_ref[...]
    at = 0
    factor = [[None] * nparams for i in range(nparams)]
    for i in range(nparams):
        for c in range(i + 1):
            factor[i][c] = aux[:, at : at + 1]
            at += 1
    update = jnp.concatenate([regional_step, global_step], axis=1)
    target = []
    for i in range(nparams):
        target.append(
            aux[:, at : at + 1] - jnp.sum(red_ref[8 * i : 8 * i + 8, :] * update, axis=1, keepdims=True)
        )
        at += 1
    found = backward_small(factor, target)
    sub = lax.broadcasted_iota(jnp.int32, (8, 8), 0)
    lane = lax.broadcasted_iota(jnp.int32, (8, 8), 1)
    for i in range(nparams):
        local_ref[i : i + 1, :] = jnp.sum(jnp.where(sub == lane, found[i], 0.0), axis=0, keepdims=True)


def shape(*dims, dtype=f32):
    return jax.ShapeDtypeStruct(dims, dtype)


VMEM = pl.BlockSpec(memory_space=pltpu.VMEM)
SMEM = pl.BlockSpec(memory_space=pltpu.SMEM)


def whole_block(dims):
    return pl.BlockSpec(dims, lambda i: (0,) * len(dims))


def call(kernel, out_shape, scratch, specs, flops, grid=(), limit=16):
    return pl.pallas_call(
        kernel,
        grid=grid,
        out_shape=out_shape,
        in_specs=specs,
        out_specs=[VMEM] * len(out_shape),
        scratch_shapes=scratch,
        name=kernel.__name__,
        compiler_params=pltpu.CompilerParams(vmem_limit_bytes=limit * 1024 * 1024),
        cost_estimate=pl.CostEstimate(flops=flops, bytes_accessed=4_000_000, transcendentals=0),
    )


def part_sums(value, axis, parts):
    moved = lax.all_to_all(value, axis, 0, 0, tiled=True)
    return jnp.sum(moved.reshape((parts, value.shape[0] // parts) + value.shape[1:]), axis=0)


def copies_back(piece, axis, parts):
    copies = jnp.broadcast_to(piece[None], (parts,) + piece.shape).reshape((-1,) + piece.shape[1:])
    return lax.all_to_all(copies, axis, 0, 0, tiled=True)


def body(
    local_jac,
    global_jac,
    coeff_index,
    coeff_weight,
    residual,
    obs_weight,
    obs_count,
    local_prior,
    regional_prior,
    global_prior,
):
    nx, nz = lax.axis_size("x"), lax.axis_size("z")
    rows = residual.shape[0]
    nparams = local_jac.shape[0]
    width = global_jac.shape[1]
    stack = 2 * rows + 3 * RPAD
    gg, main, rg, red, aux, prior = call(
        assemble_kernel,
        [
            shape(REG_PARTS * PART_ROWS, NB),
            shape(SUM_AT, NB),
            shape(NBLK * width, NB),
            shape(RPAD, 2 * width),
            shape(8, NB),
            shape(8, 2 * width),
        ],
        [
            pltpu.VMEM((stack, 2 * width), bf16),
            pltpu.VMEM((stack, 2 * width), bf16),
            pltpu.VMEM((NB, 512), f32),
        ],
        [
            whole_block(local_jac.shape), whole_block(global_jac.shape), whole_block(coeff_index.shape),
            whole_block(coeff_weight.shape), whole_block((1, rows)), whole_block((1, rows)), SMEM,
            whole_block(local_prior.shape), whole_block((1, width)), whole_block((1, width)),
        ],
        2_000_000_000,
        grid=(1,),
        limit=60,
    )(
        local_jac, global_jac, coeff_index, coeff_weight, residual[None], obs_weight[None],
        obs_count, local_prior, regional_prior, global_prior[None],
    )
    share = part_sums(gg, GROUPS, REG_PARTS)
    rg = lax.psum_scatter(rg, "x", scatter_dimension=0, tiled=True)
    main = jnp.concatenate([main, share, jnp.zeros((MAIN_ROWS - SUM_AT - PART_ROWS, NB), f32)], axis=0)
    main = part_sums(main, "x", nx)
    both = part_sums(jnp.concatenate([main, rg], axis=0), "z", nz)
    both = copies_back(both, "z", nz)
    main = lax.all_gather(both[: MAIN_ROWS // nx], "x", axis=0, tiled=True)
    main, rg = lax.optimization_barrier((main, both[MAIN_ROWS // nx :]))
    rg = copies_back(rg, "x", nx)
    lower, pivot = call(
        regional_kernel,
        [shape(width, width), shape(width, NB)],
        [pltpu.VMEM((width, width), f32), pltpu.VMEM((PB // 2, 128), f32)],
        [VMEM] * 2,
        20_000_000_000,
    )(main, prior)
    outer, scaled, q = call(
        coupling_kernel,
        [shape(REG_PARTS * PART_ROWS, NB), shape(width, width), shape(width, NB)],
        [
            pltpu.VMEM((width, width + NB), bf16),
            pltpu.VMEM((width, width + NB), bf16),
            pltpu.VMEM((width, width), bf16),
            pltpu.VMEM((width, width), bf16),
            pltpu.VMEM((width, width + NB), bf16),
            pltpu.VMEM((width, width + NB), bf16),
        ],
        [VMEM] * 4,
        4_000_000_000,
    )(main, rg, lower, pivot)
    outer = part_sums(outer, GROUPS, REG_PARTS)
    mine = main[SUM_AT : SUM_AT + PART] - outer[:PART]
    matrix = lax.all_gather(mine, GROUPS, axis=0, tiled=True)
    local_step, regional_step, global_step = call(
        finish_kernel,
        [shape(nparams, 8), shape(1, width), shape(1, width)],
        [
            pltpu.VMEM((width, width), f32),
            pltpu.VMEM((PB // 2, 128), f32),
            pltpu.VMEM((width, width), f32),
            pltpu.VMEM((width, NB), f32),
        ],
        [VMEM] * 9,
        20_000_000_000,
    )(matrix, outer[PART:], main, prior, lower, scaled, q, red, aux)
    return local_step, regional_step, global_step[0]


def solution(mesh):
    devices = mesh.devices.reshape(4, 2, 4, 16)
    split = Mesh(devices, ("y", "core", "x", "z"))
    both = GROUPS + LAYERS
    return jax.shard_map(
        body,
        mesh=split,
        in_specs=(
            P(None, both),
            P(both, None),
            P(None, both),
            P(None, both),
            P(both),
            P(both),
            P(both),
            P(None, both),
            P(GROUPS, None),
            P(),
        ),
        out_specs=(P(None, both), P(GROUPS, None), P()),
        check_vma=False,
    )
```
